32 devices in a mesh: dp: 16 (over z, x, core), space: 2 (over y).
Axes of the slice: x: 2, y: 2, z: 4, core: 2. Of those that a mesh axis runs over, the one named last changes fastest.
Arguments:
- fields: bfloat16 [16, 126, 252, 192], P('dp', 'space'), may hold values from -6 to 6
- cotangent: bfloat16 [16, 126, 252, 192], P('dp', 'space'), may hold values from -1.796875 to 1.796875
- spec_real: bfloat16 [126, 192], replicated, may hold values from -4.1875 to 4.1875
- spec_imag: bfloat16 [126, 192], replicated, may hold values from -4.1875 to 4.1875
Outputs:
- grad_real: float32 [126, 192], replicated
- grad_imag: float32 [126, 192], replicated
The draws below stay inside these ranges and needn't reach their ends.
All inputs are finite; a program needn't handle non-finite values.
Results may differ from the reference program's by a relative error of at most 0.015.
Values may be sent and summed in bfloat16 or wider, within the bound.
No kernel may reach another device: no remote copies, remote signals or barrier semaphores. Data moves between devices by JAX's collectives and lax.ppermute only.
A program may use at most 128 MiB of HBM per device.

```python
import math
import jax
import jax.numpy as jnp
from jax import lax

C = 192
NLAT = 126
NLON = 252
MODES = 126
BATCH = 16


def block_levels(rng, shape, cuts, least, largest):
    gain = 1.0
    for position, parts in cuts:
        draws = jax.random.uniform(jax.random.fold_in(jax.random.fold_in(rng, 6), position), (parts,), jnp.float32, least / len(cuts), largest / len(cuts))
        gain = gain * jnp.repeat(jnp.exp(draws), shape[position] // parts).reshape((-1,) + (1,) * (len(shape) - 1 - position))
    return gain


def gaussian(stream_key, extent, spread, most, pieces=(), kind=jnp.bfloat16):
    array = spread * jax.random.normal(stream_key, extent, jnp.float32)
    if pieces:
        array = array * block_levels(stream_key, extent, pieces, -0.22, 0.18)
    return jnp.clip(array, -most, most).astype(kind)


def setup_inputs(seed: int = 0) -> dict:
    key_list = jax.random.split(jax.random.key(seed), 5)
    fields = gaussian(key_list[0], (BATCH, NLAT, NLON, C), 1.0, 6.0, ((0, 16), (1, 2)))
    cotangent = gaussian(key_list[1], (BATCH, NLAT, NLON, C), 0.3, 1.796875, ((0, 16), (1, 2)))
    spec_real = gaussian(key_list[2], (MODES, C), 0.7, 4.1875)
    spec_imag = gaussian(key_list[3], (MODES, C), 0.7, 4.1875)
    return {"fields": fields, "cotangent": cotangent, "spec_real": spec_real, "spec_imag": spec_imag}


def grid_tables():
    latitude = jnp.arange(NLAT, dtype=jnp.float32)
    colatitude = math.pi * (latitude + 0.5) / NLAT
    sin_theta = jnp.sin(colatitude)
    quad_weight = math.pi / NLAT * (2.0 * math.pi / NLON) * sin_theta
    return (jnp.cos(colatitude), sin_theta, quad_weight)

def fourier_tables(orders):
    longitude = jnp.arange(NLON, dtype=jnp.int32)
    phase_index = orders[:, None] * longitude[None, :] % NLON
    angles = 2.0 * math.pi / NLON * phase_index.astype(jnp.float32)
    basis_rows = jnp.stack([jnp.cos(angles), -jnp.sin(angles)], axis=1)
    factor = jnp.where(orders == 0, 1.0, 2.0).astype(jnp.float32)
    return (basis_rows.astype(jnp.bfloat16), (basis_rows * factor[:, None, None]).astype(jnp.bfloat16))

def legendre(orders, cos_theta, sin_theta):
    counters = jnp.arange(1, MODES, dtype=jnp.float32)
    log_steps = 0.5 * jnp.log((2.0 * counters + 1.0) / (2.0 * counters))
    log_table = jnp.concatenate([jnp.zeros((1,), jnp.float32), jnp.cumsum(log_steps)])
    order_float = orders.astype(jnp.float32)[:, None]
    log_diagonal = 0.5 * jnp.log(1.0 / (4.0 * math.pi)) + log_table[orders][:, None] + order_float * jnp.log(sin_theta)[None, :]
    diagonal_start = jnp.exp(log_diagonal)
    cos_row = cos_theta[None, :]

    def advance(state_pair, degree):
        previous, earlier = state_pair
        degree_float = degree.astype(jnp.float32)
        growth = jnp.sqrt(jnp.maximum(4.0 * degree_float * degree_float - 1.0, 0.0) / jnp.maximum(degree_float * degree_float - order_float * order_float, 1.0))
        below = degree_float - 1.0
        damping = jnp.sqrt(jnp.maximum(below * below - order_float * order_float, 0.0) / jnp.maximum(4.0 * below * below - 1.0, 1.0))
        recurrence = growth * (cos_row * previous - damping * earlier)
        current = jnp.where(degree_float == order_float, diagonal_start, jnp.where(degree_float > order_float, recurrence, 0.0))
        return ((current, previous), current)
    empty_rows = jnp.zeros_like(diagonal_start)
    final_state, stacked = lax.scan(advance, (empty_rows, empty_rows), jnp.arange(MODES, dtype=jnp.int32), unroll=6)
    return jnp.swapaxes(stacked, 0, 1)

def gelu_slope(values):
    cumulative = 0.5 * (1.0 + lax.erf(values / math.sqrt(2.0)))
    density = jnp.exp(-0.5 * values * values) / math.sqrt(2.0 * math.pi)
    return cumulative + values * density

def reference(fields, cotangent, spec_real, spec_imag):
    cos_theta, sin_theta, quad_weight = grid_tables()
    orders = jnp.arange(MODES, dtype=jnp.int32)
    forward_basis, inverse_basis = fourier_tables(orders)
    associated = legendre(orders, cos_theta, sin_theta)
    weighted = (associated * quad_weight[None, None, :]).astype(jnp.bfloat16).astype(jnp.float32)
    plain = associated.astype(jnp.bfloat16).astype(jnp.float32)
    forward_wide = forward_basis.astype(jnp.float32)
    inverse_wide = inverse_basis.astype(jnp.float32)
    filter_real = spec_real.astype(jnp.float32)[None]
    filter_imag = spec_imag.astype(jnp.float32)[None]

    def one_sample(inputs_pair):
        sample, incoming = inputs_pair
        coeffs = jnp.einsum('alc,mpl->mapc', sample.astype(jnp.float32), forward_wide)
        coeffs = coeffs.reshape(MODES, NLAT, 2 * C).astype(jnp.bfloat16)
        spectral = jnp.einsum('mlj,mjc->mlc', weighted, coeffs.astype(jnp.float32)).astype(jnp.bfloat16)
        spec_values = spectral.astype(jnp.float32)
        real_part = spec_values[..., :C]
        imag_part = spec_values[..., C:]
        mixed = jnp.concatenate([real_part * filter_real - imag_part * filter_imag, real_part * filter_imag + imag_part * filter_real], axis=-1).astype(jnp.bfloat16)
        synthesized = jnp.einsum('mlj,mlc->mjc', plain, mixed.astype(jnp.float32)).astype(jnp.bfloat16)
        signal = jnp.einsum('mapc,mpl->alc', synthesized.reshape(MODES, NLAT, 2, C).astype(jnp.float32), inverse_wide)
        upstream = (incoming.astype(jnp.float32) * gelu_slope(signal)).astype(jnp.bfloat16)
        back_coeffs = jnp.einsum('alc,mpl->mapc', upstream.astype(jnp.float32), inverse_wide)
        back_coeffs = back_coeffs.reshape(MODES, NLAT, 2 * C).astype(jnp.bfloat16)
        back_spectral = jnp.einsum('mlj,mjc->mlc', plain, back_coeffs.astype(jnp.float32)).astype(jnp.bfloat16)
        back_values = back_spectral.astype(jnp.float32)
        back_real = back_values[..., :C]
        back_imag = back_values[..., C:]
        real_term = lax.optimization_barrier(jnp.sum(real_part * back_real + imag_part * back_imag, axis=0))
        imag_term = lax.optimization_barrier(jnp.sum(real_part * back_imag - imag_part * back_real, axis=0))
        return (real_term, imag_term)
    real_terms, imag_terms = lax.map(one_sample, (fields, cotangent))
    grad_real = lax.optimization_barrier(jnp.sum(real_terms, axis=0)) / BATCH
    grad_imag = lax.optimization_barrier(jnp.sum(imag_terms, axis=0)) / BATCH
    return (grad_real, grad_imag)
```

```python
import functools
import math

import jax
import jax.numpy as jnp
import ml_dtypes
import numpy as np
from jax import lax
from jax.experimental import pallas as pl
from jax.experimental.pallas import tpu as pltpu
from jax.sharding import PartitionSpec as P

NLAT = 126
NLON = 252
MODES = 126
LANES = 128
GROUP = 16
PAIRS = 8
VMEM = 56 * 1024 * 1024


def round_up(value, step):
    return -(-value // step) * step


def legendre_table():
    colatitude = math.pi * (np.arange(NLAT) + 0.5) / NLAT
    cos_theta, sin_theta = np.cos(colatitude), np.sin(colatitude)
    counters = np.arange(1, MODES)
    log_steps = 0.5 * np.log((2.0 * counters + 1.0) / (2.0 * counters))
    log_table = np.concatenate([[0.0], np.cumsum(log_steps)])
    table = np.zeros((MODES, MODES, NLAT))
    for order in range(MODES):
        table[order, order] = np.exp(
            0.5 * math.log(1.0 / (4.0 * math.pi)) + log_table[order] + order * np.log(sin_theta)
        )
        for degree in range(order + 1, MODES):
            growth = math.sqrt((4.0 * degree**2 - 1.0) / (degree**2 - order**2))
            below = degree - 1
            current = cos_theta * table[order, below]
            if below > order:
                damping = math.sqrt((below**2 - order**2) / (4.0 * below**2 - 1.0))
                current = current - damping * table[order, degree - 2]
            table[order, degree] = growth * current
    weight = math.pi / NLAT * (2.0 * math.pi / NLON) * sin_theta
    return table, table * weight


def to_bf16(array):
    return np.where(np.abs(array) < 2.0**-126, 0.0, array).astype(ml_dtypes.bfloat16)


class Layout:
    def __init__(self, parts, local):
        self.parts, self.local = parts, local
        self.rows = round_up(local + 1, 16)
        self.half = self.rows // 2
        self.low = max(MODES - local, 0)
        high = MODES - self.low
        self.pairs = (high + 1) // 2
        self.blocks = self.low + self.pairs
        self.slots = round_up(self.low + 2 * self.pairs, 8)
        self.degrees = round_up(MODES, 16)
        self.first_natural = self.rows - MODES + self.low
        self.partner = MODES - 1 + self.low
        orders = list(range(self.low))
        for pair in range(self.pairs):
            order = self.low + pair
            orders += [order, self.partner - order if self.partner - order != order else -1]
        self.orders = np.array(orders + [-1] * (self.slots - len(orders)))


@functools.lru_cache(maxsize=None)
def fourier_constants(parts, local):
    layout = Layout(parts, local)
    orders = np.maximum(layout.orders, 0)
    angles = 2.0 * math.pi / NLON * (orders[:, None] * np.arange(NLON)[None] % NLON)
    live = (layout.orders >= 0)[:, None]
    basis = np.concatenate([np.cos(angles) * live, -np.sin(angles) * live])
    factor = np.where(layout.orders == 0, 1.0, 2.0)[:, None]
    inverse = basis * np.concatenate([factor, factor])
    return to_bf16(basis), to_bf16(inverse), to_bf16(inverse.T)


@functools.lru_cache(maxsize=None)
def legendre_constants(parts, local):
    layout = Layout(parts, local)
    plain, weighted = legendre_table()
    rows, degrees, low, pairs = layout.rows, layout.degrees, layout.low, layout.pairs
    analysis = np.zeros((low, 2 * parts * rows, degrees))
    synth_low = np.zeros((low, parts * rows, degrees))
    pair_fwd = np.zeros((parts, pairs, rows, 2 * rows))
    pair_back = np.zeros((parts, pairs, rows, 2 * rows))
    for part in range(parts):
        own = slice(part * local, (part + 1) * local)
        start = part * rows
        synth_low[:, start : start + local, :MODES] = np.swapaxes(plain[:low, :, own], 1, 2)
        for turn in (1, 2):
            start = (turn * parts - 1 - part) * rows
            analysis[:, start : start + local, :MODES] = np.swapaxes(weighted[:low, :, own], 1, 2)
        for pair in range(pairs):
            order = low + pair
            mate = layout.partner - order
            for target, table in ((pair_fwd, weighted), (pair_back, plain)):
                count = MODES - order
                target[part, pair, rows - count :, :local] = table[order, order:, own]
                if mate != order:
                    count = MODES - mate
                    target[part, pair, :count, rows : rows + local] = table[mate, mate:, own][::-1]
    place = np.zeros((degrees, 2 * rows))
    for row in range(rows):
        if row >= rows - MODES + low:
            place[MODES - rows + row, row] = 1.0
        if MODES - 1 - row >= 0:
            place[MODES - 1 - row, rows + row] = 1.0
    return {
        "analysis": to_bf16(analysis),
        "synth_low": to_bf16(synth_low),
        "pair_fwd": to_bf16(pair_fwd),
        "pair_back": to_bf16(pair_back),
        "pair_synth": to_bf16(np.swapaxes(pair_back, -1, -2)),
        "place": place.astype(np.float32),
    }


def dot(left, right):
    return jnp.dot(left, right, preferred_element_type=jnp.float32)


def swap_halves(values):
    return pltpu.roll(values, LANES // 2, 1)


def interleave(first, second):
    lane = lax.broadcasted_iota(jnp.int32, first.shape, 1)
    below = lane < LANES // 2
    return (
        jnp.where(below, first, swap_halves(second)),
        jnp.where(below, swap_halves(first), second),
    )


def gelu_slope(values):
    size = jnp.abs(values)
    step = 1.0 / (1.0 + 0.2316419 * size)
    scale = 1.0 / math.sqrt(2.0 * math.pi)
    series = 1.330274429 * scale
    for term in (-1.821255978, 1.781477937, -0.356563782, 0.319381530):
        series = series * step + term * scale
    below = jnp.exp(-0.5 * values * values) * (series * step - scale * size)
    return jnp.where(values >= 0.0, 1.0 - below, below)


def grid_rows(layout, side, north, south, quad, group):
    low, width = side * (LANES // 2), LANES // 2
    columns = []
    for pair in (2 * quad, 2 * quad + 1):
        columns.append(north[0, pair][:, low : low + width])
        values = south[0, pair][:, low : low + width]
        if layout.rows > layout.local:
            latitude = layout.half + group * PAIRS + pair
            values = jnp.where(latitude < layout.local, values, jnp.zeros_like(values))
        columns.append(values)
    return jnp.concatenate(columns, axis=1)


def scatter_rows(layout, values, scratch, quad, group):
    slots = layout.slots
    for which in range(2):
        columns = slice(which * LANES, (which + 1) * LANES)
        upper, lower = interleave(values[:slots, columns], values[slots:, columns])
        latitude = group * PAIRS + 2 * quad + which
        scratch[pl.ds(latitude, slots, stride=layout.rows), :] = upper
        scratch[pl.ds(latitude + layout.half, slots, stride=layout.rows), :] = lower


def gather_rows(layout, scratch, quad, group):
    slots = layout.slots
    cosine, sine = [], []
    for which in range(2):
        latitude = group * PAIRS + 2 * quad + which
        upper = scratch[pl.ds(latitude, slots, stride=layout.rows), :]
        lower = scratch[pl.ds(latitude + layout.half, slots, stride=layout.rows), :]
        first, second = interleave(upper, lower)
        cosine.append(first.astype(jnp.bfloat16))
        sine.append(second.astype(jnp.bfloat16))
    return jnp.concatenate(
        [jnp.concatenate(cosine, axis=1), jnp.concatenate(sine, axis=1)], axis=0
    )


def order_rows(layout, scratch, first, count):
    start = pl.multiple_of(first * layout.rows, layout.rows)
    return scratch[pl.ds(start, count * layout.rows), :].astype(jnp.bfloat16)


def forward_kernel(layout, side, north, south, basis, pair_fwd, out, scratch):
    group = pl.program_id(0)
    for quad in range(PAIRS // 2):
        grid = grid_rows(layout, side, north, south, quad, group)
        scatter_rows(layout, dot(basis[...], grid), scratch, quad, group)

    @pl.when(group == pl.num_programs(0) - 1)
    def _():
        def low_block(order, carry):
            out[order] = order_rows(layout, scratch, order, 1)
            return carry

        def pair_block(pair, carry):
            values = order_rows(layout, scratch, layout.low + 2 * pair, 2)
            out[layout.low + pair] = dot(pair_fwd[pair], values).astype(jnp.bfloat16)
            return carry

        lax.fori_loop(0, layout.low, low_block, 0, unroll=4)
        lax.fori_loop(0, layout.pairs, pair_block, 0, unroll=4)


def mix(spectral, real_rows, imag_rows):
    return (spectral * real_rows + swap_halves(spectral) * imag_rows).astype(jnp.bfloat16)


def spectral_kernel(layout, side, *refs):
    own, others = refs[0], refs[1 : layout.parts]
    north, south, basis, basis_t, analysis, synth_low, back_low = refs[layout.parts : layout.parts + 7]
    pair_synth, pair_back, place, real_ref, imag_ref = refs[layout.parts + 7 : layout.parts + 12]
    out, scratch, spec_low, spec_pair = refs[layout.parts + 12 :]
    group = pl.program_id(0)
    rows, degrees, low = layout.rows, layout.degrees, layout.low

    def groups():
        for start in range(0, low, GROUP):
            yield start, min(start + GROUP, low), start // 16 * 16

    @pl.when(group == 0)
    def _():
        for start, stop, top in groups():
            real_rows = real_ref[top:degrees, :]
            imag_rows = imag_ref[top:degrees, :]

            def low_block(order, carry):
                values = jnp.concatenate([own[order]] + [ref[order] for ref in others], axis=0)
                spectral = dot(analysis[order, top:degrees, :], values).astype(jnp.bfloat16)
                spec_low[order, top:degrees, :] = spectral
                mixed = mix(spectral.astype(jnp.float32), real_rows, imag_rows)
                begin = pl.multiple_of(order * rows, rows)
                scratch[pl.ds(begin, rows), :] = dot(synth_low[order, :, top:degrees], mixed)
                return carry

            lax.fori_loop(start, stop, low_block, 0, unroll=4)

        line = lax.broadcasted_iota(jnp.int32, (rows, LANES), 0)

        def pair_block(pair, carry):
            total = own[low + pair].astype(jnp.float32)
            for ref in others:
                total = total + ref[low + pair].astype(jnp.float32)
            spectral = total.astype(jnp.bfloat16)
            spec_pair[pair] = spectral
            natural = line >= layout.first_natural + pair
            real_rows = jnp.where(natural, real_ref[degrees : degrees + rows, :], real_ref[degrees + rows :, :])
            imag_rows = jnp.where(natural, imag_ref[degrees : degrees + rows, :], imag_ref[degrees + rows :, :])
            mixed = mix(spectral.astype(jnp.float32), real_rows, imag_rows)
            begin = pl.multiple_of((low + 2 * pair) * rows, rows)
            scratch[pl.ds(begin, 2 * rows), :] = dot(pair_synth[pair], mixed)
            return carry

        lax.fori_loop(0, layout.pairs, pair_block, 0, unroll=4)
        used = (low + 2 * layout.pairs) * rows
        if used < layout.slots * rows:
            scratch[used:, :] = jnp.zeros((layout.slots * rows - used, LANES), jnp.float32)

    for quad in range(PAIRS // 2):
        modes = gather_rows(layout, scratch, quad, group)
        signal = dot(basis_t[...], modes)
        incoming = grid_rows(layout, side, north, south, quad, group).astype(jnp.float32)
        upstream = (incoming * gelu_slope(signal)).astype(jnp.bfloat16)
        scatter_rows(layout, dot(basis[...], upstream), scratch, quad, group)

    @pl.when(group == pl.num_programs(0) - 1)
    def _():
        def products(spectral, back):
            spectral = spectral.astype(jnp.float32)
            back = back.astype(jnp.bfloat16).astype(jnp.float32)
            return spectral * back, spectral * swap_halves(back)

        zeros = jnp.zeros((degrees, LANES), jnp.float32)
        same, cross = zeros, zeros
        for start, stop, top in groups():

            def low_block(order, carry):
                back = dot(back_low[order, top:degrees, :], order_rows(layout, scratch, order, 1))
                first, second = products(spec_low[order, top:degrees, :], back)
                return carry[0] + first, carry[1] + second

            part = jnp.zeros((degrees - top, LANES), jnp.float32)
            first, second = lax.fori_loop(start, stop, low_block, (part, part), unroll=4)
            if top:
                empty = jnp.zeros((top, LANES), jnp.float32)
                first = jnp.concatenate([empty, first], axis=0)
                second = jnp.concatenate([empty, second], axis=0)
            same, cross = same + first, cross + second

        line = lax.broadcasted_iota(jnp.int32, (rows, LANES), 0)

        def pair_block(pair, carry):
            values = order_rows(layout, scratch, low + 2 * pair, 2)
            first, second = products(spec_pair[pair], dot(pair_back[pair], values))
            natural = line >= layout.first_natural + pair
            return (
                carry[0] + jnp.where(natural, first, 0.0),
                carry[1] + jnp.where(natural, second, 0.0),
                carry[2] + jnp.where(natural, 0.0, first),
                carry[3] + jnp.where(natural, 0.0, second),
            )

        part = jnp.zeros((rows, LANES), jnp.float32)
        sums = lax.fori_loop(0, layout.pairs, pair_block, (part,) * 4, unroll=4)
        placed = jnp.dot(
            place[...],
            jnp.concatenate(
                [jnp.concatenate(sums[:2], axis=1), jnp.concatenate(sums[2:], axis=1)], axis=0
            ),
            preferred_element_type=jnp.float32,
            precision=lax.Precision.HIGHEST,
        )
        same = same + placed[:, :LANES]
        cross = cross + placed[:, LANES:]
        real = same + swap_halves(same)
        imag = swap_halves(cross) - cross
        lane = lax.broadcasted_iota(jnp.int32, real.shape, 1)
        out[...] = jnp.where(lane < LANES // 2, real, imag)


def grid_specs(layout, tile):
    last = -(-layout.local // PAIRS) - 1
    shift = layout.half // PAIRS
    block = (1, PAIRS, NLON, LANES)
    return [
        pl.BlockSpec(block, lambda g: (0, jnp.minimum(g, last), 0, tile)),
        pl.BlockSpec(block, lambda g: (0, jnp.minimum(shift + g, last), 0, tile)),
    ]


def whole():
    return pl.BlockSpec(memory_space=pltpu.VMEM)


def forward_call(layout, chunk, fields, basis, pair_fwd):
    work = 2 * 2 * layout.slots * NLON * layout.rows * LANES // 2
    return pl.pallas_call(
        functools.partial(forward_kernel, layout, chunk % 2),
        grid=(layout.half // PAIRS,),
        in_specs=grid_specs(layout, chunk // 2) + [whole()] * 2,
        out_specs=whole(),
        out_shape=jax.ShapeDtypeStruct((layout.blocks, layout.rows, LANES), jnp.bfloat16),
        scratch_shapes=[pltpu.VMEM((layout.slots * layout.rows, LANES), jnp.float32)],
        compiler_params=pltpu.CompilerParams(vmem_limit_bytes=VMEM),
        cost_estimate=pl.CostEstimate(flops=2 * work, bytes_accessed=8_000_000, transcendentals=0),
        name=f"forward_{chunk}",
    )(fields, fields, basis, pair_fwd)


def spectral_call(layout, chunk, coeffs, cotangent, tables, real_rows, imag_rows):
    work = 2 * 2 * layout.slots * NLON * layout.rows * LANES // 2
    operands = list(coeffs) + [cotangent, cotangent] + list(tables) + [real_rows, imag_rows]
    return pl.pallas_call(
        functools.partial(spectral_kernel, layout, chunk % 2),
        grid=(layout.half // PAIRS,),
        in_specs=[whole()] * layout.parts
        + grid_specs(layout, chunk // 2)
        + [whole()] * (len(tables) + 2),
        out_specs=whole(),
        out_shape=jax.ShapeDtypeStruct((layout.degrees, LANES), jnp.float32),
        scratch_shapes=[
            pltpu.VMEM((layout.slots * layout.rows, LANES), jnp.float32),
            pltpu.VMEM((layout.low, layout.degrees, LANES), jnp.bfloat16),
            pltpu.VMEM((layout.pairs, layout.rows, LANES), jnp.bfloat16),
        ],
        compiler_params=pltpu.CompilerParams(vmem_limit_bytes=VMEM),
        cost_estimate=pl.CostEstimate(flops=6 * work, bytes_accessed=16_000_000, transcendentals=0),
        name=f"spectral_{chunk}",
    )(*operands)


def radices(size):
    found, factor = [], 2
    while size > 1:
        while size % factor == 0:
            found.append(factor)
            size //= factor
        factor += 1
    return found


def sum_over(value, axis):
    size = lax.axis_size(axis)
    stride = 1
    for radix in radices(size):
        total = value
        for turn in range(1, radix):
            pairs = []
            for index in range(size):
                digit = index // stride % radix
                pairs.append((index, index + ((digit + turn) % radix - digit) * stride))
            total = total + lax.ppermute(value, axis, pairs)
        value = total
        stride *= radix
    return value


def filter_rows(layout, spec):
    padded = jnp.pad(spec, ((0, layout.degrees - MODES), (0, 0)))
    front = jnp.pad(spec, ((layout.rows, layout.rows), (0, 0)))
    natural = front[MODES : MODES + layout.rows]
    backward = front[layout.rows + MODES - layout.rows : layout.rows + MODES][::-1]
    return jnp.concatenate([padded, natural, backward], axis=0).astype(jnp.float32)


def on_device(fields, cotangent, spec_real, spec_imag):
    parts = lax.axis_size("space")
    index = lax.axis_index("space")
    layout = Layout(parts, fields.shape[1])
    width = LANES // 2
    chunks = fields.shape[-1] // width
    basis, inverse, inverse_t = (jnp.asarray(a) for a in fourier_constants(parts, layout.local))
    constants = legendre_constants(parts, layout.local)

    def local_table(name):
        return lax.dynamic_index_in_dim(jnp.asarray(constants[name]), index, keepdims=False)

    pair_fwd = local_table("pair_fwd")
    def bands(name, first, count):
        table = jnp.asarray(constants[name])
        return lax.optimization_barrier(
            lax.dynamic_slice_in_dim(table, first * layout.rows, count * layout.rows, 1)
        )

    analysis = jnp.swapaxes(bands("analysis", parts - 1 - index, parts), 1, 2)
    synth_low = bands("synth_low", index, 1)
    back_low = jnp.swapaxes(synth_low, 1, 2)
    pair_tables = [local_table(name) for name in ("pair_synth", "pair_back")]
    tables = [inverse, inverse_t, analysis, synth_low, back_low] + pair_tables + [jnp.asarray(constants["place"])]
    real_all = filter_rows(layout, spec_real)
    imag_all = filter_rows(layout, spec_imag)

    received = []
    for chunk in range(chunks):
        own = forward_call(layout, chunk, fields, basis, pair_fwd)
        blocks = [own]
        for shift in range(1, parts):
            route = [(source, (source + shift) % parts) for source in range(parts)]
            blocks.append(lax.ppermute(own, "space", route))
        received.append(blocks)

    totals = []
    for chunk in range(chunks):
        columns = slice(chunk * width, (chunk + 1) * width)
        real, imag = real_all[:, columns], imag_all[:, columns]
        real_rows = jnp.concatenate([real, real], axis=1)
        imag_rows = jnp.concatenate([-imag, imag], axis=1)
        grads = spectral_call(layout, chunk, received[chunk], cotangent, tables, real_rows, imag_rows)
        totals.append(sum_over(sum_over(grads, "dp"), "space"))

    batch_total = fields.shape[0] * lax.axis_size("dp")
    real = jnp.concatenate([total[:MODES, :width] for total in totals], axis=1)
    imag = jnp.concatenate([total[:MODES, width:] for total in totals], axis=1)
    return (real / batch_total, imag / batch_total)


def solution(mesh):
    in_specs = (P("dp", "space", None, None), P("dp", "space", None, None), P(), P())
    out_specs = (P(), P())
    return jax.shard_map(
        on_device, mesh=mesh, in_specs=in_specs, out_specs=out_specs, check_vma=False
    )
```

```python
import functools
import math

import jax
import jax.numpy as jnp
import ml_dtypes
import numpy as np
from jax import lax
from jax.experimental import pallas as pl
from jax.experimental.pallas import tpu as pltpu
from jax.sharding import PartitionSpec as P

NLAT = 126
NLON = 252
MODES = 126
LANES = 128
GROUP = 16
PAIRS = 8
VMEM = 30 * 1024 * 1024


def round_up(value, step):
    return -(-value // step) * step


def legendre_table():
    colatitude = math.pi * (np.arange(NLAT) + 0.5) / NLAT
    cos_theta, sin_theta = np.cos(colatitude), np.sin(colatitude)
    counters = np.arange(1, MODES)
    log_steps = 0.5 * np.log((2.0 * counters + 1.0) / (2.0 * counters))
    log_table = np.concatenate([[0.0], np.cumsum(log_steps)])
    table = np.zeros((MODES, MODES, NLAT))
    for order in range(MODES):
        table[order, order] = np.exp(
            0.5 * math.log(1.0 / (4.0 * math.pi)) + log_table[order] + order * np.log(sin_theta)
        )
        for degree in range(order + 1, MODES):
            growth = math.sqrt((4.0 * degree**2 - 1.0) / (degree**2 - order**2))
            below = degree - 1
            current = cos_theta * table[order, below]
            if below > order:
                damping = math.sqrt((below**2 - order**2) / (4.0 * below**2 - 1.0))
                current = current - damping * table[order, degree - 2]
            table[order, degree] = growth * current
    weight = math.pi / NLAT * (2.0 * math.pi / NLON) * sin_theta
    return table, table * weight


def to_bf16(array):
    return np.where(np.abs(array) < 2.0**-126, 0.0, array).astype(ml_dtypes.bfloat16)


class Layout:
    def __init__(self, parts, local):
        self.parts, self.local = parts, local
        self.rows = round_up(local + 1, 16)
        self.half = self.rows // 2
        self.pitch = self.rows + 8
        self.low = max(MODES - local, 0)
        high = MODES - self.low
        self.pairs = (high + 1) // 2
        self.blocks = self.low + self.pairs
        self.slots = round_up(self.low + 2 * self.pairs, 8)
        self.degrees = round_up(MODES, 16)
        self.first_natural = self.rows - MODES + self.low
        self.partner = MODES - 1 + self.low
        orders = list(range(self.low))
        for pair in range(self.pairs):
            order = self.low + pair
            orders += [order, self.partner - order if self.partner - order != order else -1]
        self.orders = np.array(orders + [-1] * (self.slots - len(orders)))


@functools.lru_cache(maxsize=None)
def fourier_constants(parts, local):
    layout = Layout(parts, local)
    orders = np.maximum(layout.orders, 0)
    angles = 2.0 * math.pi / NLON * (orders[:, None] * np.arange(NLON)[None] % NLON)
    live = (layout.orders >= 0)[:, None]
    basis = np.concatenate([np.cos(angles) * live, -np.sin(angles) * live])
    factor = np.where(layout.orders == 0, 1.0, 2.0)[:, None]
    inverse = basis * np.concatenate([factor, factor])
    return to_bf16(basis), to_bf16(inverse)


@functools.lru_cache(maxsize=None)
def legendre_constants(parts, local):
    layout = Layout(parts, local)
    plain, weighted = legendre_table()
    rows, degrees, low, pairs = layout.rows, layout.degrees, layout.low, layout.pairs
    analysis = np.zeros((low, 2 * parts * rows, degrees))
    synth_low = np.zeros((low, parts * rows, degrees))
    pair_fwd = np.zeros((parts, pairs, rows, 2 * rows))
    pair_back = np.zeros((parts, pairs, rows, 2 * rows))
    for part in range(parts):
        own = slice(part * local, (part + 1) * local)
        start = part * rows
        synth_low[:, start : start + local, :MODES] = np.swapaxes(plain[:low, :, own], 1, 2)
        for turn in (1, 2):
            start = (turn * parts - 1 - part) * rows
            analysis[:, start : start + local, :MODES] = np.swapaxes(weighted[:low, :, own], 1, 2)
        for pair in range(pairs):
            order = low + pair
            mate = layout.partner - order
            for target, table in ((pair_fwd, weighted), (pair_back, plain)):
                count = MODES - order
                target[part, pair, rows - count :, :local] = table[order, order:, own]
                if mate != order:
                    count = MODES - mate
                    target[part, pair, :count, rows : rows + local] = table[mate, mate:, own][::-1]
    place = np.zeros((degrees, 2 * rows))
    for row in range(rows):
        if row >= rows - MODES + low:
            place[MODES - rows + row, row] = 1.0
        if MODES - 1 - row >= 0:
            place[MODES - 1 - row, rows + row] = 1.0
    return {
        "analysis": to_bf16(analysis),
        "synth_low": to_bf16(synth_low),
        "pair_fwd": to_bf16(pair_fwd),
        "pair_back": to_bf16(pair_back),
        "pair_synth": to_bf16(np.swapaxes(pair_back, -1, -2)),
        "place": place.astype(np.float32),
    }


def dot(left, right, sides=(1, 0)):
    contract = (((sides[0],), (sides[1],)), ((), ()))
    return lax.dot_general(left, right, contract, preferred_element_type=jnp.float32)


def swap_halves(values):
    return pltpu.roll(values, LANES // 2, 1)


def interleave(first, second):
    lane = lax.broadcasted_iota(jnp.int32, first.shape, 1)
    below = lane < LANES // 2
    return (
        jnp.where(below, first, swap_halves(second)),
        jnp.where(below, swap_halves(first), second),
    )


def gelu_slope(values):
    size = jnp.abs(values)
    step = 1.0 / (1.0 + 0.2316419 * size)
    scale = 1.0 / math.sqrt(2.0 * math.pi)
    series = 1.330274429 * scale
    for term in (-1.821255978, 1.781477937, -0.356563782, 0.319381530):
        series = series * step + term * scale
    below = jnp.exp(-0.5 * values * values) * (series * step - scale * size)
    return jnp.where(values >= 0.0, 1.0 - below, below)


def grid_rows(layout, north, south, quad, group):
    rows = []
    for pair in (2 * quad, 2 * quad + 1):
        rows.append(north[0, pair])
        values = south[0, pair]
        if layout.rows > layout.local:
            latitude = layout.half + group * PAIRS + pair
            values = jnp.where(latitude < layout.local, values, jnp.zeros_like(values))
        rows.append(values)
    return jnp.concatenate(rows, axis=0)


def scatter_rows(layout, values, scratch, quad, group):
    slots = layout.slots
    for which in range(2):
        columns = slice(which * LANES, (which + 1) * LANES)
        upper, lower = interleave(values[:slots, columns], values[slots:, columns])
        latitude = group * PAIRS + 2 * quad + which
        scratch[pl.ds(latitude, slots, stride=layout.pitch), :] = upper
        scratch[pl.ds(latitude + layout.half, slots, stride=layout.pitch), :] = lower


def gather_rows(layout, scratch, quad, group):
    slots = layout.slots
    cosine, sine = [], []
    for which in range(2):
        latitude = group * PAIRS + 2 * quad + which
        upper = scratch[pl.ds(latitude, slots, stride=layout.pitch), :]
        lower = scratch[pl.ds(latitude + layout.half, slots, stride=layout.pitch), :]
        first, second = interleave(upper, lower)
        cosine.append(first.astype(jnp.bfloat16))
        sine.append(second.astype(jnp.bfloat16))
    return jnp.concatenate(
        [jnp.concatenate(cosine, axis=1), jnp.concatenate(sine, axis=1)], axis=0
    )


def order_rows(layout, scratch, first, count):
    parts = []
    for order in range(count):
        start = pl.multiple_of((first + order) * layout.pitch, 8)
        parts.append(scratch[pl.ds(start, layout.rows), :])
    return jnp.concatenate(parts, axis=0).astype(jnp.bfloat16)


def forward_kernel(layout, north, south, basis, pair_fwd, out, scratch):
    group = pl.program_id(0)
    for quad in range(PAIRS // 2):
        grid = grid_rows(layout, north, south, quad, group)
        scatter_rows(layout, dot(basis[...], grid, (1, 1)), scratch, quad, group)

    @pl.when(group == pl.num_programs(0) - 1)
    def _():
        def low_block(order, carry):
            out[order] = order_rows(layout, scratch, order, 1)
            return carry

        def pair_block(pair, carry):
            values = order_rows(layout, scratch, layout.low + 2 * pair, 2)
            out[layout.low + pair] = dot(pair_fwd[pair], values).astype(jnp.bfloat16)
            return carry

        lax.fori_loop(0, layout.low, low_block, 0, unroll=8)
        lax.fori_loop(0, layout.pairs, pair_block, 0, unroll=8)


def mix(spectral, swapped, real_rows, imag_rows):
    return (spectral * real_rows + swapped * imag_rows).astype(jnp.bfloat16)


def spectral_kernel(layout, *refs):
    own, others = refs[0], refs[1 : layout.parts]
    north, south, basis, analysis, synth_low, back_low = refs[layout.parts : layout.parts + 6]
    pair_synth, pair_back, place, real_ref, imag_ref = refs[layout.parts + 6 : layout.parts + 11]
    out, scratch, returned, spec_low, swap_low, spec_pair, swap_pair = refs[layout.parts + 11 :]
    group = pl.program_id(0)
    rows, degrees, low = layout.rows, layout.degrees, layout.low

    def groups():
        for start in range(0, low, GROUP):
            yield start, min(start + GROUP, low), start // 16 * 16

    @pl.when(group == 0)
    def _():
        for start, stop, top in groups():
            real_rows = real_ref[top:degrees, :]
            imag_rows = imag_ref[top:degrees, :]

            def low_block(order, carry):
                values = jnp.concatenate([own[order]] + [ref[order] for ref in others], axis=0)
                spectral = dot(analysis[order, top:degrees, :], values).astype(jnp.bfloat16)
                spec_low[order, top:degrees, :] = spectral
                return carry

            def mix_block(order, carry):
                spectral = spec_low[order, top:degrees, :].astype(jnp.float32)
                swapped = swap_halves(spectral)
                swap_low[order, top:degrees, :] = swapped.astype(jnp.bfloat16)
                mixed = mix(spectral, swapped, real_rows, imag_rows)
                begin = pl.multiple_of(order * layout.pitch, 8)
                scratch[pl.ds(begin, rows), :] = dot(synth_low[order, :, top:degrees], mixed)
                return carry

            lax.fori_loop(start, stop, low_block, 0, unroll=8)
            lax.fori_loop(start, stop, mix_block, 0, unroll=8)

        line = lax.broadcasted_iota(jnp.int32, (rows, LANES), 0)

        def pair_block(pair, carry):
            total = own[low + pair].astype(jnp.float32)
            for ref in others:
                total = total + ref[low + pair].astype(jnp.float32)
            spectral = total.astype(jnp.bfloat16)
            spec_pair[pair] = spectral
            natural = line >= layout.first_natural + pair
            real_rows = jnp.where(natural, real_ref[degrees : degrees + rows, :], real_ref[degrees + rows :, :])
            imag_rows = jnp.where(natural, imag_ref[degrees : degrees + rows, :], imag_ref[degrees + rows :, :])
            spectral = spectral.astype(jnp.float32)
            swapped = swap_halves(spectral)
            swap_pair[pair] = swapped.astype(jnp.bfloat16)
            mixed = mix(spectral, swapped, real_rows, imag_rows)
            values = dot(pair_synth[pair], mixed)
            for which in range(2):
                begin = pl.multiple_of((low + 2 * pair + which) * layout.pitch, 8)
                scratch[pl.ds(begin, rows), :] = values[which * rows : (which + 1) * rows]
            return carry

        lax.fori_loop(0, layout.pairs, pair_block, 0, unroll=8)
        used = (low + 2 * layout.pairs) * layout.pitch
        if used < layout.slots * layout.pitch:
            scratch[used : layout.slots * layout.pitch, :] = jnp.zeros(
                (layout.slots * layout.pitch - used, LANES), jnp.float32
            )

    for quad in range(PAIRS // 2):
        modes = gather_rows(layout, scratch, quad, group)
        signal = dot(modes, basis[...], (0, 0))
        incoming = grid_rows(layout, north, south, quad, group).astype(jnp.float32)
        upstream = (incoming * gelu_slope(signal)).astype(jnp.bfloat16)
        scatter_rows(layout, dot(basis[...], upstream, (1, 1)), returned, quad, group)

    @pl.when(group == pl.num_programs(0) - 1)
    def _():
        def products(spectral, swapped, back):
            return spectral.astype(jnp.float32) * back, swapped.astype(jnp.float32) * back

        zeros = jnp.zeros((degrees, LANES), jnp.float32)
        same, cross = zeros, zeros
        for start, stop, top in groups():

            def low_block(order, carry):
                back = dot(back_low[order, top:degrees, :], order_rows(layout, returned, order, 1))
                first, second = products(
                    spec_low[order, top:degrees, :], swap_low[order, top:degrees, :], back
                )
                return carry[0] + first, carry[1] + second

            part = jnp.zeros((degrees - top, LANES), jnp.float32)
            first, second = lax.fori_loop(start, stop, low_block, (part, part), unroll=8)
            if top:
                empty = jnp.zeros((top, LANES), jnp.float32)
                first = jnp.concatenate([empty, first], axis=0)
                second = jnp.concatenate([empty, second], axis=0)
            same, cross = same + first, cross + second

        line = lax.broadcasted_iota(jnp.int32, (rows, LANES), 0)

        def pair_block(pair, carry):
            back = dot(pair_back[pair], order_rows(layout, returned, low + 2 * pair, 2))
            first, second = products(spec_pair[pair], swap_pair[pair], back)
            natural = line >= layout.first_natural + pair
            return (
                carry[0] + jnp.where(natural, first, 0.0),
                carry[1] + jnp.where(natural, second, 0.0),
                carry[2] + jnp.where(natural, 0.0, first),
                carry[3] + jnp.where(natural, 0.0, second),
            )

        part = jnp.zeros((rows, LANES), jnp.float32)
        sums = lax.fori_loop(0, layout.pairs, pair_block, (part,) * 4, unroll=8)
        placed = jnp.dot(
            place[...],
            jnp.concatenate(
                [jnp.concatenate(sums[:2], axis=1), jnp.concatenate(sums[2:], axis=1)], axis=0
            ),
            preferred_element_type=jnp.float32,
            precision=lax.Precision.HIGHEST,
        )
        same = same + placed[:, :LANES]
        cross = cross + placed[:, LANES:]
        real = same + swap_halves(same)
        imag = cross - swap_halves(cross)
        lane = lax.broadcasted_iota(jnp.int32, real.shape, 1)
        out[...] = jnp.where(lane < LANES // 2, real, imag)


def grid_specs(layout, chunk):
    last = -(-layout.local // PAIRS) - 1
    shift = layout.half // PAIRS
    block = (1, PAIRS, LANES // 2, NLON)
    return [
        pl.BlockSpec(block, lambda g: (0, jnp.minimum(g, last), chunk, 0)),
        pl.BlockSpec(block, lambda g: (0, jnp.minimum(shift + g, last), chunk, 0)),
    ]


def whole():
    return pl.BlockSpec(memory_space=pltpu.VMEM)


def forward_call(layout, chunk, fields, basis, pair_fwd):
    work = 2 * 2 * layout.slots * NLON * layout.rows * LANES // 2
    return pl.pallas_call(
        functools.partial(forward_kernel, layout),
        grid=(layout.half // PAIRS,),
        in_specs=grid_specs(layout, chunk) + [whole()] * 2,
        out_specs=whole(),
        out_shape=jax.ShapeDtypeStruct((layout.blocks, layout.rows, LANES), jnp.bfloat16),
        scratch_shapes=[pltpu.VMEM((layout.slots * layout.pitch, LANES), jnp.float32)],
        compiler_params=pltpu.CompilerParams(vmem_limit_bytes=VMEM),
        cost_estimate=pl.CostEstimate(flops=2 * work, bytes_accessed=8_000_000, transcendentals=0),
        name=f"forward_{chunk}",
    )(fields, fields, basis, pair_fwd)


def spectral_call(layout, chunk, coeffs, cotangent, tables, real_rows, imag_rows):
    work = 2 * 2 * layout.slots * NLON * layout.rows * LANES // 2
    operands = list(coeffs) + [cotangent, cotangent] + list(tables) + [real_rows, imag_rows]
    return pl.pallas_call(
        functools.partial(spectral_kernel, layout),
        grid=(layout.half // PAIRS,),
        in_specs=[whole()] * layout.parts
        + grid_specs(layout, chunk)
        + [whole()] * (len(tables) + 2),
        out_specs=whole(),
        out_shape=jax.ShapeDtypeStruct((layout.degrees, LANES), jnp.float32),
        scratch_shapes=[
            pltpu.VMEM((layout.slots * layout.pitch, LANES), jnp.float32),
            pltpu.VMEM((layout.slots * layout.pitch, LANES), jnp.float32),
            pltpu.VMEM((layout.low, layout.degrees, LANES), jnp.bfloat16),
            pltpu.VMEM((layout.low, layout.degrees, LANES), jnp.bfloat16),
            pltpu.VMEM((layout.pairs, layout.rows, LANES), jnp.bfloat16),
            pltpu.VMEM((layout.pairs, layout.rows, LANES), jnp.bfloat16),
        ],
        compiler_params=pltpu.CompilerParams(vmem_limit_bytes=VMEM),
        cost_estimate=pl.CostEstimate(flops=6 * work, bytes_accessed=16_000_000, transcendentals=0),
        name=f"spectral_{chunk}",
    )(*operands)


def radices(size):
    found, factor = [], 2
    while size > 1:
        while size % factor == 0:
            found.append(factor)
            size //= factor
        factor += 1
    return found


def sum_over(value, axis):
    size = lax.axis_size(axis)
    stride = 1
    for radix in radices(size):
        total = value
        for turn in range(1, radix):
            pairs = []
            for index in range(size):
                digit = index // stride % radix
                pairs.append((index, index + ((digit + turn) % radix - digit) * stride))
            total = total + lax.ppermute(value, axis, pairs)
        value = total
        stride *= radix
    return value


def filter_rows(layout, spec):
    padded = jnp.pad(spec, ((0, layout.degrees - MODES), (0, 0)))
    front = jnp.pad(spec, ((layout.rows, layout.rows), (0, 0)))
    natural = front[MODES : MODES + layout.rows]
    backward = front[layout.rows + MODES - layout.rows : layout.rows + MODES][::-1]
    return jnp.concatenate([padded, natural, backward], axis=0).astype(jnp.float32)


def on_device(fields, cotangent, spec_real, spec_imag):
    parts = lax.axis_size("space")
    index = lax.axis_index("space")
    layout = Layout(parts, fields.shape[1])
    width = LANES // 2
    chunks = fields.shape[-1] // width
    basis, inverse = (jnp.asarray(a) for a in fourier_constants(parts, layout.local))
    constants = legendre_constants(parts, layout.local)

    def local_table(name):
        return lax.dynamic_index_in_dim(jnp.asarray(constants[name]), index, keepdims=False)

    pair_fwd = local_table("pair_fwd")
    def bands(name, first, count):
        table = jnp.asarray(constants[name])
        return lax.optimization_barrier(
            lax.dynamic_slice_in_dim(table, first * layout.rows, count * layout.rows, 1)
        )

    analysis = jnp.swapaxes(bands("analysis", parts - 1 - index, parts), 1, 2)
    synth_low = bands("synth_low", index, 1)
    back_low = jnp.swapaxes(synth_low, 1, 2)
    pair_tables = [local_table(name) for name in ("pair_synth", "pair_back")]
    tables = [inverse, analysis, synth_low, back_low] + pair_tables + [jnp.asarray(constants["place"])]
    fields, cotangent = jnp.swapaxes(fields, 2, 3), jnp.swapaxes(cotangent, 2, 3)
    real_all = filter_rows(layout, spec_real)
    imag_all = filter_rows(layout, spec_imag)

    received = []
    for chunk in range(chunks):
        own = forward_call(layout, chunk, fields, basis, pair_fwd)
        blocks = [own]
        for shift in range(1, parts):
            route = [(source, (source + shift) % parts) for source in range(parts)]
            blocks.append(lax.ppermute(own, "space", route))
        received.append(blocks)

    totals = []
    for chunk in range(chunks):
        columns = slice(chunk * width, (chunk + 1) * width)
        real, imag = real_all[:, columns], imag_all[:, columns]
        real_rows = jnp.concatenate([real, real], axis=1)
        imag_rows = jnp.concatenate([-imag, imag], axis=1)
        grads = spectral_call(layout, chunk, received[chunk], cotangent, tables, real_rows, imag_rows)
        totals.append(sum_over(sum_over(grads, "dp"), "space"))

    batch_total = fields.shape[0] * lax.axis_size("dp")
    real = jnp.concatenate([total[:MODES, :width] for total in totals], axis=1)
    imag = jnp.concatenate([total[:MODES, width:] for total in totals], axis=1)
    return (real / batch_total, imag / batch_total)


def solution(mesh):
    in_specs = (P("dp", "space", None, None), P("dp", "space", None, None), P(), P())
    out_specs = (P(), P())
    return jax.shard_map(
        on_device, mesh=mesh, in_specs=in_specs, out_specs=out_specs, check_vma=False
    )
```

```python
import functools
import math

import jax
import jax.numpy as jnp
import ml_dtypes
import numpy as np
from jax import lax
from jax.experimental import pallas as pl
from jax.experimental.pallas import tpu as pltpu
from jax.sharding import PartitionSpec as P

NLAT = 126
NLON = 252
MODES = 126
LANES = 128
GROUP = 16
PAIRS = 8
VMEM = 30 * 1024 * 1024
FORWARD_VMEM = 56 * 1024 * 1024


def round_up(value, step):
    return -(-value // step) * step


def legendre_table():
    colatitude = math.pi * (np.arange(NLAT) + 0.5) / NLAT
    cos_theta, sin_theta = np.cos(colatitude), np.sin(colatitude)
    counters = np.arange(1, MODES)
    log_steps = 0.5 * np.log((2.0 * counters + 1.0) / (2.0 * counters))
    log_table = np.concatenate([[0.0], np.cumsum(log_steps)])
    table = np.zeros((MODES, MODES, NLAT))
    for order in range(MODES):
        table[order, order] = np.exp(
            0.5 * math.log(1.0 / (4.0 * math.pi)) + log_table[order] + order * np.log(sin_theta)
        )
        for degree in range(order + 1, MODES):
            growth = math.sqrt((4.0 * degree**2 - 1.0) / (degree**2 - order**2))
            below = degree - 1
            current = cos_theta * table[order, below]
            if below > order:
                damping = math.sqrt((below**2 - order**2) / (4.0 * below**2 - 1.0))
                current = current - damping * table[order, degree - 2]
            table[order, degree] = growth * current
    weight = math.pi / NLAT * (2.0 * math.pi / NLON) * sin_theta
    return table, table * weight


def to_bf16(array):
    return np.where(np.abs(array) < 2.0**-126, 0.0, array).astype(ml_dtypes.bfloat16)


class Layout:
    def __init__(self, parts, local):
        self.parts, self.local = parts, local
        self.rows = round_up(local + 1, 16)
        self.half = self.rows // 2
        self.pitch = self.rows + 8
        self.low = max(MODES - local, 0)
        high = MODES - self.low
        self.pairs = (high + 1) // 2
        self.blocks = self.low + self.pairs
        self.slots = round_up(self.low + 2 * self.pairs, 8)
        self.degrees = round_up(MODES, 16)
        self.first_natural = self.rows - MODES + self.low
        self.partner = MODES - 1 + self.low
        orders = list(range(self.low))
        for pair in range(self.pairs):
            order = self.low + pair
            orders += [order, self.partner - order if self.partner - order != order else -1]
        self.orders = np.array(orders + [-1] * (self.slots - len(orders)))


@functools.lru_cache(maxsize=None)
def fourier_constants(parts, local):
    layout = Layout(parts, local)
    orders = np.maximum(layout.orders, 0)
    angles = 2.0 * math.pi / NLON * (orders[:, None] * np.arange(NLON)[None] % NLON)
    live = (layout.orders >= 0)[:, None]
    basis = np.concatenate([np.cos(angles) * live, -np.sin(angles) * live])
    factor = np.where(layout.orders == 0, 1.0, 2.0)[:, None]
    inverse = basis * np.concatenate([factor, factor])
    return to_bf16(basis), to_bf16(inverse)


@functools.lru_cache(maxsize=None)
def legendre_constants(parts, local):
    layout = Layout(parts, local)
    plain, weighted = legendre_table()
    rows, degrees, low, pairs = layout.rows, layout.degrees, layout.low, layout.pairs
    analysis = np.zeros((low, 2 * parts * rows, degrees))
    synth_low = np.zeros((low, parts * rows, degrees))
    pair_fwd = np.zeros((parts, pairs, rows, 2 * rows))
    pair_back = np.zeros((parts, pairs, rows, 2 * rows))
    for part in range(parts):
        own = slice(part * local, (part + 1) * local)
        start = part * rows
        synth_low[:, start : start + local, :MODES] = np.swapaxes(plain[:low, :, own], 1, 2)
        for turn in (1, 2):
            start = (turn * parts - 1 - part) * rows
            analysis[:, start : start + local, :MODES] = np.swapaxes(weighted[:low, :, own], 1, 2)
        for pair in range(pairs):
            order = low + pair
            mate = layout.partner - order
            for target, table in ((pair_fwd, weighted), (pair_back, plain)):
                count = MODES - order
                target[part, pair, rows - count :, :local] = table[order, order:, own]
                if mate != order:
                    count = MODES - mate
                    target[part, pair, :count, rows : rows + local] = table[mate, mate:, own][::-1]
    place = np.zeros((degrees, 2 * rows))
    for row in range(rows):
        if row >= rows - MODES + low:
            place[MODES - rows + row, row] = 1.0
        if MODES - 1 - row >= 0:
            place[MODES - 1 - row, rows + row] = 1.0
    return {
        "analysis": to_bf16(analysis),
        "synth_low": to_bf16(synth_low),
        "pair_fwd": to_bf16(pair_fwd),
        "pair_back": to_bf16(pair_back),
        "pair_synth": to_bf16(np.swapaxes(pair_back, -1, -2)),
        "place": place.astype(np.float32),
    }


def dot(left, right, sides=(1, 0)):
    contract = (((sides[0],), (sides[1],)), ((), ()))
    return lax.dot_general(left, right, contract, preferred_element_type=jnp.float32)


def swap_halves(values):
    return pltpu.roll(values, LANES // 2, 1)


def interleave(first, second):
    lane = lax.broadcasted_iota(jnp.int32, first.shape, 1)
    below = lane < LANES // 2
    return (
        jnp.where(below, first, swap_halves(second)),
        jnp.where(below, swap_halves(first), second),
    )


def gelu_slope(values):
    size = jnp.abs(values)
    step = 1.0 / (1.0 + 0.2316419 * size)
    scale = 1.0 / math.sqrt(2.0 * math.pi)
    series = 1.330274429 * scale
    for term in (-1.821255978, 1.781477937, -0.356563782, 0.319381530):
        series = series * step + term * scale
    below = jnp.exp(-0.5 * values * values) * (series * step - scale * size)
    return jnp.where(values >= 0.0, 1.0 - below, below)


def grid_rows(layout, north, south, quad, group):
    rows = []
    for pair in (2 * quad, 2 * quad + 1):
        rows.append(north[0, pair])
        values = south[0, pair]
        if layout.rows > layout.local:
            latitude = layout.half + group * PAIRS + pair
            values = jnp.where(latitude < layout.local, values, jnp.zeros_like(values))
        rows.append(values)
    return jnp.concatenate(rows, axis=0)


def scatter_rows(layout, values, scratch, quad, group):
    slots = layout.slots
    for which in range(2):
        columns = slice(which * LANES, (which + 1) * LANES)
        upper, lower = interleave(values[:slots, columns], values[slots:, columns])
        latitude = group * PAIRS + 2 * quad + which
        scratch[pl.ds(latitude, slots, stride=layout.pitch), :] = upper
        scratch[pl.ds(latitude + layout.half, slots, stride=layout.pitch), :] = lower


def gather_rows(layout, scratch, quad, group):
    slots = layout.slots
    cosine, sine = [], []
    for which in range(2):
        latitude = group * PAIRS + 2 * quad + which
        upper = scratch[pl.ds(latitude, slots, stride=layout.pitch), :]
        lower = scratch[pl.ds(latitude + layout.half, slots, stride=layout.pitch), :]
        first, second = interleave(upper, lower)
        cosine.append(first.astype(jnp.bfloat16))
        sine.append(second.astype(jnp.bfloat16))
    return jnp.concatenate(
        [jnp.concatenate(cosine, axis=1), jnp.concatenate(sine, axis=1)], axis=0
    )


def order_rows(layout, scratch, first, count):
    parts = []
    for order in range(count):
        start = pl.multiple_of((first + order) * layout.pitch, 8)
        parts.append(scratch[pl.ds(start, layout.rows), :])
    return jnp.concatenate(parts, axis=0).astype(jnp.bfloat16)


def band_copies(layout, chunk, fields, buffer, sems):
    width = LANES // 2
    copies = []
    for group in range(layout.half // PAIRS):
        started = []
        for side in range(2):
            first = side * layout.half + group * PAIRS
            count = min(PAIRS, layout.local - first)
            if count > 0:
                started.append(
                    pltpu.make_async_copy(
                        fields.at[0, pl.ds(first, count), pl.ds(chunk * width, width), :],
                        buffer.at[pl.ds(first, count)],
                        sems.at[2 * group + side],
                    )
                )
        copies.append(started)
    return copies


def forward_kernel(layout, chunk, index, fields, basis, pair_all, out, scratch, buffer, pair_fwd, sems, pair_sem):
    copies = band_copies(layout, chunk, fields, buffer, sems)
    for started in copies:
        for copy in started:
            copy.start()
    tables = pltpu.make_async_copy(pair_all.at[index[0]], pair_fwd, pair_sem)
    tables.start()
    if layout.rows > layout.local:
        shape = (layout.rows - layout.local,) + buffer.shape[1:]
        buffer[layout.local :] = jnp.zeros(shape, buffer.dtype)
    for group, started in enumerate(copies):
        for copy in started:
            copy.wait()
        for quad in range(PAIRS // 2):
            rows = []
            for which in range(2):
                latitude = group * PAIRS + 2 * quad + which
                rows += [buffer[latitude], buffer[latitude + layout.half]]
            grid = jnp.concatenate(rows, axis=0)
            scatter_rows(layout, dot(basis[...], grid, (1, 1)), scratch, quad, group)
    tables.wait()

    def low_block(order, carry):
        out[order] = order_rows(layout, scratch, order, 1)
        return carry

    def pair_block(pair, carry):
        values = order_rows(layout, scratch, layout.low + 2 * pair, 2)
        out[layout.low + pair] = dot(pair_fwd[pair], values).astype(jnp.bfloat16)
        return carry

    lax.fori_loop(0, layout.low, low_block, 0, unroll=8)
    lax.fori_loop(0, layout.pairs, pair_block, 0, unroll=8)


def mix(spectral, swapped, real_rows, imag_rows):
    return (spectral * real_rows + swapped * imag_rows).astype(jnp.bfloat16)


def spectral_kernel(layout, carries, *refs):
    ahead = None
    if carries:
        ahead, refs = refs[0], refs[1:]
    own, others = refs[0], refs[1 : layout.parts]
    north, south, basis, analysis, synth_low, back_low = refs[layout.parts : layout.parts + 6]
    pair_synth, pair_back, place, real_ref, imag_ref = refs[layout.parts + 6 : layout.parts + 11]
    out, scratch, returned, spec_low, swap_low, spec_pair, swap_pair = refs[layout.parts + 11 :]
    group = pl.program_id(0)
    rows, degrees, low = layout.rows, layout.degrees, layout.low

    def groups():
        for start in range(0, low, GROUP):
            yield start, min(start + GROUP, low), start // 16 * 16

    @pl.when(group == 0)
    def _():
        for start, stop, top in groups():
            real_rows = real_ref[top:degrees, :]
            imag_rows = imag_ref[top:degrees, :]

            def low_block(order, carry):
                values = jnp.concatenate([own[order]] + [ref[order] for ref in others], axis=0)
                spectral = dot(analysis[order, top:degrees, :], values).astype(jnp.bfloat16)
                spec_low[order, top:degrees, :] = spectral
                return carry

            def mix_block(order, carry):
                spectral = spec_low[order, top:degrees, :].astype(jnp.float32)
                swapped = swap_halves(spectral)
                swap_low[order, top:degrees, :] = swapped.astype(jnp.bfloat16)
                mixed = mix(spectral, swapped, real_rows, imag_rows)
                begin = pl.multiple_of(order * layout.pitch, 8)
                scratch[pl.ds(begin, rows), :] = dot(synth_low[order, :, top:degrees], mixed)
                return carry

            lax.fori_loop(start, stop, low_block, 0, unroll=8)
            lax.fori_loop(start, stop, mix_block, 0, unroll=8)

        line = lax.broadcasted_iota(jnp.int32, (rows, LANES), 0)

        def pair_block(pair, carry):
            total = own[low + pair].astype(jnp.float32)
            for ref in others:
                total = total + ref[low + pair].astype(jnp.float32)
            spectral = total.astype(jnp.bfloat16)
            spec_pair[pair] = spectral
            natural = line >= layout.first_natural + pair
            real_rows = jnp.where(natural, real_ref[degrees : degrees + rows, :], real_ref[degrees + rows :, :])
            imag_rows = jnp.where(natural, imag_ref[degrees : degrees + rows, :], imag_ref[degrees + rows :, :])
            spectral = spectral.astype(jnp.float32)
            swapped = swap_halves(spectral)
            swap_pair[pair] = swapped.astype(jnp.bfloat16)
            mixed = mix(spectral, swapped, real_rows, imag_rows)
            values = dot(pair_synth[pair], mixed)
            for which in range(2):
                begin = pl.multiple_of((low + 2 * pair + which) * layout.pitch, 8)
                scratch[pl.ds(begin, rows), :] = values[which * rows : (which + 1) * rows]
            return carry

        lax.fori_loop(0, layout.pairs, pair_block, 0, unroll=8)
        used = (low + 2 * layout.pairs) * layout.pitch
        if used < layout.slots * layout.pitch:
            scratch[used : layout.slots * layout.pitch, :] = jnp.zeros(
                (layout.slots * layout.pitch - used, LANES), jnp.float32
            )

    for quad in range(PAIRS // 2):
        modes = gather_rows(layout, scratch, quad, group)
        signal = dot(modes, basis[...], (0, 0))
        incoming = grid_rows(layout, north, south, quad, group).astype(jnp.float32)
        upstream = (incoming * gelu_slope(signal)).astype(jnp.bfloat16)
        scatter_rows(layout, dot(basis[...], upstream, (1, 1)), returned, quad, group)

    @pl.when(group == pl.num_programs(0) - 1)
    def _():
        def products(spectral, swapped, back):
            return spectral.astype(jnp.float32) * back, swapped.astype(jnp.float32) * back

        zeros = jnp.zeros((degrees, LANES), jnp.float32)
        same, cross = zeros, zeros
        for start, stop, top in groups():

            def low_block(order, carry):
                back = dot(back_low[order, top:degrees, :], order_rows(layout, returned, order, 1))
                first, second = products(
                    spec_low[order, top:degrees, :], swap_low[order, top:degrees, :], back
                )
                return carry[0] + first, carry[1] + second

            part = jnp.zeros((degrees - top, LANES), jnp.float32)
            first, second = lax.fori_loop(start, stop, low_block, (part, part), unroll=8)
            if top:
                empty = jnp.zeros((top, LANES), jnp.float32)
                first = jnp.concatenate([empty, first], axis=0)
                second = jnp.concatenate([empty, second], axis=0)
            same, cross = same + first, cross + second

        line = lax.broadcasted_iota(jnp.int32, (rows, LANES), 0)

        def pair_block(pair, carry):
            back = dot(pair_back[pair], order_rows(layout, returned, low + 2 * pair, 2))
            first, second = products(spec_pair[pair], swap_pair[pair], back)
            natural = line >= layout.first_natural + pair
            return (
                carry[0] + jnp.where(natural, first, 0.0),
                carry[1] + jnp.where(natural, second, 0.0),
                carry[2] + jnp.where(natural, 0.0, first),
                carry[3] + jnp.where(natural, 0.0, second),
            )

        part = jnp.zeros((rows, LANES), jnp.float32)
        sums = lax.fori_loop(0, layout.pairs, pair_block, (part,) * 4, unroll=8)
        placed = jnp.dot(
            place[...],
            jnp.concatenate(
                [jnp.concatenate(sums[:2], axis=1), jnp.concatenate(sums[2:], axis=1)], axis=0
            ),
            preferred_element_type=jnp.float32,
            precision=lax.Precision.HIGHEST,
        )
        same = same + placed[:, :LANES]
        cross = cross + placed[:, LANES:]
        real = same + swap_halves(same)
        imag = cross - swap_halves(cross)
        lane = lax.broadcasted_iota(jnp.int32, real.shape, 1)
        grads = jnp.where(lane < LANES // 2, real, imag)
        out[out.shape[0] - LANES :, :] = grads.T
        if ahead is not None:
            out[: out.shape[0] - LANES, :] = ahead[...]


def grid_specs(layout, chunk):
    last = -(-layout.local // PAIRS) - 1
    shift = layout.half // PAIRS
    block = (1, PAIRS, LANES // 2, NLON)
    return [
        pl.BlockSpec(block, lambda g: (0, jnp.minimum(g, last), chunk, 0)),
        pl.BlockSpec(block, lambda g: (0, jnp.minimum(shift + g, last), chunk, 0)),
    ]


def whole():
    return pl.BlockSpec(memory_space=pltpu.VMEM)


def forward_call(layout, chunk, index, fields, basis, pair_fwd):
    work = 2 * 2 * layout.slots * NLON * layout.rows * LANES // 2
    groups = layout.half // PAIRS
    return pl.pallas_call(
        functools.partial(forward_kernel, layout, chunk),
        in_specs=[
            pl.BlockSpec(memory_space=pltpu.SMEM),
            pl.BlockSpec(memory_space=pl.ANY),
            whole(),
            pl.BlockSpec(memory_space=pl.ANY),
        ],
        out_specs=whole(),
        out_shape=jax.ShapeDtypeStruct((layout.blocks, layout.rows, LANES), jnp.bfloat16),
        scratch_shapes=[
            pltpu.VMEM((layout.slots * layout.pitch, LANES), jnp.float32),
            pltpu.VMEM((layout.rows, LANES // 2, NLON), jnp.bfloat16),
            pltpu.VMEM(pair_fwd.shape[1:], jnp.bfloat16),
            pltpu.SemaphoreType.DMA((2 * groups,)),
            pltpu.SemaphoreType.DMA,
        ],
        compiler_params=pltpu.CompilerParams(vmem_limit_bytes=FORWARD_VMEM),
        cost_estimate=pl.CostEstimate(flops=2 * work, bytes_accessed=8_000_000, transcendentals=0),
        name=f"forward_{chunk}",
    )(index, fields, basis, pair_fwd)


def spectral_call(layout, chunk, coeffs, cotangent, tables, real_rows, imag_rows, ahead=None):
    work = 2 * 2 * layout.slots * NLON * layout.rows * LANES // 2
    operands = list(coeffs) + [cotangent, cotangent] + list(tables) + [real_rows, imag_rows]
    specs = [whole()] * layout.parts + grid_specs(layout, chunk) + [whole()] * (len(tables) + 2)
    height = LANES
    if ahead is not None:
        operands, specs = [ahead] + operands, [whole()] + specs
        height += ahead.shape[0]
    return pl.pallas_call(
        functools.partial(spectral_kernel, layout, ahead is not None),
        grid=(layout.half // PAIRS,),
        in_specs=specs,
        out_specs=whole(),
        out_shape=jax.ShapeDtypeStruct((height, layout.degrees), jnp.float32),
        scratch_shapes=[
            pltpu.VMEM((layout.slots * layout.pitch, LANES), jnp.float32),
            pltpu.VMEM((layout.slots * layout.pitch, LANES), jnp.float32),
            pltpu.VMEM((layout.low, layout.degrees, LANES), jnp.bfloat16),
            pltpu.VMEM((layout.low, layout.degrees, LANES), jnp.bfloat16),
            pltpu.VMEM((layout.pairs, layout.rows, LANES), jnp.bfloat16),
            pltpu.VMEM((layout.pairs, layout.rows, LANES), jnp.bfloat16),
        ],
        compiler_params=pltpu.CompilerParams(vmem_limit_bytes=VMEM),
        cost_estimate=pl.CostEstimate(flops=6 * work, bytes_accessed=16_000_000, transcendentals=0),
        name=f"spectral_{chunk}",
    )(*operands)


def radices(size):
    found, factor = [], 2
    while size > 1:
        while size % factor == 0:
            found.append(factor)
            size //= factor
        factor += 1
    return found


def sum_over(value, axis):
    size = lax.axis_size(axis)
    stride = 1
    for radix in radices(size):
        total = value
        for turn in range(1, radix):
            pairs = []
            for index in range(size):
                digit = index // stride % radix
                pairs.append((index, index + ((digit + turn) % radix - digit) * stride))
            total = total + lax.ppermute(value, axis, pairs)
        value = total
        stride *= radix
    return value


def filter_rows(layout, spec):
    padded = jnp.pad(spec, ((0, layout.degrees - MODES), (0, 0)))
    front = jnp.pad(spec, ((layout.rows, layout.rows), (0, 0)))
    natural = front[MODES : MODES + layout.rows]
    backward = front[layout.rows + MODES - layout.rows : layout.rows + MODES][::-1]
    return jnp.concatenate([padded, natural, backward], axis=0).astype(jnp.float32)


def on_device(fields, cotangent, spec_real, spec_imag):
    parts = lax.axis_size("space")
    index = lax.axis_index("space")
    layout = Layout(parts, fields.shape[1])
    width = LANES // 2
    chunks = fields.shape[-1] // width
    basis, inverse = (jnp.asarray(a) for a in fourier_constants(parts, layout.local))
    constants = legendre_constants(parts, layout.local)

    def local_table(name):
        return lax.dynamic_index_in_dim(jnp.asarray(constants[name]), index, keepdims=False)

    pair_fwd = jnp.asarray(constants["pair_fwd"])
    place = jnp.reshape(index, (1,)).astype(jnp.int32)
    def bands(name, first, count):
        table = jnp.asarray(constants[name])
        return lax.optimization_barrier(
            lax.dynamic_slice_in_dim(table, first * layout.rows, count * layout.rows, 1)
        )

    analysis = jnp.swapaxes(bands("analysis", parts - 1 - index, parts), 1, 2)
    synth_low = bands("synth_low", index, 1)
    back_low = jnp.swapaxes(synth_low, 1, 2)
    pair_tables = [local_table(name) for name in ("pair_synth", "pair_back")]
    tables = [inverse, analysis, synth_low, back_low] + pair_tables + [jnp.asarray(constants["place"])]
    fields, cotangent = jnp.swapaxes(fields, 2, 3), jnp.swapaxes(cotangent, 2, 3)
    real_all = filter_rows(layout, spec_real)
    imag_all = filter_rows(layout, spec_imag)

    received = []
    for chunk in range(chunks):
        own = forward_call(layout, chunk, place, fields, basis, pair_fwd)
        blocks = [own]
        for shift in range(1, parts):
            route = [(source, (source + shift) % parts) for source in range(parts)]
            blocks.append(lax.ppermute(own, "space", route))
        received.append(blocks)

    totals, ahead = [], None
    for chunk in range(chunks):
        columns = slice(chunk * width, (chunk + 1) * width)
        real, imag = real_all[:, columns], imag_all[:, columns]
        real_rows = jnp.concatenate([real, real], axis=1)
        imag_rows = jnp.concatenate([-imag, imag], axis=1)
        coeffs = received[chunk]
        if totals:
            coeffs[0], totals[-1] = lax.optimization_barrier((coeffs[0], totals[-1]))
        grads = spectral_call(layout, chunk, coeffs, cotangent, tables, real_rows, imag_rows, ahead)
        if chunk == chunks - 2:
            ahead = grads
        else:
            totals.append(sum_over(sum_over(grads, "dp"), "space"))

    batch_total = fields.shape[0] * lax.axis_size("dp")
    rows = jnp.concatenate(totals, axis=0).reshape(chunks, 2, width, layout.degrees)
    real, imag = (rows[:, part, :, :MODES].reshape(chunks * width, MODES) for part in range(2))
    return (real.T / batch_total, imag.T / batch_total)


def solution(mesh):
    in_specs = (P("dp", "space", None, None), P("dp", "space", None, None), P(), P())
    out_specs = (P(), P())
    return jax.shard_map(
        on_device, mesh=mesh, in_specs=in_specs, out_specs=out_specs, check_vma=False
    )
```

```python
import functools
import math

import jax
import jax.numpy as jnp
import ml_dtypes
import numpy as np
from jax import lax
from jax.experimental import pallas as pl
from jax.experimental.pallas import tpu as pltpu
from jax.sharding import PartitionSpec as P

NLAT = 126
NLON = 252
MODES = 126
LANES = 128
GROUP = 16
PAIRS = 8
VMEM = 30 * 1024 * 1024
FORWARD_VMEM = 56 * 1024 * 1024


def round_up(value, step):
    return -(-value // step) * step


def legendre_table():
    colatitude = math.pi * (np.arange(NLAT) + 0.5) / NLAT
    cos_theta, sin_theta = np.cos(colatitude), np.sin(colatitude)
    counters = np.arange(1, MODES)
    log_steps = 0.5 * np.log((2.0 * counters + 1.0) / (2.0 * counters))
    log_table = np.concatenate([[0.0], np.cumsum(log_steps)])
    table = np.zeros((MODES, MODES, NLAT))
    for order in range(MODES):
        table[order, order] = np.exp(
            0.5 * math.log(1.0 / (4.0 * math.pi)) + log_table[order] + order * np.log(sin_theta)
        )
        for degree in range(order + 1, MODES):
            growth = math.sqrt((4.0 * degree**2 - 1.0) / (degree**2 - order**2))
            below = degree - 1
            current = cos_theta * table[order, below]
            if below > order:
                damping = math.sqrt((below**2 - order**2) / (4.0 * below**2 - 1.0))
                current = current - damping * table[order, degree - 2]
            table[order, degree] = growth * current
    weight = math.pi / NLAT * (2.0 * math.pi / NLON) * sin_theta
    return table, table * weight


def to_bf16(array):
    return np.where(np.abs(array) < 2.0**-126, 0.0, array).astype(ml_dtypes.bfloat16)


class Layout:
    def __init__(self, parts, local):
        self.parts, self.local = parts, local
        self.rows = round_up(local + 1, 16)
        self.half = self.rows // 2
        self.pitch = self.rows + 8
        self.low = max(MODES - local, 0)
        high = MODES - self.low
        self.pairs = (high + 1) // 2
        self.blocks = self.low + self.pairs
        self.slots = round_up(self.low + 2 * self.pairs, 8)
        self.degrees = round_up(MODES, 16)
        self.first_natural = self.rows - MODES + self.low
        self.partner = MODES - 1 + self.low
        orders = list(range(self.low))
        for pair in range(self.pairs):
            order = self.low + pair
            orders += [order, self.partner - order if self.partner - order != order else -1]
        self.orders = np.array(orders + [-1] * (self.slots - len(orders)))
        self.split = round_up(self.low // 2, GROUP)

    def piece_slots(self, first, last):
        start = first + max(first - self.low, 0)
        stop = last + max(last - self.low, 0)
        return start, round_up(stop - start, 8)


@functools.lru_cache(maxsize=None)
def fourier_constants(layout, first, last):
    start, slots = layout.piece_slots(first, last)
    live_orders = np.full(slots, -1)
    part = layout.orders[start : start + slots]
    live_orders[: len(part)] = part
    stop = last + max(last - layout.low, 0)
    live_orders[stop - start :] = -1
    orders = np.maximum(live_orders, 0)
    angles = 2.0 * math.pi / NLON * (orders[:, None] * np.arange(NLON)[None] % NLON)
    live = (live_orders >= 0)[:, None]
    basis = np.concatenate([np.cos(angles) * live, -np.sin(angles) * live])
    factor = np.where(live_orders == 0, 1.0, 2.0)[:, None]
    inverse = basis * np.concatenate([factor, factor])
    return to_bf16(basis), to_bf16(inverse)


@functools.lru_cache(maxsize=None)
def legendre_constants(parts, local):
    layout = Layout(parts, local)
    plain, weighted = legendre_table()
    rows, degrees, low, pairs = layout.rows, layout.degrees, layout.low, layout.pairs
    analysis = np.zeros((low, 2 * parts * rows, degrees))
    synth_low = np.zeros((low, parts * rows, degrees))
    pair_fwd = np.zeros((parts, pairs, rows, 2 * rows))
    pair_back = np.zeros((parts, pairs, rows, 2 * rows))
    for part in range(parts):
        own = slice(part * local, (part + 1) * local)
        start = part * rows
        synth_low[:, start : start + local, :MODES] = np.swapaxes(plain[:low, :, own], 1, 2)
        for turn in (1, 2):
            start = (turn * parts - 1 - part) * rows
            analysis[:, start : start + local, :MODES] = np.swapaxes(weighted[:low, :, own], 1, 2)
        for pair in range(pairs):
            order = low + pair
            mate = layout.partner - order
            for target, table in ((pair_fwd, weighted), (pair_back, plain)):
                count = MODES - order
                target[part, pair, rows - count :, :local] = table[order, order:, own]
                if mate != order:
                    count = MODES - mate
                    target[part, pair, :count, rows : rows + local] = table[mate, mate:, own][::-1]
    place = np.zeros((degrees, 2 * rows))
    for row in range(rows):
        if row >= rows - MODES + low:
            place[MODES - rows + row, row] = 1.0
        if MODES - 1 - row >= 0:
            place[MODES - 1 - row, rows + row] = 1.0
    return {
        "analysis": to_bf16(analysis),
        "synth_low": to_bf16(synth_low),
        "pair_fwd": to_bf16(pair_fwd),
        "pair_back": to_bf16(pair_back),
        "pair_synth": to_bf16(np.swapaxes(pair_back, -1, -2)),
        "place": place.astype(np.float32),
    }


def dot(left, right, sides=(1, 0)):
    contract = (((sides[0],), (sides[1],)), ((), ()))
    return lax.dot_general(left, right, contract, preferred_element_type=jnp.float32)


def swap_halves(values):
    return pltpu.roll(values, LANES // 2, 1)


def interleave(first, second):
    lane = lax.broadcasted_iota(jnp.int32, first.shape, 1)
    below = lane < LANES // 2
    return (
        jnp.where(below, first, swap_halves(second)),
        jnp.where(below, swap_halves(first), second),
    )


def gelu_slope(values):
    cumulative = 0.5 * (1.0 + lax.erf(values / math.sqrt(2.0)))
    density = jnp.exp(-0.5 * values * values) / math.sqrt(2.0 * math.pi)
    return cumulative + values * density


def grid_rows(layout, north, south, quad, group):
    rows = []
    for pair in (2 * quad, 2 * quad + 1):
        rows.append(north[0, pair])
        values = south[0, pair]
        if layout.rows > layout.local:
            latitude = layout.half + group * PAIRS + pair
            values = jnp.where(latitude < layout.local, values, jnp.zeros_like(values))
        rows.append(values)
    return jnp.concatenate(rows, axis=0)


def scatter_rows(layout, values, scratch, quad, group):
    slots = values.shape[0] // 2
    for which in range(2):
        columns = slice(which * LANES, (which + 1) * LANES)
        upper, lower = interleave(values[:slots, columns], values[slots:, columns])
        latitude = group * PAIRS + 2 * quad + which
        scratch[pl.ds(latitude, slots, stride=layout.pitch), :] = upper
        scratch[pl.ds(latitude + layout.half, slots, stride=layout.pitch), :] = lower


def gather_rows(layout, scratch, quad, group):
    slots = layout.slots
    cosine, sine = [], []
    for which in range(2):
        latitude = group * PAIRS + 2 * quad + which
        upper = scratch[pl.ds(latitude, slots, stride=layout.pitch), :]
        lower = scratch[pl.ds(latitude + layout.half, slots, stride=layout.pitch), :]
        first, second = interleave(upper, lower)
        cosine.append(first.astype(jnp.bfloat16))
        sine.append(second.astype(jnp.bfloat16))
    return jnp.concatenate(
        [jnp.concatenate(cosine, axis=1), jnp.concatenate(sine, axis=1)], axis=0
    )


def order_rows(layout, scratch, first, count):
    parts = []
    for order in range(count):
        start = pl.multiple_of((first + order) * layout.pitch, 8)
        parts.append(scratch[pl.ds(start, layout.rows), :])
    return jnp.concatenate(parts, axis=0).astype(jnp.bfloat16)


def band_copies(layout, chunk, fields, buffer, sems):
    width = LANES // 2
    copies = []
    for group in range(layout.half // PAIRS):
        started = []
        for side in range(2):
            first = side * layout.half + group * PAIRS
            count = min(PAIRS, layout.local - first)
            if count > 0:
                started.append(
                    pltpu.make_async_copy(
                        fields.at[0, pl.ds(first, count), pl.ds(chunk * width, width), :],
                        buffer.at[pl.ds(first, count)],
                        sems.at[2 * group + side],
                    )
                )
        copies.append(started)
    return copies


def forward_kernel(layout, chunk, first, last, index, fields, basis, pair_all, out, scratch, buffer, pair_fwd, sems, pair_sem):
    copies = band_copies(layout, chunk, fields, buffer, sems)
    for started in copies:
        for copy in started:
            copy.start()
    if last > layout.low:
        tables = pltpu.make_async_copy(pair_all.at[index[0]], pair_fwd, pair_sem)
        tables.start()
    if layout.rows > layout.local:
        shape = (layout.rows - layout.local,) + buffer.shape[1:]
        buffer[layout.local :] = jnp.zeros(shape, buffer.dtype)
    for group, started in enumerate(copies):
        for copy in started:
            copy.wait()
        for quad in range(PAIRS // 2):
            rows = []
            for which in range(2):
                latitude = group * PAIRS + 2 * quad + which
                rows += [buffer[latitude], buffer[latitude + layout.half]]
            grid = jnp.concatenate(rows, axis=0)
            scatter_rows(layout, dot(basis[...], grid, (1, 1)), scratch, quad, group)
    if last > layout.low:
        tables.wait()

    lows = min(last, layout.low) - first

    def low_block(order, carry):
        out[order] = order_rows(layout, scratch, order, 1)
        return carry

    def pair_block(pair, carry):
        values = order_rows(layout, scratch, lows + 2 * pair, 2)
        out[lows + pair] = dot(pair_fwd[pair], values).astype(jnp.bfloat16)
        return carry

    lax.fori_loop(0, lows, low_block, 0, unroll=8)
    lax.fori_loop(0, last - first - lows, pair_block, 0, unroll=8)


def mix(spectral, swapped, real_rows, imag_rows):
    return (spectral * real_rows + swapped * imag_rows).astype(jnp.bfloat16)


def spectral_kernel(layout, carries, bounds, *refs):
    ahead = None
    if carries:
        ahead, refs = refs[0], refs[1:]
    pieces = [refs[at : at + layout.parts] for at in range(0, layout.parts * (len(bounds) - 1), layout.parts)]
    refs = refs[layout.parts * len(pieces) :]

    def sources(block):
        at = max(at for at in range(len(pieces)) if bounds[at] <= block)
        return pieces[at], bounds[at]

    north, south, basis, analysis, synth_low, back_low = refs[:6]
    pair_synth, pair_back, place, real_ref, imag_ref = refs[6:11]
    out, scratch, returned, spec_low, swap_low, spec_pair, swap_pair = refs[11:]
    group = pl.program_id(0)
    rows, degrees, low = layout.rows, layout.degrees, layout.low

    def groups():
        for start in range(0, low, GROUP):
            yield start, min(start + GROUP, low), start // 16 * 16

    @pl.when(group == 0)
    def _():
        for start, stop, top in groups():
            real_rows = real_ref[top:degrees, :]
            imag_rows = imag_ref[top:degrees, :]
            held, offset = sources(start)

            def low_block(order, carry):
                values = jnp.concatenate([ref[order - offset] for ref in held], axis=0)
                spectral = dot(analysis[order, top:degrees, :], values).astype(jnp.bfloat16)
                spec_low[order, top:degrees, :] = spectral
                return carry

            def mix_block(order, carry):
                spectral = spec_low[order, top:degrees, :].astype(jnp.float32)
                swapped = swap_halves(spectral)
                swap_low[order, top:degrees, :] = swapped.astype(jnp.bfloat16)
                mixed = mix(spectral, swapped, real_rows, imag_rows)
                begin = pl.multiple_of(order * layout.pitch, 8)
                scratch[pl.ds(begin, rows), :] = dot(synth_low[order, :, top:degrees], mixed)
                return carry

            lax.fori_loop(start, stop, low_block, 0, unroll=8)
            lax.fori_loop(start, stop, mix_block, 0, unroll=8)

        line = lax.broadcasted_iota(jnp.int32, (rows, LANES), 0)

        held, offset = sources(low)

        def pair_block(pair, carry):
            total = sum(ref[low + pair - offset].astype(jnp.float32) for ref in held)
            spectral = total.astype(jnp.bfloat16)
            spec_pair[pair] = spectral
            natural = line >= layout.first_natural + pair
            real_rows = jnp.where(natural, real_ref[degrees : degrees + rows, :], real_ref[degrees + rows :, :])
            imag_rows = jnp.where(natural, imag_ref[degrees : degrees + rows, :], imag_ref[degrees + rows :, :])
            spectral = spectral.astype(jnp.float32)
            swapped = swap_halves(spectral)
            swap_pair[pair] = swapped.astype(jnp.bfloat16)
            mixed = mix(spectral, swapped, real_rows, imag_rows)
            values = dot(pair_synth[pair], mixed)
            for which in range(2):
                begin = pl.multiple_of((low + 2 * pair + which) * layout.pitch, 8)
                scratch[pl.ds(begin, rows), :] = values[which * rows : (which + 1) * rows]
            return carry

        lax.fori_loop(0, layout.pairs, pair_block, 0, unroll=8)
        used = (low + 2 * layout.pairs) * layout.pitch
        if used < layout.slots * layout.pitch:
            scratch[used : layout.slots * layout.pitch, :] = jnp.zeros(
                (layout.slots * layout.pitch - used, LANES), jnp.float32
            )

    for quad in range(PAIRS // 2):
        modes = gather_rows(layout, scratch, quad, group)
        signal = dot(modes, basis[...], (0, 0))
        incoming = grid_rows(layout, north, south, quad, group).astype(jnp.float32)
        upstream = (incoming * gelu_slope(signal)).astype(jnp.bfloat16)
        scatter_rows(layout, dot(basis[...], upstream, (1, 1)), returned, quad, group)

    @pl.when(group == pl.num_programs(0) - 1)
    def _():
        def products(spectral, swapped, back):
            return spectral.astype(jnp.float32) * back, swapped.astype(jnp.float32) * back

        zeros = jnp.zeros((degrees, LANES), jnp.float32)
        same, cross = zeros, zeros
        for start, stop, top in groups():

            def low_block(order, carry):
                back = dot(back_low[order, top:degrees, :], order_rows(layout, returned, order, 1))
                first, second = products(
                    spec_low[order, top:degrees, :], swap_low[order, top:degrees, :], back
                )
                return carry[0] + first, carry[1] + second

            part = jnp.zeros((degrees - top, LANES), jnp.float32)
            first, second = lax.fori_loop(start, stop, low_block, (part, part), unroll=8)
            if top:
                empty = jnp.zeros((top, LANES), jnp.float32)
                first = jnp.concatenate([empty, first], axis=0)
                second = jnp.concatenate([empty, second], axis=0)
            same, cross = same + first, cross + second

        line = lax.broadcasted_iota(jnp.int32, (rows, LANES), 0)

        def pair_block(pair, carry):
            back = dot(pair_back[pair], order_rows(layout, returned, low + 2 * pair, 2))
            first, second = products(spec_pair[pair], swap_pair[pair], back)
            natural = line >= layout.first_natural + pair
            return (
                carry[0] + jnp.where(natural, first, 0.0),
                carry[1] + jnp.where(natural, second, 0.0),
                carry[2] + jnp.where(natural, 0.0, first),
                carry[3] + jnp.where(natural, 0.0, second),
            )

        part = jnp.zeros((rows, LANES), jnp.float32)
        sums = lax.fori_loop(0, layout.pairs, pair_block, (part,) * 4, unroll=8)
        placed = jnp.dot(
            place[...],
            jnp.concatenate(
                [jnp.concatenate(sums[:2], axis=1), jnp.concatenate(sums[2:], axis=1)], axis=0
            ),
            preferred_element_type=jnp.float32,
            precision=lax.Precision.HIGHEST,
        )
        same = same + placed[:, :LANES]
        cross = cross + placed[:, LANES:]
        real = same + swap_halves(same)
        imag = cross - swap_halves(cross)
        lane = lax.broadcasted_iota(jnp.int32, real.shape, 1)
        grads = jnp.where(lane < LANES // 2, real, imag)
        out[out.shape[0] - LANES :, :] = grads.T
        if ahead is not None:
            out[: out.shape[0] - LANES, :] = ahead[...]


def grid_specs(layout, chunk):
    last = -(-layout.local // PAIRS) - 1
    shift = layout.half // PAIRS
    block = (1, PAIRS, LANES // 2, NLON)
    return [
        pl.BlockSpec(block, lambda g: (0, jnp.minimum(g, last), chunk, 0)),
        pl.BlockSpec(block, lambda g: (0, jnp.minimum(shift + g, last), chunk, 0)),
    ]


def whole():
    return pl.BlockSpec(memory_space=pltpu.VMEM)


def forward_call(layout, chunk, first, last, index, fields, pair_fwd):
    basis = jnp.asarray(fourier_constants(layout, first, last)[0])
    slots = basis.shape[0] // 2
    work = 2 * 2 * slots * NLON * layout.rows * LANES // 2
    groups = layout.half // PAIRS
    return pl.pallas_call(
        functools.partial(forward_kernel, layout, chunk, first, last),
        in_specs=[
            pl.BlockSpec(memory_space=pltpu.SMEM),
            pl.BlockSpec(memory_space=pl.ANY),
            whole(),
            pl.BlockSpec(memory_space=pl.ANY),
        ],
        out_specs=whole(),
        out_shape=jax.ShapeDtypeStruct((last - first, layout.rows, LANES), jnp.bfloat16),
        scratch_shapes=[
            pltpu.VMEM((slots * layout.pitch, LANES), jnp.float32),
            pltpu.VMEM((layout.rows, LANES // 2, NLON), jnp.bfloat16),
            pltpu.VMEM(pair_fwd.shape[1:], jnp.bfloat16),
            pltpu.SemaphoreType.DMA((2 * groups,)),
            pltpu.SemaphoreType.DMA,
        ],
        compiler_params=pltpu.CompilerParams(vmem_limit_bytes=FORWARD_VMEM),
        cost_estimate=pl.CostEstimate(flops=2 * work, bytes_accessed=8_000_000, transcendentals=0),
        name=f"forward_{chunk}_{first}",
    )(index, fields, basis, pair_fwd)


def spectral_call(layout, chunk, bounds, coeffs, cotangent, tables, real_rows, imag_rows, ahead=None):
    work = 2 * 2 * layout.slots * NLON * layout.rows * LANES // 2
    operands = list(coeffs) + [cotangent, cotangent] + list(tables) + [real_rows, imag_rows]
    specs = [whole()] * len(coeffs) + grid_specs(layout, chunk) + [whole()] * (len(tables) + 2)
    height = LANES
    if ahead is not None:
        operands, specs = [ahead] + operands, [whole()] + specs
        height += ahead.shape[0]
    return pl.pallas_call(
        functools.partial(spectral_kernel, layout, ahead is not None, bounds),
        grid=(layout.half // PAIRS,),
        in_specs=specs,
        out_specs=whole(),
        out_shape=jax.ShapeDtypeStruct((height, layout.degrees), jnp.float32),
        scratch_shapes=[
            pltpu.VMEM((layout.slots * layout.pitch, LANES), jnp.float32),
            pltpu.VMEM((layout.slots * layout.pitch, LANES), jnp.float32),
            pltpu.VMEM((layout.low, layout.degrees, LANES), jnp.bfloat16),
            pltpu.VMEM((layout.low, layout.degrees, LANES), jnp.bfloat16),
            pltpu.VMEM((layout.pairs, layout.rows, LANES), jnp.bfloat16),
            pltpu.VMEM((layout.pairs, layout.rows, LANES), jnp.bfloat16),
        ],
        compiler_params=pltpu.CompilerParams(vmem_limit_bytes=VMEM),
        cost_estimate=pl.CostEstimate(flops=6 * work, bytes_accessed=16_000_000, transcendentals=0),
        name=f"spectral_{chunk}",
    )(*operands)


def radices(size):
    found, factor = [], 2
    while size > 1:
        while size % factor == 0:
            found.append(factor)
            size //= factor
        factor += 1
    return found


def sum_steps(axis):
    size = lax.axis_size(axis)
    steps, stride = [], 1
    for radix in radices(size):
        steps.append((axis, stride, radix))
        stride *= radix
    return steps


def sum_over(value, steps):
    for axis, stride, radix in steps:
        total = value
        for turn in range(1, radix):
            pairs = []
            for index in range(lax.axis_size(axis)):
                digit = index // stride % radix
                pairs.append((index, index + ((digit + turn) % radix - digit) * stride))
            total = total + lax.ppermute(value, axis, pairs)
        value = total
    return value


def filter_rows(layout, spec):
    padded = jnp.pad(spec, ((0, layout.degrees - MODES), (0, 0)))
    front = jnp.pad(spec, ((layout.rows, layout.rows), (0, 0)))
    natural = front[MODES : MODES + layout.rows]
    backward = front[layout.rows + MODES - layout.rows : layout.rows + MODES][::-1]
    return jnp.concatenate([padded, natural, backward], axis=0).astype(jnp.float32)


def on_device(fields, cotangent, spec_real, spec_imag):
    parts = lax.axis_size("space")
    index = lax.axis_index("space")
    layout = Layout(parts, fields.shape[1])
    width = LANES // 2
    chunks = fields.shape[-1] // width
    inverse = jnp.asarray(fourier_constants(layout, 0, layout.blocks)[1])
    constants = legendre_constants(parts, layout.local)

    def local_table(name):
        return lax.dynamic_index_in_dim(jnp.asarray(constants[name]), index, keepdims=False)

    pair_fwd = jnp.asarray(constants["pair_fwd"])
    place = jnp.reshape(index, (1,)).astype(jnp.int32)
    def bands(name, first, count):
        table = jnp.asarray(constants[name])
        return lax.optimization_barrier(
            lax.dynamic_slice_in_dim(table, first * layout.rows, count * layout.rows, 1)
        )

    analysis = jnp.swapaxes(bands("analysis", parts - 1 - index, parts), 1, 2)
    synth_low = bands("synth_low", index, 1)
    back_low = jnp.swapaxes(synth_low, 1, 2)
    pair_tables = [local_table(name) for name in ("pair_synth", "pair_back")]
    tables = [inverse, analysis, synth_low, back_low] + pair_tables + [jnp.asarray(constants["place"])]
    fields, cotangent = jnp.swapaxes(fields, 2, 3), jnp.swapaxes(cotangent, 2, 3)
    real_all = filter_rows(layout, spec_real)
    imag_all = filter_rows(layout, spec_imag)

    received = []
    for chunk in range(chunks):
        bounds = [0, layout.blocks] if chunk else sorted({0, layout.split, layout.blocks})
        blocks = []
        for first, last in zip(bounds, bounds[1:]):
            own = forward_call(layout, chunk, first, last, place, fields, pair_fwd)
            blocks.append(own)
            for shift in range(1, parts):
                route = [(source, (source + shift) % parts) for source in range(parts)]
                blocks.append(lax.ppermute(own, "space", route))
        received.append((tuple(bounds), blocks))

    steps = sum_steps("dp")
    early = []
    for chunk in range(chunks):
        columns = slice(chunk * width, (chunk + 1) * width)
        real, imag = real_all[:, columns], imag_all[:, columns]
        real_rows = jnp.concatenate([real, real], axis=1)
        imag_rows = jnp.concatenate([-imag, imag], axis=1)
        bounds, coeffs = received[chunk]
        if early:
            coeffs[0], early = lax.optimization_barrier((coeffs[0], early))
        ahead = grads if 0 < chunk == chunks - 1 else None
        grads = spectral_call(
            layout, chunk, bounds, coeffs, cotangent, tables, real_rows, imag_rows, ahead
        )
        half = len(steps) // 2
        if 0 < chunk <= len(early):
            early[chunk - 1], grads = lax.optimization_barrier((early[chunk - 1], grads))
            early[chunk - 1] = sum_over(early[chunk - 1], steps[half:])
        if chunk < chunks - 2:
            early.append(sum_over(grads, steps[:half]))
    rows = jnp.concatenate(early + [sum_over(grads, steps)], axis=0)
    rows = sum_over(rows, sum_steps("space")).reshape(chunks, 2, width, layout.degrees)

    batch_total = fields.shape[0] * lax.axis_size("dp")
    real, imag = (rows[:, part, :, :MODES].reshape(chunks * width, MODES) for part in range(2))
    return (real.T / batch_total, imag.T / batch_total)


def solution(mesh):
    in_specs = (P("dp", "space", None, None), P("dp", "space", None, None), P(), P())
    out_specs = (P(), P())
    return jax.shard_map(
        on_device, mesh=mesh, in_specs=in_specs, out_specs=out_specs, check_vma=False
    )
```

```python
import functools
import math

import jax
import jax.numpy as jnp
import ml_dtypes
import numpy as np
from jax import lax
from jax.experimental import pallas as pl
from jax.experimental.pallas import tpu as pltpu
from jax.sharding import PartitionSpec as P

NLAT = 126
NLON = 252
MODES = 126
LANES = 128
GROUP = 16
PAIRS = 8
VMEM = 30 * 1024 * 1024
FORWARD_VMEM = 56 * 1024 * 1024


def round_up(value, step):
    return -(-value // step) * step


def legendre_table():
    colatitude = math.pi * (np.arange(NLAT) + 0.5) / NLAT
    cos_theta, sin_theta = np.cos(colatitude), np.sin(colatitude)
    counters = np.arange(1, MODES)
    log_steps = 0.5 * np.log((2.0 * counters + 1.0) / (2.0 * counters))
    log_table = np.concatenate([[0.0], np.cumsum(log_steps)])
    table = np.zeros((MODES, MODES, NLAT))
    for order in range(MODES):
        table[order, order] = np.exp(
            0.5 * math.log(1.0 / (4.0 * math.pi)) + log_table[order] + order * np.log(sin_theta)
        )
        for degree in range(order + 1, MODES):
            growth = math.sqrt((4.0 * degree**2 - 1.0) / (degree**2 - order**2))
            below = degree - 1
            current = cos_theta * table[order, below]
            if below > order:
                damping = math.sqrt((below**2 - order**2) / (4.0 * below**2 - 1.0))
                current = current - damping * table[order, degree - 2]
            table[order, degree] = growth * current
    weight = math.pi / NLAT * (2.0 * math.pi / NLON) * sin_theta
    return table, table * weight


def to_bf16(array):
    return np.where(np.abs(array) < 2.0**-126, 0.0, array).astype(ml_dtypes.bfloat16)


class Layout:
    def __init__(self, parts, local):
        self.parts, self.local = parts, local
        self.rows = round_up(local + 1, 16)
        self.half = self.rows // 2
        self.pitch = self.rows + 8
        self.low = max(MODES - local, 0)
        high = MODES - self.low
        self.pairs = (high + 1) // 2
        self.blocks = self.low + self.pairs
        self.slots = round_up(self.low + 2 * self.pairs, 8)
        self.degrees = round_up(MODES, 16)
        self.first_natural = self.rows - MODES + self.low
        self.partner = MODES - 1 + self.low
        orders = list(range(self.low))
        for pair in range(self.pairs):
            order = self.low + pair
            orders += [order, self.partner - order if self.partner - order != order else -1]
        self.orders = np.array(orders + [-1] * (self.slots - len(orders)))


def fourier_constants(layout):
    orders = np.maximum(layout.orders, 0)
    angles = 2.0 * math.pi / NLON * (orders[:, None] * np.arange(NLON)[None] % NLON)
    live = (layout.orders >= 0)[:, None]
    basis = np.concatenate([np.cos(angles) * live, -np.sin(angles) * live])
    factor = np.where(layout.orders == 0, 1.0, 2.0)[:, None]
    inverse = basis * np.concatenate([factor, factor])
    return to_bf16(basis), to_bf16(inverse)


@functools.lru_cache(maxsize=None)
def legendre_constants(parts, local):
    layout = Layout(parts, local)
    plain, weighted = legendre_table()
    rows, degrees, low, pairs = layout.rows, layout.degrees, layout.low, layout.pairs
    analysis = np.zeros((low, 2 * parts * rows, degrees))
    synth_low = np.zeros((low, parts * rows, degrees))
    pair_fwd = np.zeros((parts, pairs, rows, 2 * rows))
    pair_back = np.zeros((parts, pairs, rows, 2 * rows))
    for part in range(parts):
        own = slice(part * local, (part + 1) * local)
        start = part * rows
        synth_low[:, start : start + local, :MODES] = np.swapaxes(plain[:low, :, own], 1, 2)
        for turn in (1, 2):
            start = (turn * parts - 1 - part) * rows
            analysis[:, start : start + local, :MODES] = np.swapaxes(weighted[:low, :, own], 1, 2)
        for pair in range(pairs):
            order = low + pair
            mate = layout.partner - order
            for target, table in ((pair_fwd, weighted), (pair_back, plain)):
                count = MODES - order
                target[part, pair, rows - count :, :local] = table[order, order:, own]
                if mate != order:
                    count = MODES - mate
                    target[part, pair, :count, rows : rows + local] = table[mate, mate:, own][::-1]
    place = np.zeros((degrees, 2 * rows))
    for row in range(rows):
        if row >= rows - MODES + low:
            place[MODES - rows + row, row] = 1.0
        if MODES - 1 - row >= 0:
            place[MODES - 1 - row, rows + row] = 1.0
    return {
        "analysis": to_bf16(analysis),
        "synth_low": to_bf16(synth_low),
        "pair_fwd": to_bf16(pair_fwd),
        "pair_back": to_bf16(pair_back),
        "pair_synth": to_bf16(np.swapaxes(pair_back, -1, -2)),
        "place": place.astype(np.float32),
    }


def dot(left, right, sides=(1, 0)):
    contract = (((sides[0],), (sides[1],)), ((), ()))
    return lax.dot_general(left, right, contract, preferred_element_type=jnp.float32)


def swap_halves(values):
    return pltpu.roll(values, LANES // 2, 1)


def interleave(first, second):
    lane = lax.broadcasted_iota(jnp.int32, first.shape, 1)
    below = lane < LANES // 2
    return (
        jnp.where(below, first, swap_halves(second)),
        jnp.where(below, swap_halves(first), second),
    )


def gelu_slope(values):
    cumulative = 0.5 * (1.0 + lax.erf(values / math.sqrt(2.0)))
    density = jnp.exp(-0.5 * values * values) / math.sqrt(2.0 * math.pi)
    return cumulative + values * density


def grid_rows(layout, north, south, quad, group):
    rows = []
    for pair in (2 * quad, 2 * quad + 1):
        rows.append(north[0, pair])
        values = south[0, pair]
        if layout.rows > layout.local:
            latitude = layout.half + group * PAIRS + pair
            values = jnp.where(latitude < layout.local, values, jnp.zeros_like(values))
        rows.append(values)
    return jnp.concatenate(rows, axis=0)


def scatter_rows(layout, values, scratch, quad, group):
    slots = values.shape[0] // 2
    for which in range(2):
        columns = slice(which * LANES, (which + 1) * LANES)
        upper, lower = interleave(values[:slots, columns], values[slots:, columns])
        latitude = group * PAIRS + 2 * quad + which
        scratch[pl.ds(latitude, slots, stride=layout.pitch), :] = upper
        scratch[pl.ds(latitude + layout.half, slots, stride=layout.pitch), :] = lower


def gather_rows(layout, scratch, quad, group):
    slots = layout.slots
    cosine, sine = [], []
    for which in range(2):
        latitude = group * PAIRS + 2 * quad + which
        upper = scratch[pl.ds(latitude, slots, stride=layout.pitch), :]
        lower = scratch[pl.ds(latitude + layout.half, slots, stride=layout.pitch), :]
        first, second = interleave(upper, lower)
        cosine.append(first.astype(jnp.bfloat16))
        sine.append(second.astype(jnp.bfloat16))
    return jnp.concatenate(
        [jnp.concatenate(cosine, axis=1), jnp.concatenate(sine, axis=1)], axis=0
    )


def order_rows(layout, scratch, first, count):
    parts = []
    for order in range(count):
        start = pl.multiple_of((first + order) * layout.pitch, 8)
        parts.append(scratch[pl.ds(start, layout.rows), :])
    return jnp.concatenate(parts, axis=0).astype(jnp.bfloat16)


def band_copies(layout, chunk, fields, buffer, sems):
    width = LANES // 2
    copies = []
    for group in range(layout.half // PAIRS):
        started = []
        for side in range(2):
            first = side * layout.half + group * PAIRS
            count = min(PAIRS, layout.local - first)
            if count > 0:
                started.append(
                    pltpu.make_async_copy(
                        fields.at[0, pl.ds(first, count), pl.ds(chunk * width, width), :],
                        buffer.at[pl.ds(first, count)],
                        sems.at[2 * group + side],
                    )
                )
        copies.append(started)
    return copies


def forward_kernel(layout, chunk, bounds, index, fields, basis_all, pair_all, *refs):
    outs, refs = refs[: len(bounds) - 1], refs[len(bounds) - 1 :]
    scratch, buffer, basis, stage, pair_fwd, sems, basis_sem, pair_sem, out_sems = refs
    basis_copy = pltpu.make_async_copy(basis_all, basis, basis_sem)
    basis_copy.start()
    copies = band_copies(layout, chunk, fields, buffer, sems)
    for started in copies:
        for copy in started:
            copy.start()
    tables = pltpu.make_async_copy(pair_all.at[index[0]], pair_fwd, pair_sem)
    tables.start()
    if layout.rows > layout.local:
        shape = (layout.rows - layout.local,) + buffer.shape[1:]
        buffer[layout.local :] = jnp.zeros(shape, buffer.dtype)
    basis_copy.wait()
    for group, started in enumerate(copies):
        for copy in started:
            copy.wait()
        for quad in range(PAIRS // 2):
            rows = []
            for which in range(2):
                latitude = group * PAIRS + 2 * quad + which
                rows += [buffer[latitude], buffer[latitude + layout.half]]
            grid = jnp.concatenate(rows, axis=0)
            scatter_rows(layout, dot(basis[...], grid, (1, 1)), scratch, quad, group)

    def low_block(order, carry):
        stage[order] = order_rows(layout, scratch, order, 1)
        return carry

    def pair_block(pair, carry):
        values = order_rows(layout, scratch, layout.low + 2 * pair, 2)
        stage[layout.low + pair] = dot(pair_fwd[pair], values).astype(jnp.bfloat16)
        return carry

    flushes = []

    def flush(first, last):
        at = max(at for at in range(len(outs)) if bounds[at] <= first)
        flushes.append(
            pltpu.make_async_copy(
                stage.at[pl.ds(first, last - first)],
                outs[at].at[pl.ds(first - bounds[at], last - first)],
                out_sems.at[len(flushes)],
            )
        )
        flushes[-1].start()

    middle = layout.low // 2
    for first, last in ((0, middle), (middle, layout.low)):
        lax.fori_loop(first, last, low_block, 0, unroll=8)
        flush(first, last)
    tables.wait()
    lax.fori_loop(0, layout.pairs, pair_block, 0, unroll=8)
    flush(layout.low, layout.blocks)
    for copy in flushes:
        copy.wait()


def mix(spectral, swapped, real_rows, imag_rows):
    return (spectral * real_rows + swapped * imag_rows).astype(jnp.bfloat16)


def order_groups(layout):
    for start in range(0, layout.low, GROUP):
        yield start, min(start + GROUP, layout.low), start // 16 * 16


def low_kernel(layout, *refs):
    low_orders(layout, refs[: layout.parts], *refs[layout.parts :])


def low_orders(layout, held, analysis, synth_low, real_ref, imag_ref, grid_low, spec_low, swap_low):
    degrees = layout.degrees
    for start, stop, top in order_groups(layout):
        real_rows = real_ref[top:degrees, :]
        imag_rows = imag_ref[top:degrees, :]

        def low_block(order, carry):
            values = jnp.concatenate([ref[order] for ref in held], axis=0)
            spectral = dot(analysis[order, top:degrees, :], values).astype(jnp.bfloat16)
            spec_low[order, top:degrees, :] = spectral
            return carry

        def mix_block(order, carry):
            spectral = spec_low[order, top:degrees, :].astype(jnp.float32)
            swapped = swap_halves(spectral)
            swap_low[order, top:degrees, :] = swapped.astype(jnp.bfloat16)
            mixed = mix(spectral, swapped, real_rows, imag_rows)
            begin = pl.multiple_of(order * layout.pitch, 8)
            grid_low[pl.ds(begin, layout.rows), :] = dot(synth_low[order, :, top:degrees], mixed)
            return carry

        lax.fori_loop(start, stop, low_block, 0, unroll=8)
        lax.fori_loop(start, stop, mix_block, 0, unroll=8)


def spectral_kernel(layout, apart, *refs):
    held, lows, refs = refs[: layout.parts], refs[layout.parts : layout.parts + 2 + apart], refs[layout.parts + 2 + apart :]
    north, south, basis, back_low, pair_synth, pair_back, place, real_ref, imag_ref = refs[:9]
    out, scratch, returned, spec_low, swap_low, spec_pair, swap_pair, sems = refs[9:]
    offset = 0 if apart else layout.low
    group = pl.program_id(0)
    rows, degrees, low = layout.rows, layout.degrees, layout.low
    if apart:
        targets = (scratch.at[pl.ds(0, low * layout.pitch)], spec_low, swap_low)
        copies = [pltpu.make_async_copy(lows[at], targets[at], sems.at[at]) for at in range(3)]

    @pl.when(group == 0)
    def _():
        if apart:
            for copy in copies:
                copy.start()
        else:
            low_orders(layout, held, *lows, real_ref, imag_ref, scratch, spec_low, swap_low)
        line = lax.broadcasted_iota(jnp.int32, (rows, LANES), 0)

        def pair_block(pair, carry):
            total = sum(ref[offset + pair].astype(jnp.float32) for ref in held)
            spectral = total.astype(jnp.bfloat16)
            spec_pair[pair] = spectral
            natural = line >= layout.first_natural + pair
            real_rows = jnp.where(natural, real_ref[degrees : degrees + rows, :], real_ref[degrees + rows :, :])
            imag_rows = jnp.where(natural, imag_ref[degrees : degrees + rows, :], imag_ref[degrees + rows :, :])
            spectral = spectral.astype(jnp.float32)
            swapped = swap_halves(spectral)
            swap_pair[pair] = swapped.astype(jnp.bfloat16)
            mixed = mix(spectral, swapped, real_rows, imag_rows)
            values = dot(pair_synth[pair], mixed)
            for which in range(2):
                begin = pl.multiple_of((low + 2 * pair + which) * layout.pitch, 8)
                scratch[pl.ds(begin, rows), :] = values[which * rows : (which + 1) * rows]
            return carry

        lax.fori_loop(0, layout.pairs, pair_block, 0, unroll=8)
        used = (low + 2 * layout.pairs) * layout.pitch
        if used < layout.slots * layout.pitch:
            scratch[used : layout.slots * layout.pitch, :] = jnp.zeros(
                (layout.slots * layout.pitch - used, LANES), jnp.float32
            )
        if apart:
            copies[0].wait()

    for quad in range(PAIRS // 2):
        modes = gather_rows(layout, scratch, quad, group)
        signal = dot(modes, basis[...], (0, 0))
        incoming = grid_rows(layout, north, south, quad, group).astype(jnp.float32)
        upstream = (incoming * gelu_slope(signal)).astype(jnp.bfloat16)
        scatter_rows(layout, dot(basis[...], upstream, (1, 1)), returned, quad, group)

    @pl.when(group == pl.num_programs(0) - 1)
    def _():
        if apart:
            copies[1].wait()
            copies[2].wait()

        def products(spectral, swapped, back):
            return spectral.astype(jnp.float32) * back, swapped.astype(jnp.float32) * back

        zeros = jnp.zeros((degrees, LANES), jnp.float32)
        same, cross = zeros, zeros
        for start, stop, top in order_groups(layout):

            def low_block(order, carry):
                back = dot(back_low[order, top:degrees, :], order_rows(layout, returned, order, 1))
                first, second = products(
                    spec_low[order, top:degrees, :], swap_low[order, top:degrees, :], back
                )
                return carry[0] + first, carry[1] + second

            part = jnp.zeros((degrees - top, LANES), jnp.float32)
            first, second = lax.fori_loop(start, stop, low_block, (part, part), unroll=8)
            if top:
                empty = jnp.zeros((top, LANES), jnp.float32)
                first = jnp.concatenate([empty, first], axis=0)
                second = jnp.concatenate([empty, second], axis=0)
            same, cross = same + first, cross + second

        line = lax.broadcasted_iota(jnp.int32, (rows, LANES), 0)

        def pair_block(pair, carry):
            back = dot(pair_back[pair], order_rows(layout, returned, low + 2 * pair, 2))
            first, second = products(spec_pair[pair], swap_pair[pair], back)
            natural = line >= layout.first_natural + pair
            return (
                carry[0] + jnp.where(natural, first, 0.0),
                carry[1] + jnp.where(natural, second, 0.0),
                carry[2] + jnp.where(natural, 0.0, first),
                carry[3] + jnp.where(natural, 0.0, second),
            )

        part = jnp.zeros((rows, LANES), jnp.float32)
        sums = lax.fori_loop(0, layout.pairs, pair_block, (part,) * 4, unroll=8)
        placed = jnp.dot(
            place[...],
            jnp.concatenate(
                [jnp.concatenate(sums[:2], axis=1), jnp.concatenate(sums[2:], axis=1)], axis=0
            ),
            preferred_element_type=jnp.float32,
            precision=lax.Precision.HIGHEST,
        )
        same = same + placed[:, :LANES]
        cross = cross + placed[:, LANES:]
        real = same + swap_halves(same)
        imag = cross - swap_halves(cross)
        lane = lax.broadcasted_iota(jnp.int32, real.shape, 1)
        out[...] = jnp.where(lane < LANES // 2, real, imag).T


def grid_specs(layout, chunk):
    last = -(-layout.local // PAIRS) - 1
    shift = layout.half // PAIRS
    block = (1, PAIRS, LANES // 2, NLON)
    return [
        pl.BlockSpec(block, lambda g: (0, jnp.minimum(g, last), chunk, 0)),
        pl.BlockSpec(block, lambda g: (0, jnp.minimum(shift + g, last), chunk, 0)),
    ]


def whole():
    return pl.BlockSpec(memory_space=pltpu.VMEM)


def forward_call(layout, chunk, bounds, index, fields, pair_fwd):
    basis = jnp.asarray(fourier_constants(layout)[0])
    slots = basis.shape[0] // 2
    groups = layout.half // PAIRS
    anywhere = pl.BlockSpec(memory_space=pl.ANY)
    counts = [last - first for first, last in zip(bounds, bounds[1:])]
    return pl.pallas_call(
        functools.partial(forward_kernel, layout, chunk, bounds),
        in_specs=[pl.BlockSpec(memory_space=pltpu.SMEM)] + [anywhere] * 3,
        out_specs=[anywhere] * len(counts),
        out_shape=[jax.ShapeDtypeStruct((count, layout.rows, LANES), jnp.bfloat16) for count in counts],
        scratch_shapes=[
            pltpu.VMEM((slots * layout.pitch, LANES), jnp.float32),
            pltpu.VMEM((layout.rows, LANES // 2, NLON), jnp.bfloat16),
            pltpu.VMEM(basis.shape, jnp.bfloat16),
            pltpu.VMEM((layout.blocks, layout.rows, LANES), jnp.bfloat16),
            pltpu.VMEM(pair_fwd.shape[1:], jnp.bfloat16),
            pltpu.SemaphoreType.DMA((2 * groups,)),
            pltpu.SemaphoreType.DMA,
            pltpu.SemaphoreType.DMA,
            pltpu.SemaphoreType.DMA((3,)),
        ],
        compiler_params=pltpu.CompilerParams(vmem_limit_bytes=FORWARD_VMEM),
        cost_estimate=pl.CostEstimate(flops=1_000_000, bytes_accessed=100_000, transcendentals=0),
        name=f"forward_{chunk}",
    )(index, fields, basis, pair_fwd)


def low_call(layout, chunk, coeffs, tables, real_rows, imag_rows):
    operands = list(coeffs) + list(tables) + [real_rows, imag_rows]
    spectra = jax.ShapeDtypeStruct((layout.low, layout.degrees, LANES), jnp.bfloat16)
    return pl.pallas_call(
        functools.partial(low_kernel, layout),
        in_specs=[whole()] * len(operands),
        out_specs=[whole()] * 3,
        out_shape=[jax.ShapeDtypeStruct((layout.low * layout.pitch, LANES), jnp.float32), spectra, spectra],
        compiler_params=pltpu.CompilerParams(vmem_limit_bytes=VMEM),
        cost_estimate=pl.CostEstimate(flops=8_000_000_000, bytes_accessed=30_000_000, transcendentals=0),
        name=f"low_{chunk}",
    )(*operands)


def spectral_call(layout, chunk, apart, blocks, lows, cotangent, tables, real_rows, imag_rows):
    operands = list(blocks) + list(lows) + [cotangent, cotangent] + list(tables) + [real_rows, imag_rows]
    low_spec = pl.BlockSpec(memory_space=pl.ANY) if apart else whole()
    specs = [whole()] * len(blocks) + [low_spec] * len(lows)
    specs += grid_specs(layout, chunk) + [whole()] * (len(tables) + 2)
    return pl.pallas_call(
        functools.partial(spectral_kernel, layout, apart),
        grid=(layout.half // PAIRS,),
        in_specs=specs,
        out_specs=whole(),
        out_shape=jax.ShapeDtypeStruct((LANES, layout.degrees), jnp.float32),
        scratch_shapes=[
            pltpu.VMEM((layout.slots * layout.pitch, LANES), jnp.float32),
            pltpu.VMEM((layout.slots * layout.pitch, LANES), jnp.float32),
            pltpu.VMEM((layout.low, layout.degrees, LANES), jnp.bfloat16),
            pltpu.VMEM((layout.low, layout.degrees, LANES), jnp.bfloat16),
            pltpu.VMEM((layout.pairs, layout.rows, LANES), jnp.bfloat16),
            pltpu.VMEM((layout.pairs, layout.rows, LANES), jnp.bfloat16),
            pltpu.SemaphoreType.DMA((3,)),
        ],
        compiler_params=pltpu.CompilerParams(vmem_limit_bytes=VMEM),
        cost_estimate=pl.CostEstimate(flops=8_000_000_000, bytes_accessed=30_000_000, transcendentals=0),
        name=f"spectral_{chunk}",
    )(*operands)


def radices(size):
    found, factor = [], 2
    while size > 1:
        while size % factor == 0:
            found.append(factor)
            size //= factor
        factor += 1
    return found


def sum_steps(axis):
    size = lax.axis_size(axis)
    steps, stride = [], 1
    for radix in radices(size):
        steps.append((axis, stride, radix))
        stride *= radix
    return steps


def hop_parcels(value, step):
    axis, stride, radix = step
    parcels = []
    for turn in range(1, radix):
        pairs = []
        for index in range(lax.axis_size(axis)):
            digit = index // stride % radix
            pairs.append((index, index + ((digit + turn) % radix - digit) * stride))
        parcels.append(lax.ppermute(value, axis, pairs))
    return parcels


def sum_over(value, steps):
    for step in steps:
        value = sum(hop_parcels(value, step), value)
    return value


def filter_rows(layout, spec):
    padded = jnp.pad(spec, ((0, layout.degrees - MODES), (0, 0)))
    front = jnp.pad(spec, ((layout.rows, layout.rows), (0, 0)))
    natural = front[MODES : MODES + layout.rows]
    backward = front[layout.rows + MODES - layout.rows : layout.rows + MODES][::-1]
    return jnp.concatenate([padded, natural, backward], axis=0).astype(jnp.float32)


def on_device(fields, cotangent, spec_real, spec_imag):
    parts = lax.axis_size("space")
    index = lax.axis_index("space")
    layout = Layout(parts, fields.shape[1])
    width = LANES // 2
    chunks = fields.shape[-1] // width
    inverse = jnp.asarray(fourier_constants(layout)[1])
    constants = legendre_constants(parts, layout.local)

    def local_table(name):
        return lax.dynamic_index_in_dim(jnp.asarray(constants[name]), index, keepdims=False)

    pair_fwd = jnp.asarray(constants["pair_fwd"])
    place = jnp.reshape(index, (1,)).astype(jnp.int32)
    def bands(name, first, count):
        table = jnp.asarray(constants[name])
        return lax.optimization_barrier(
            lax.dynamic_slice_in_dim(table, first * layout.rows, count * layout.rows, 1)
        )

    analysis = jnp.swapaxes(bands("analysis", parts - 1 - index, parts), 1, 2)
    synth_low = bands("synth_low", index, 1)
    back_low = jnp.swapaxes(synth_low, 1, 2)
    pair_tables = [local_table(name) for name in ("pair_synth", "pair_back")]
    low_tables = [analysis, synth_low]
    tables = [inverse, back_low] + pair_tables + [jnp.asarray(constants["place"])]
    fields, cotangent = jnp.swapaxes(fields, 2, 3), jnp.swapaxes(cotangent, 2, 3)
    real_all = filter_rows(layout, spec_real)
    imag_all = filter_rows(layout, spec_imag)

    def others(sent):
        routes = [[(source, (source + shift) % parts) for source in range(parts)] for shift in range(1, parts)]
        return [lax.ppermute(sent, "space", route) for route in routes]

    held = []
    for chunk in range(chunks):
        if chunk == chunks - 1:
            place, low_tables, tables = lax.optimization_barrier((place, low_tables, tables))
        bounds = (0, layout.blocks) if chunk < chunks - 1 else (0, layout.low, layout.blocks)
        made = forward_call(layout, chunk, bounds, place, fields, pair_fwd)
        place, made = lax.optimization_barrier((place, list(made)))
        if len(made) > 1 and held:
            made[1], held[0][1] = lax.optimization_barrier((made[1], held[0][1]))
        held += [[own] + others(own) for own in made]

    hops, last_hops = sum_steps("dp"), sum_steps("space")
    waiting = []

    def hop_all(limit, tie):
        moved = []
        for value, done in waiting:
            if done < limit:
                parcels = hop_parcels(value, (hops + last_hops)[done])
                parcels, value, tie = lax.optimization_barrier((parcels, value, tie))
                value, done = sum(parcels, value), done + 1
            moved.append((value, done))
        waiting[:] = moved
        return tie

    def before(values):
        if not waiting:
            return values
        values, sums = lax.optimization_barrier((values, [value for value, _ in waiting]))
        waiting[:] = [(value, done) for value, (_, done) in zip(sums, waiting)]
        return values

    for chunk in range(chunks):
        columns = slice(chunk * width, (chunk + 1) * width)
        real, imag = real_all[:, columns], imag_all[:, columns]
        real_rows = jnp.concatenate([real, real], axis=1)
        imag_rows = jnp.concatenate([-imag, imag], axis=1)
        blocks, lows, apart = held[chunk], low_tables, chunk == chunks - 1
        if apart:
            lows = low_call(layout, chunk, blocks, low_tables, real_rows, imag_rows)
            lows = before(hop_all(len(hops), lows))
            blocks = held[-1]
        grads = spectral_call(layout, chunk, apart, blocks, lows, cotangent, tables, real_rows, imag_rows)
        if not apart:
            grads = hop_all(len(hops), grads)
            waiting.append((grads, 0))
            if chunk < chunks - 2:
                for _ in range(len(hops) // 2):
                    waiting[-1] = (sum_over(waiting[-1][0], hops[waiting[-1][1] :][:1]), waiting[-1][1] + 1)
                held[chunk + 1] = before(held[chunk + 1])
        else:
            grads = hop_all(len(hops) + len(last_hops), grads)
            waiting.append((grads, 0))

    total, done = waiting.pop()
    hops = hops + last_hops
    while done < len(hops):
        joined = [value for value, at in waiting if at == done]
        waiting = [(value, at) for value, at in waiting if at != done]
        if joined:
            total = jnp.concatenate(joined + [total], axis=0)
        total, done = sum_over(total, hops[done : done + 1]), done + 1
    rows = jnp.concatenate([value for value, _ in waiting] + [total], axis=0)
    rows = rows.reshape(chunks, 2, width, layout.degrees)

    batch_total = fields.shape[0] * lax.axis_size("dp")
    real, imag = (rows[:, part, :, :MODES].reshape(chunks * width, MODES) for part in range(2))
    return (real.T / batch_total, imag.T / batch_total)


def solution(mesh):
    in_specs = (P("dp", "space", None, None), P("dp", "space", None, None), P(), P())
    out_specs = (P(), P())
    return jax.shard_map(
        on_device, mesh=mesh, in_specs=in_specs, out_specs=out_specs, check_vma=False
    )
```

```python
import functools
import math

import jax
import jax.numpy as jnp
import ml_dtypes
import numpy as np
from jax import lax
from jax.experimental import pallas as pl
from jax.experimental.pallas import tpu as pltpu
from jax.sharding import PartitionSpec as P

NLAT = 126
NLON = 252
MODES = 126
LANES = 128
GROUP = 16
PAIRS = 8
VMEM = 30 * 1024 * 1024
FORWARD_VMEM = 56 * 1024 * 1024


def round_up(value, step):
    return -(-value // step) * step


def legendre_table():
    colatitude = math.pi * (np.arange(NLAT) + 0.5) / NLAT
    cos_theta, sin_theta = np.cos(colatitude), np.sin(colatitude)
    counters = np.arange(1, MODES)
    log_steps = 0.5 * np.log((2.0 * counters + 1.0) / (2.0 * counters))
    log_table = np.concatenate([[0.0], np.cumsum(log_steps)])
    table = np.zeros((MODES, MODES, NLAT))
    for order in range(MODES):
        table[order, order] = np.exp(
            0.5 * math.log(1.0 / (4.0 * math.pi)) + log_table[order] + order * np.log(sin_theta)
        )
        for degree in range(order + 1, MODES):
            growth = math.sqrt((4.0 * degree**2 - 1.0) / (degree**2 - order**2))
            below = degree - 1
            current = cos_theta * table[order, below]
            if below > order:
                damping = math.sqrt((below**2 - order**2) / (4.0 * below**2 - 1.0))
                current = current - damping * table[order, degree - 2]
            table[order, degree] = growth * current
    weight = math.pi / NLAT * (2.0 * math.pi / NLON) * sin_theta
    return table, table * weight


def to_bf16(array):
    return np.where(np.abs(array) < 2.0**-126, 0.0, array).astype(ml_dtypes.bfloat16)


class Layout:
    def __init__(self, parts, local):
        self.parts, self.local = parts, local
        self.rows = round_up(local + 1, 16)
        self.half = self.rows // 2
        self.pitch = self.rows + 8
        self.low = max(MODES - local, 0)
        high = MODES - self.low
        self.pairs = round_up((high + 1) // 2, 2)
        self.twos = round_up(self.low, 2) // 2
        self.blocks = self.low + self.pairs
        self.slots = round_up(self.low + 2 * self.pairs, 8)
        self.degrees = round_up(MODES, 16)
        self.first_natural = self.rows - MODES + self.low
        self.partner = MODES - 1 + self.low
        orders = list(range(self.low))
        for pair in range(self.pairs):
            order, mate = self.low + pair, self.partner - self.low - pair
            orders += [order if order <= mate else -1, mate if order < mate else -1]
        self.orders = np.array(orders + [-1] * (self.slots - len(orders)))


def fourier_constants(layout):
    orders = np.maximum(layout.orders, 0)
    angles = 2.0 * math.pi / NLON * (orders[:, None] * np.arange(NLON)[None] % NLON)
    live = (layout.orders >= 0)[:, None]
    basis = np.concatenate([np.cos(angles) * live, -np.sin(angles) * live])
    factor = np.where(layout.orders == 0, 1.0, 2.0)[:, None]
    inverse = basis * np.concatenate([factor, factor])
    return to_bf16(basis), to_bf16(inverse)


@functools.lru_cache(maxsize=None)
def legendre_constants(parts, local):
    layout = Layout(parts, local)
    plain, weighted = legendre_table()
    rows, degrees, low, pairs = layout.rows, layout.degrees, layout.low, layout.pairs
    analysis = np.zeros((2 * layout.twos, 2 * parts * rows, degrees))
    synth_low = np.zeros((2 * layout.twos, parts * rows, degrees))
    pair_fwd = np.zeros((parts, pairs, rows, 2 * rows))
    pair_back = np.zeros((parts, pairs, rows, 2 * rows))
    for part in range(parts):
        own = slice(part * local, (part + 1) * local)
        start = part * rows
        synth_low[:low, start : start + local, :MODES] = np.swapaxes(plain[:low, :, own], 1, 2)
        for turn in (1, 2):
            start = (turn * parts - 1 - part) * rows
            analysis[:low, start : start + local, :MODES] = np.swapaxes(weighted[:low, :, own], 1, 2)
        for pair in range(pairs):
            order = low + pair
            mate = layout.partner - order
            for target, table in ((pair_fwd, weighted), (pair_back, plain)):
                if order <= mate:
                    count = MODES - order
                    target[part, pair, rows - count :, :local] = table[order, order:, own]
                if order < mate:
                    count = MODES - mate
                    target[part, pair, :count, rows : rows + local] = table[mate, mate:, own][::-1]
    pair_synth = np.swapaxes(pair_back, -1, -2)
    place = np.zeros((degrees, 2 * rows))
    for row in range(rows):
        if row >= rows - MODES + low:
            place[MODES - rows + row, row] = 1.0
        if MODES - 1 - row >= 0:
            place[MODES - 1 - row, rows + row] = 1.0
    return {
        "analysis": to_bf16(analysis),
        "synth_low": to_bf16(synth_low),
        "pair_fwd": to_bf16(pair_fwd),
        "pair_back": to_bf16(np.concatenate([pair_back[:, ::2], pair_back[:, 1::2]], axis=3)),
        "pair_synth": to_bf16(np.concatenate([pair_synth[:, ::2], pair_synth[:, 1::2]], axis=3)),
        "place": place.astype(np.float32),
    }


def dot(left, right, sides=(1, 0)):
    contract = (((sides[0],), (sides[1],)), ((), ()))
    return lax.dot_general(left, right, contract, preferred_element_type=jnp.float32)


def dot_two(left, first, second):
    upper = jnp.concatenate([first, jnp.zeros_like(first)], axis=1)
    lower = jnp.concatenate([jnp.zeros_like(second), second], axis=1)
    return dot(left, jnp.concatenate([upper, lower], axis=0))


def swap_halves(values):
    return pltpu.roll(values, LANES // 2, 1)


def interleave(first, second):
    lane = lax.broadcasted_iota(jnp.int32, first.shape, 1)
    below = lane < LANES // 2
    return (
        jnp.where(below, first, swap_halves(second)),
        jnp.where(below, swap_halves(first), second),
    )


def gelu_slope(values):
    cumulative = 0.5 * (1.0 + lax.erf(values / math.sqrt(2.0)))
    density = jnp.exp(-0.5 * values * values) / math.sqrt(2.0 * math.pi)
    return cumulative + values * density


def grid_rows(layout, north, south, quad, group):
    rows = []
    for pair in (2 * quad, 2 * quad + 1):
        rows.append(north[0, pair])
        values = south[0, pair]
        if layout.rows > layout.local:
            latitude = layout.half + group * PAIRS + pair
            values = jnp.where(latitude < layout.local, values, jnp.zeros_like(values))
        rows.append(values)
    return jnp.concatenate(rows, axis=0)


def scatter_rows(layout, values, scratch, quad, group):
    slots = values.shape[0] // 2
    for which in range(2):
        columns = slice(which * LANES, (which + 1) * LANES)
        upper, lower = interleave(values[:slots, columns], values[slots:, columns])
        latitude = group * PAIRS + 2 * quad + which
        scratch[pl.ds(latitude, slots, stride=layout.pitch), :] = upper
        scratch[pl.ds(latitude + layout.half, slots, stride=layout.pitch), :] = lower


def gather_rows(layout, scratch, quad, group):
    slots = layout.slots
    cosine, sine = [], []
    for which in range(2):
        latitude = group * PAIRS + 2 * quad + which
        upper = scratch[pl.ds(latitude, slots, stride=layout.pitch), :]
        lower = scratch[pl.ds(latitude + layout.half, slots, stride=layout.pitch), :]
        first, second = interleave(upper, lower)
        cosine.append(first.astype(jnp.bfloat16))
        sine.append(second.astype(jnp.bfloat16))
    return jnp.concatenate(
        [jnp.concatenate(cosine, axis=1), jnp.concatenate(sine, axis=1)], axis=0
    )


def order_rows(layout, scratch, first, count):
    parts = []
    for order in range(count):
        start = pl.multiple_of((first + order) * layout.pitch, 8)
        parts.append(scratch[pl.ds(start, layout.rows), :])
    return jnp.concatenate(parts, axis=0).astype(jnp.bfloat16)


def band_copies(layout, chunk, fields, buffer, sems):
    width = LANES // 2
    copies = []
    for group in range(layout.half // PAIRS):
        started = []
        for side in range(2):
            first = side * layout.half + group * PAIRS
            count = min(PAIRS, layout.local - first)
            if count > 0:
                started.append(
                    pltpu.make_async_copy(
                        fields.at[0, pl.ds(first, count), pl.ds(chunk * width, width), :],
                        buffer.at[pl.ds(first, count)],
                        sems.at[2 * group + side],
                    )
                )
        copies.append(started)
    return copies


def forward_kernel(layout, chunk, bounds, index, fields, basis_all, pair_all, *refs):
    outs, refs = refs[: len(bounds) - 1], refs[len(bounds) - 1 :]
    scratch, buffer, basis, stage, pair_fwd, sems, basis_sem, pair_sem, out_sems = refs
    basis_copy = pltpu.make_async_copy(basis_all, basis, basis_sem)
    basis_copy.start()
    copies = band_copies(layout, chunk, fields, buffer, sems)
    for started in copies[:2]:
        for copy in started:
            copy.start()
    tables = pltpu.make_async_copy(pair_all.at[index[0]], pair_fwd, pair_sem)
    tables.start()
    if layout.rows > layout.local:
        shape = (layout.rows - layout.local,) + buffer.shape[1:]
        buffer[layout.local :] = jnp.zeros(shape, buffer.dtype)
    basis_copy.wait()
    for group, started in enumerate(copies):
        for copy in started:
            copy.wait()
        for copy in sum(copies[group + 2 : group + 3], []):
            copy.start()
        for quad in range(PAIRS // 2):
            rows = []
            for which in range(2):
                latitude = group * PAIRS + 2 * quad + which
                rows += [buffer[latitude], buffer[latitude + layout.half]]
            grid = jnp.concatenate(rows, axis=0)
            scatter_rows(layout, dot(basis[...], grid, (1, 1)), scratch, quad, group)

    def low_block(order, carry):
        stage[order] = order_rows(layout, scratch, order, 1)
        return carry

    def pair_block(pair, carry):
        values = order_rows(layout, scratch, layout.low + 2 * pair, 2)
        stage[layout.low + pair] = dot(pair_fwd[pair], values).astype(jnp.bfloat16)
        return carry

    flushes = []

    def flush(first, last):
        at = max(at for at in range(len(outs)) if bounds[at] <= first)
        flushes.append(
            pltpu.make_async_copy(
                stage.at[pl.ds(first, last - first)],
                outs[at].at[pl.ds(first - bounds[at], last - first)],
                out_sems.at[len(flushes)],
            )
        )
        flushes[-1].start()

    middle = layout.low // 2
    for first, last in ((0, middle), (middle, layout.low)):
        lax.fori_loop(first, last, low_block, 0, unroll=8)
        flush(first, last)
    tables.wait()
    lax.fori_loop(0, layout.pairs, pair_block, 0, unroll=8)
    flush(layout.low, layout.blocks)
    for copy in flushes:
        copy.wait()


def mix(spectral, swapped, real_rows, imag_rows):
    return (spectral * real_rows + swapped * imag_rows).astype(jnp.bfloat16)


def order_groups(layout):
    for start in range(0, layout.low, GROUP):
        stop = min(start + GROUP, layout.low)
        yield start // 2, (stop + 1) // 2, start // 16 * 16


def low_kernel(layout, *refs):
    low_orders(layout, refs[: layout.parts], *refs[layout.parts :])


def low_orders(layout, held, analysis, synth_low, real_ref, imag_ref, grid_low, spec_low, swap_low):
    degrees = layout.degrees
    for start, stop, top in order_groups(layout):
        real_rows = real_ref[top:degrees, :]
        imag_rows = imag_ref[top:degrees, :]

        def low_block(two, carry):
            values = []
            for order in (2 * two, jnp.minimum(2 * two + 1, layout.low - 1)):
                values.append(jnp.concatenate([ref[order] for ref in held], axis=0))
            spectral = dot_two(analysis[two, top:degrees, :], *values).astype(jnp.bfloat16)
            for which in range(2):
                spec_low[2 * two + which, top:degrees, :] = spectral[:, which * LANES : (which + 1) * LANES]
            return carry

        def mix_block(two, carry):
            mixed = []
            for order in (2 * two, 2 * two + 1):
                spectral = spec_low[order, top:degrees, :].astype(jnp.float32)
                swapped = swap_halves(spectral)
                swap_low[order, top:degrees, :] = swapped.astype(jnp.bfloat16)
                values = mix(spectral, swapped, real_rows, imag_rows)
                if top:
                    values = jnp.concatenate([jnp.zeros((top, LANES), values.dtype), values], axis=0)
                mixed.append(values)
            values = dot_two(synth_low[two], *mixed)
            for which in range(2):
                begin = pl.multiple_of((2 * two + which) * layout.pitch, 8)
                grid_low[pl.ds(begin, layout.rows), :] = values[:, which * LANES : (which + 1) * LANES]
            return carry

        lax.fori_loop(start, stop, low_block, 0, unroll=4)
        lax.fori_loop(start, stop, mix_block, 0, unroll=4)


def spectral_kernel(layout, apart, *refs):
    held, lows, refs = refs[: layout.parts], refs[layout.parts : layout.parts + 2 + apart], refs[layout.parts + 2 + apart :]
    north, south, basis, back_low, pair_synth, pair_back, place, real_ref, imag_ref = refs[:9]
    out, scratch, returned, spec_low, swap_low, spec_pair, swap_pair, sems = refs[9:]
    offset = 0 if apart else layout.low
    group = pl.program_id(0)
    rows, degrees, low = layout.rows, layout.degrees, layout.low
    if apart:
        sources = (lows[0].at[pl.ds(0, low * layout.pitch)], lows[1], lows[2])
        targets = (scratch.at[pl.ds(0, low * layout.pitch)], spec_low, swap_low)
        copies = [pltpu.make_async_copy(*ends, sems.at[at]) for at, ends in enumerate(zip(sources, targets))]

    @pl.when(group == 0)
    def _():
        if apart:
            for copy in copies:
                copy.start()
        else:
            low_orders(layout, held, *lows, real_ref, imag_ref, scratch, spec_low, swap_low)
        line = lax.broadcasted_iota(jnp.int32, (rows, LANES), 0)

        def pair_block(two, carry):
            mixed = []
            for pair in (2 * two, 2 * two + 1):
                total = sum(ref[offset + pair].astype(jnp.float32) for ref in held)
                spectral = total.astype(jnp.bfloat16)
                spec_pair[pair] = spectral
                natural = line >= layout.first_natural + pair
                real_rows = jnp.where(natural, real_ref[degrees : degrees + rows, :], real_ref[degrees + rows :, :])
                imag_rows = jnp.where(natural, imag_ref[degrees : degrees + rows, :], imag_ref[degrees + rows :, :])
                spectral = spectral.astype(jnp.float32)
                swapped = swap_halves(spectral)
                swap_pair[pair] = swapped.astype(jnp.bfloat16)
                mixed.append(mix(spectral, swapped, real_rows, imag_rows))
            values = dot_two(pair_synth[two], *mixed)
            for which in range(4):
                begin = pl.multiple_of((low + 4 * two + which) * layout.pitch, 8)
                columns = slice(which // 2 * LANES, (which // 2 + 1) * LANES)
                scratch[pl.ds(begin, rows), :] = values[which % 2 * rows : (which % 2 + 1) * rows, columns]
            return carry

        lax.fori_loop(0, layout.pairs // 2, pair_block, 0, unroll=4)
        used = (low + 2 * layout.pairs) * layout.pitch
        if used < layout.slots * layout.pitch:
            scratch[used : layout.slots * layout.pitch, :] = jnp.zeros(
                (layout.slots * layout.pitch - used, LANES), jnp.float32
            )
        if apart:
            copies[0].wait()

    for quad in range(PAIRS // 2):
        modes = gather_rows(layout, scratch, quad, group)
        signal = dot(modes, basis[...], (0, 0))
        incoming = grid_rows(layout, north, south, quad, group).astype(jnp.float32)
        upstream = (incoming * gelu_slope(signal)).astype(jnp.bfloat16)
        scatter_rows(layout, dot(basis[...], upstream, (1, 1)), returned, quad, group)

    @pl.when(group == pl.num_programs(0) - 1)
    def _():
        if apart:
            copies[1].wait()
            copies[2].wait()

        def products(spectral, swapped, back):
            return spectral.astype(jnp.float32) * back, swapped.astype(jnp.float32) * back

        zeros = jnp.zeros((degrees, LANES), jnp.float32)
        same, cross = zeros, zeros
        for start, stop, top in order_groups(layout):

            def low_block(two, carry):
                values = [order_rows(layout, returned, 2 * two + which, 1) for which in range(2)]
                back = dot_two(back_low[two, top:degrees, :], *values)
                for which in range(2):
                    order = 2 * two + which
                    first, second = products(
                        spec_low[order, top:degrees, :],
                        swap_low[order, top:degrees, :],
                        back[:, which * LANES : (which + 1) * LANES],
                    )
                    carry = carry[0] + first, carry[1] + second
                return carry

            part = jnp.zeros((degrees - top, LANES), jnp.float32)
            first, second = lax.fori_loop(start, stop, low_block, (part, part), unroll=4)
            if top:
                empty = jnp.zeros((top, LANES), jnp.float32)
                first = jnp.concatenate([empty, first], axis=0)
                second = jnp.concatenate([empty, second], axis=0)
            same, cross = same + first, cross + second

        line = lax.broadcasted_iota(jnp.int32, (rows, LANES), 0)

        def pair_block(two, carry):
            values = [order_rows(layout, returned, low + 4 * two + 2 * which, 2) for which in range(2)]
            back = dot_two(pair_back[two], *values)
            for which in range(2):
                pair = 2 * two + which
                first, second = products(
                    spec_pair[pair], swap_pair[pair], back[:, which * LANES : (which + 1) * LANES]
                )
                natural = line >= layout.first_natural + pair
                carry = (
                    carry[0] + jnp.where(natural, first, 0.0),
                    carry[1] + jnp.where(natural, second, 0.0),
                    carry[2] + jnp.where(natural, 0.0, first),
                    carry[3] + jnp.where(natural, 0.0, second),
                )
            return carry

        part = jnp.zeros((rows, LANES), jnp.float32)
        sums = lax.fori_loop(0, layout.pairs // 2, pair_block, (part,) * 4, unroll=4)
        placed = jnp.dot(
            place[...],
            jnp.concatenate(
                [jnp.concatenate(sums[:2], axis=1), jnp.concatenate(sums[2:], axis=1)], axis=0
            ),
            preferred_element_type=jnp.float32,
            precision=lax.Precision.HIGHEST,
        )
        same = same + placed[:, :LANES]
        cross = cross + placed[:, LANES:]
        real = same + swap_halves(same)
        imag = cross - swap_halves(cross)
        lane = lax.broadcasted_iota(jnp.int32, real.shape, 1)
        out[...] = jnp.where(lane < LANES // 2, real, imag).T


def grid_specs(layout, chunk):
    last = -(-layout.local // PAIRS) - 1
    shift = layout.half // PAIRS
    block = (1, PAIRS, LANES // 2, NLON)
    return [
        pl.BlockSpec(block, lambda g: (0, jnp.minimum(g, last), chunk, 0)),
        pl.BlockSpec(block, lambda g: (0, jnp.minimum(shift + g, last), chunk, 0)),
    ]


def whole():
    return pl.BlockSpec(memory_space=pltpu.VMEM)


def forward_call(layout, chunk, bounds, index, fields, pair_fwd):
    basis = jnp.asarray(fourier_constants(layout)[0])
    slots = basis.shape[0] // 2
    groups = layout.half // PAIRS
    anywhere = pl.BlockSpec(memory_space=pl.ANY)
    counts = [last - first for first, last in zip(bounds, bounds[1:])]
    return pl.pallas_call(
        functools.partial(forward_kernel, layout, chunk, bounds),
        in_specs=[pl.BlockSpec(memory_space=pltpu.SMEM)] + [anywhere] * 3,
        out_specs=[anywhere] * len(counts),
        out_shape=[jax.ShapeDtypeStruct((count, layout.rows, LANES), jnp.bfloat16) for count in counts],
        scratch_shapes=[
            pltpu.VMEM((slots * layout.pitch, LANES), jnp.float32),
            pltpu.VMEM((layout.rows, LANES // 2, NLON), jnp.bfloat16),
            pltpu.VMEM(basis.shape, jnp.bfloat16),
            pltpu.VMEM((layout.blocks, layout.rows, LANES), jnp.bfloat16),
            pltpu.VMEM(pair_fwd.shape[1:], jnp.bfloat16),
            pltpu.SemaphoreType.DMA((2 * groups,)),
            pltpu.SemaphoreType.DMA,
            pltpu.SemaphoreType.DMA,
            pltpu.SemaphoreType.DMA((3,)),
        ],
        compiler_params=pltpu.CompilerParams(vmem_limit_bytes=FORWARD_VMEM),
        cost_estimate=pl.CostEstimate(flops=1_000_000, bytes_accessed=100_000, transcendentals=0),
        name=f"forward_{chunk}",
    )(index, fields, basis, pair_fwd)


def low_call(layout, chunk, coeffs, tables, real_rows, imag_rows):
    operands = list(coeffs) + list(tables) + [real_rows, imag_rows]
    spectra = jax.ShapeDtypeStruct((2 * layout.twos, layout.degrees, LANES), jnp.bfloat16)
    return pl.pallas_call(
        functools.partial(low_kernel, layout),
        in_specs=[whole()] * len(operands),
        out_specs=[whole()] * 3,
        out_shape=[jax.ShapeDtypeStruct((2 * layout.twos * layout.pitch, LANES), jnp.float32), spectra, spectra],
        compiler_params=pltpu.CompilerParams(vmem_limit_bytes=VMEM),
        cost_estimate=pl.CostEstimate(flops=8_000_000_000, bytes_accessed=30_000_000, transcendentals=0),
        name=f"low_{chunk}",
    )(*operands)


def spectral_call(layout, chunk, apart, blocks, lows, cotangent, tables, real_rows, imag_rows):
    operands = list(blocks) + list(lows) + [cotangent, cotangent] + list(tables) + [real_rows, imag_rows]
    low_spec = pl.BlockSpec(memory_space=pl.ANY) if apart else whole()
    specs = [whole()] * len(blocks) + [low_spec] * len(lows)
    specs += grid_specs(layout, chunk) + [whole()] * (len(tables) + 2)
    return pl.pallas_call(
        functools.partial(spectral_kernel, layout, apart),
        grid=(layout.half // PAIRS,),
        in_specs=specs,
        out_specs=whole(),
        out_shape=jax.ShapeDtypeStruct((LANES, layout.degrees), jnp.float32),
        scratch_shapes=[
            pltpu.VMEM((layout.slots * layout.pitch, LANES), jnp.float32),
            pltpu.VMEM((layout.slots * layout.pitch, LANES), jnp.float32),
            pltpu.VMEM((2 * layout.twos, layout.degrees, LANES), jnp.bfloat16),
            pltpu.VMEM((2 * layout.twos, layout.degrees, LANES), jnp.bfloat16),
            pltpu.VMEM((layout.pairs, layout.rows, LANES), jnp.bfloat16),
            pltpu.VMEM((layout.pairs, layout.rows, LANES), jnp.bfloat16),
            pltpu.SemaphoreType.DMA((3,)),
        ],
        compiler_params=pltpu.CompilerParams(vmem_limit_bytes=VMEM),
        cost_estimate=pl.CostEstimate(flops=8_000_000_000, bytes_accessed=30_000_000, transcendentals=0),
        name=f"spectral_{chunk}",
    )(*operands)


def radices(size):
    found, factor = [], 2
    while size > 1:
        while size % factor == 0:
            found.append(factor)
            size //= factor
        factor += 1
    return found


def sum_steps(axis):
    size = lax.axis_size(axis)
    steps, stride = [], 1
    for radix in radices(size):
        steps.append((axis, stride, radix))
        stride *= radix
    return steps


def hop_parcels(value, step):
    axis, stride, radix = step
    parcels = []
    for turn in range(1, radix):
        pairs = []
        for index in range(lax.axis_size(axis)):
            digit = index // stride % radix
            pairs.append((index, index + ((digit + turn) % radix - digit) * stride))
        parcels.append(lax.ppermute(value, axis, pairs))
    return parcels


def sum_over(value, steps):
    for step in steps:
        value = sum(hop_parcels(value, step), value)
    return value


def filter_rows(layout, spec):
    padded = jnp.pad(spec, ((0, layout.degrees - MODES), (0, 0)))
    front = jnp.pad(spec, ((layout.rows, layout.rows), (0, 0)))
    natural = front[MODES : MODES + layout.rows]
    backward = front[layout.rows + MODES - layout.rows : layout.rows + MODES][::-1]
    return jnp.concatenate([padded, natural, backward], axis=0).astype(jnp.float32)


def on_device(fields, cotangent, spec_real, spec_imag):
    parts = lax.axis_size("space")
    index = lax.axis_index("space")
    layout = Layout(parts, fields.shape[1])
    width = LANES // 2
    chunks = fields.shape[-1] // width
    inverse = jnp.asarray(fourier_constants(layout)[1])
    constants = legendre_constants(parts, layout.local)

    def local_table(name):
        return lax.dynamic_index_in_dim(jnp.asarray(constants[name]), index, keepdims=False)

    pair_fwd = jnp.asarray(constants["pair_fwd"])
    place = jnp.reshape(index, (1,)).astype(jnp.int32)
    def bands(name, first, count):
        table = jnp.asarray(constants[name])
        return lax.optimization_barrier(
            lax.dynamic_slice_in_dim(table, first * layout.rows, count * layout.rows, 1)
        )

    def side_by_side(table):
        return jnp.concatenate([table[::2], table[1::2]], axis=2)

    synth_own = bands("synth_low", index, 1)
    analysis = bands("analysis", parts - 1 - index, parts).reshape(layout.twos, -1, layout.degrees)
    analysis = jnp.swapaxes(analysis, 1, 2)
    back_low = jnp.swapaxes(synth_own.reshape(layout.twos, -1, layout.degrees), 1, 2)
    synth_low = side_by_side(synth_own)
    pair_tables = [local_table(name) for name in ("pair_synth", "pair_back")]
    low_tables = [analysis, synth_low]
    tables = [inverse, back_low] + pair_tables + [jnp.asarray(constants["place"])]
    fields, cotangent = jnp.swapaxes(fields, 2, 3), jnp.swapaxes(cotangent, 2, 3)
    real_all = filter_rows(layout, spec_real)
    imag_all = filter_rows(layout, spec_imag)

    def others(sent):
        routes = [[(source, (source + shift) % parts) for source in range(parts)] for shift in range(1, parts)]
        return [lax.ppermute(sent, "space", route) for route in routes]

    held = []
    for chunk in range(chunks):
        if chunk == 1:
            place, low_tables, tables = lax.optimization_barrier((place, low_tables, tables))
        bounds = (0, layout.blocks) if chunk < chunks - 1 else (0, layout.low, layout.blocks)
        made = forward_call(layout, chunk, bounds, place, fields, pair_fwd)
        place, made = lax.optimization_barrier((place, list(made)))
        if len(made) > 1 and held:
            made[1], held[0][1] = lax.optimization_barrier((made[1], held[0][1]))
        held += [[own] + others(own) for own in made]

    hops, last_hops = sum_steps("dp"), sum_steps("space")
    waiting = []

    def hop_all(limit, tie):
        moved = []
        for value, done in waiting:
            if done < limit:
                parcels = hop_parcels(value, (hops + last_hops)[done])
                parcels, value, tie = lax.optimization_barrier((parcels, value, tie))
                value, done = sum(parcels, value), done + 1
            moved.append((value, done))
        waiting[:] = moved
        return tie

    def before(values):
        if not waiting:
            return values
        values, sums = lax.optimization_barrier((values, [value for value, _ in waiting]))
        waiting[:] = [(value, done) for value, (_, done) in zip(sums, waiting)]
        return values

    for chunk in range(chunks):
        columns = slice(chunk * width, (chunk + 1) * width)
        real, imag = real_all[:, columns], imag_all[:, columns]
        real_rows = jnp.concatenate([real, real], axis=1)
        imag_rows = jnp.concatenate([-imag, imag], axis=1)
        blocks, lows, apart = held[chunk], low_tables, chunk == chunks - 1
        if apart:
            lows = low_call(layout, chunk, blocks, low_tables, real_rows, imag_rows)
            lows = before(hop_all(len(hops), lows))
            blocks = held[-1]
        grads = spectral_call(layout, chunk, apart, blocks, lows, cotangent, tables, real_rows, imag_rows)
        if not apart:
            grads = hop_all(len(hops), grads)
            waiting.append((grads, 0))
            if chunk < chunks - 2:
                for _ in range(len(hops) // 2):
                    waiting[-1] = (sum_over(waiting[-1][0], hops[waiting[-1][1] :][:1]), waiting[-1][1] + 1)
                held[chunk + 1] = before(held[chunk + 1])
        else:
            grads = hop_all(len(hops) + len(last_hops), grads)
            waiting.append((grads, 0))

    total, done = waiting.pop()
    hops = hops + last_hops
    while done < len(hops):
        joined = [value for value, at in waiting if at == done]
        waiting = [(value, at) for value, at in waiting if at != done]
        if joined:
            total = jnp.concatenate(joined + [total], axis=0)
        total, done = sum_over(total, hops[done : done + 1]), done + 1
    rows = jnp.concatenate([value for value, _ in waiting] + [total], axis=0)
    rows = rows.reshape(chunks, 2, width, layout.degrees)

    batch_total = fields.shape[0] * lax.axis_size("dp")
    real, imag = (rows[:, part, :, :MODES].reshape(chunks * width, MODES) for part in range(2))
    return (real.T / batch_total, imag.T / batch_total)


def solution(mesh):
    in_specs = (P("dp", "space", None, None), P("dp", "space", None, None), P(), P())
    out_specs = (P(), P())
    return jax.shard_map(
        on_device, mesh=mesh, in_specs=in_specs, out_specs=out_specs, check_vma=False
    )
```

```python
import functools
import math

import jax
import jax.numpy as jnp
import ml_dtypes
import numpy as np
from jax import lax
from jax.experimental import pallas as pl
from jax.experimental.pallas import tpu as pltpu
from jax.sharding import PartitionSpec as P

NLAT = 126
NLON = 252
MODES = 126
LANES = 128
GROUP = 16
PAIRS = 8
VMEM = 30 * 1024 * 1024
FORWARD_VMEM = 56 * 1024 * 1024


def round_up(value, step):
    return -(-value // step) * step


def legendre_table():
    colatitude = math.pi * (np.arange(NLAT) + 0.5) / NLAT
    cos_theta, sin_theta = np.cos(colatitude), np.sin(colatitude)
    counters = np.arange(1, MODES)
    log_steps = 0.5 * np.log((2.0 * counters + 1.0) / (2.0 * counters))
    log_table = np.concatenate([[0.0], np.cumsum(log_steps)])
    table = np.zeros((MODES, MODES, NLAT))
    for order in range(MODES):
        table[order, order] = np.exp(
            0.5 * math.log(1.0 / (4.0 * math.pi)) + log_table[order] + order * np.log(sin_theta)
        )
        for degree in range(order + 1, MODES):
            growth = math.sqrt((4.0 * degree**2 - 1.0) / (degree**2 - order**2))
            below = degree - 1
            current = cos_theta * table[order, below]
            if below > order:
                damping = math.sqrt((below**2 - order**2) / (4.0 * below**2 - 1.0))
                current = current - damping * table[order, degree - 2]
            table[order, degree] = growth * current
    weight = math.pi / NLAT * (2.0 * math.pi / NLON) * sin_theta
    return table, table * weight


def to_bf16(array):
    return np.where(np.abs(array) < 2.0**-126, 0.0, array).astype(ml_dtypes.bfloat16)


class Layout:
    def __init__(self, parts, local):
        self.parts, self.local = parts, local
        self.rows = round_up(local + 1, 16)
        self.half = self.rows // 2
        self.pitch = self.rows + 8
        self.low = max(MODES - local, 0)
        high = MODES - self.low
        self.pairs = round_up((high + 1) // 2, 2)
        self.twos = round_up(self.low, 2) // 2
        self.blocks = self.low + self.pairs
        self.slots = round_up(self.low + 2 * self.pairs, 8)
        self.degrees = round_up(MODES, 16)
        self.first_natural = self.rows - MODES + self.low
        self.partner = MODES - 1 + self.low
        orders = list(range(self.low))
        for pair in range(self.pairs):
            order, mate = self.low + pair, self.partner - self.low - pair
            orders += [order if order <= mate else -1, mate if order < mate else -1]
        self.orders = np.array(orders + [-1] * (self.slots - len(orders)))


def fourier_constants(layout):
    orders = np.maximum(layout.orders, 0)
    angles = 2.0 * math.pi / NLON * (orders[:, None] * np.arange(NLON)[None] % NLON)
    live = (layout.orders >= 0)[:, None]
    basis = np.concatenate([np.cos(angles) * live, -np.sin(angles) * live])
    factor = np.where(layout.orders == 0, 1.0, 2.0)[:, None]
    inverse = basis * np.concatenate([factor, factor])
    return to_bf16(basis), to_bf16(inverse)


@functools.lru_cache(maxsize=None)
def legendre_constants(parts, local):
    layout = Layout(parts, local)
    plain, weighted = legendre_table()
    rows, degrees, low, pairs = layout.rows, layout.degrees, layout.low, layout.pairs
    analysis = np.zeros((2 * layout.twos, 2 * parts * rows, degrees))
    synth_low = np.zeros((2 * layout.twos, parts * rows, degrees))
    pair_fwd = np.zeros((parts, pairs, rows, 2 * rows))
    pair_back = np.zeros((parts, pairs, rows, 2 * rows))
    for part in range(parts):
        own = slice(part * local, (part + 1) * local)
        start = part * rows
        synth_low[:low, start : start + local, :MODES] = np.swapaxes(plain[:low, :, own], 1, 2)
        for turn in (1, 2):
            start = (turn * parts - 1 - part) * rows
            analysis[:low, start : start + local, :MODES] = np.swapaxes(weighted[:low, :, own], 1, 2)
        for pair in range(pairs):
            order = low + pair
            mate = layout.partner - order
            for target, table in ((pair_fwd, weighted), (pair_back, plain)):
                if order <= mate:
                    count = MODES - order
                    target[part, pair, rows - count :, :local] = table[order, order:, own]
                if order < mate:
                    count = MODES - mate
                    target[part, pair, :count, rows : rows + local] = table[mate, mate:, own][::-1]
    pair_synth = np.swapaxes(pair_back, -1, -2)
    place = np.zeros((degrees, 2 * rows))
    for row in range(rows):
        if row >= rows - MODES + low:
            place[MODES - rows + row, row] = 1.0
        if MODES - 1 - row >= 0:
            place[MODES - 1 - row, rows + row] = 1.0
    return {
        "analysis": to_bf16(analysis),
        "synth_low": to_bf16(synth_low),
        "pair_fwd": to_bf16(pair_fwd),
        "pair_back": to_bf16(np.concatenate([pair_back[:, ::2], pair_back[:, 1::2]], axis=3)),
        "pair_synth": to_bf16(np.concatenate([pair_synth[:, ::2], pair_synth[:, 1::2]], axis=3)),
        "place": place.astype(np.float32),
    }


def dot(left, right, sides=(1, 0)):
    contract = (((sides[0],), (sides[1],)), ((), ()))
    return lax.dot_general(left, right, contract, preferred_element_type=jnp.float32)


def dot_two(left, first, second):
    upper = jnp.concatenate([first, jnp.zeros_like(first)], axis=1)
    lower = jnp.concatenate([jnp.zeros_like(second), second], axis=1)
    return dot(left, jnp.concatenate([upper, lower], axis=0))


def swap_halves(values):
    return pltpu.roll(values, LANES // 2, 1)


def interleave(first, second):
    lane = lax.broadcasted_iota(jnp.int32, first.shape, 1)
    below = lane < LANES // 2
    return (
        jnp.where(below, first, swap_halves(second)),
        jnp.where(below, swap_halves(first), second),
    )


def gelu_slope(values):
    cumulative = 0.5 * (1.0 + lax.erf(values / math.sqrt(2.0)))
    density = jnp.exp(-0.5 * values * values) / math.sqrt(2.0 * math.pi)
    return cumulative + values * density


def grid_rows(layout, north, south, quad, group):
    rows = []
    for pair in (2 * quad, 2 * quad + 1):
        rows.append(north[0, pair])
        values = south[0, pair]
        if layout.rows > layout.local:
            latitude = layout.half + group * PAIRS + pair
            values = jnp.where(latitude < layout.local, values, jnp.zeros_like(values))
        rows.append(values)
    return jnp.concatenate(rows, axis=0)


def scatter_rows(layout, values, scratch, quad, group):
    slots = values.shape[0] // 2
    for which in range(2):
        columns = slice(which * LANES, (which + 1) * LANES)
        upper, lower = interleave(values[:slots, columns], values[slots:, columns])
        latitude = group * PAIRS + 2 * quad + which
        scratch[pl.ds(latitude, slots, stride=layout.pitch), :] = upper
        scratch[pl.ds(latitude + layout.half, slots, stride=layout.pitch), :] = lower


def gather_rows(layout, scratch, quad, group):
    slots = layout.slots
    cosine, sine = [], []
    for which in range(2):
        latitude = group * PAIRS + 2 * quad + which
        upper = scratch[pl.ds(latitude, slots, stride=layout.pitch), :]
        lower = scratch[pl.ds(latitude + layout.half, slots, stride=layout.pitch), :]
        first, second = interleave(upper, lower)
        cosine.append(first.astype(jnp.bfloat16))
        sine.append(second.astype(jnp.bfloat16))
    return jnp.concatenate(
        [jnp.concatenate(cosine, axis=1), jnp.concatenate(sine, axis=1)], axis=0
    )


def order_rows(layout, scratch, first, count):
    parts = []
    for order in range(count):
        start = pl.multiple_of((first + order) * layout.pitch, 8)
        parts.append(scratch[pl.ds(start, layout.rows), :])
    return jnp.concatenate(parts, axis=0).astype(jnp.bfloat16)


def band_copies(layout, chunk, fields, buffer, sems):
    width = LANES // 2
    copies = []
    for group in range(layout.half // PAIRS):
        started = []
        for side in range(2):
            first = side * layout.half + group * PAIRS
            count = min(PAIRS, layout.local - first)
            if count > 0:
                started.append(
                    pltpu.make_async_copy(
                        fields.at[0, pl.ds(first, count), pl.ds(chunk * width, width), :],
                        buffer.at[pl.ds(first, count)],
                        sems.at[2 * group + side],
                    )
                )
        copies.append(started)
    return copies


def forward_kernel(layout, chunk, bounds, index, fields, basis_all, pair_all, *refs):
    outs, refs = refs[: len(bounds) - 1], refs[len(bounds) - 1 :]
    scratch, buffer, basis, stage, pair_fwd, sems, basis_sem, pair_sem, out_sems = refs
    basis_copy = pltpu.make_async_copy(basis_all, basis, basis_sem)
    basis_copy.start()
    copies = band_copies(layout, chunk, fields, buffer, sems)
    for started in copies[:2]:
        for copy in started:
            copy.start()
    tables = pltpu.make_async_copy(pair_all.at[index[0]], pair_fwd, pair_sem)
    tables.start()
    if layout.rows > layout.local:
        shape = (layout.rows - layout.local,) + buffer.shape[1:]
        buffer[layout.local :] = jnp.zeros(shape, buffer.dtype)
    basis_copy.wait()
    for group, started in enumerate(copies):
        for copy in started:
            copy.wait()
        for copy in sum(copies[group + 2 : group + 3], []):
            copy.start()
        for quad in range(PAIRS // 2):
            rows = []
            for which in range(2):
                latitude = group * PAIRS + 2 * quad + which
                rows += [buffer[latitude], buffer[latitude + layout.half]]
            grid = jnp.concatenate(rows, axis=0)
            scatter_rows(layout, dot(basis[...], grid, (1, 1)), scratch, quad, group)

    def low_block(order, carry):
        stage[order] = order_rows(layout, scratch, order, 1)
        return carry

    def pair_block(pair, carry):
        values = order_rows(layout, scratch, layout.low + 2 * pair, 2)
        stage[layout.low + pair] = dot(pair_fwd[pair], values).astype(jnp.bfloat16)
        return carry

    flushes = []

    def flush(first, last):
        at = max(at for at in range(len(outs)) if bounds[at] <= first)
        flushes.append(
            pltpu.make_async_copy(
                stage.at[pl.ds(first, last - first)],
                outs[at].at[pl.ds(first - bounds[at], last - first)],
                out_sems.at[len(flushes)],
            )
        )
        flushes[-1].start()

    middle = layout.low // 2
    for first, last in ((0, middle), (middle, layout.low)):
        lax.fori_loop(first, last, low_block, 0, unroll=8)
        flush(first, last)
    tables.wait()
    lax.fori_loop(0, layout.pairs, pair_block, 0, unroll=8)
    flush(layout.low, layout.blocks)
    for copy in flushes:
        copy.wait()


def mix(spectral, swapped, real_rows, imag_rows):
    return (spectral * real_rows + swapped * imag_rows).astype(jnp.bfloat16)


def order_groups(layout):
    for start in range(0, layout.low, GROUP):
        stop = min(start + GROUP, layout.low)
        yield start // 2, (stop + 1) // 2, start // 16 * 16


def low_kernel(layout, *refs):
    low_orders(layout, refs[: layout.parts], *refs[layout.parts :])


def low_orders(layout, held, analysis, synth_low, real_ref, imag_ref, grid_low, spec_low, swap_low):
    degrees = layout.degrees
    for start, stop, top in order_groups(layout):
        real_rows = real_ref[top:degrees, :]
        imag_rows = imag_ref[top:degrees, :]

        def low_block(two, carry):
            values = []
            for order in (2 * two, jnp.minimum(2 * two + 1, layout.low - 1)):
                values.append(jnp.concatenate([ref[order] for ref in held], axis=0))
            spectral = dot_two(analysis[two, top:degrees, :], *values).astype(jnp.bfloat16)
            for which in range(2):
                spec_low[2 * two + which, top:degrees, :] = spectral[:, which * LANES : (which + 1) * LANES]
            return carry

        def mix_block(two, carry):
            mixed = []
            for order in (2 * two, 2 * two + 1):
                spectral = spec_low[order, top:degrees, :].astype(jnp.float32)
                swapped = swap_halves(spectral)
                swap_low[order, top:degrees, :] = swapped.astype(jnp.bfloat16)
                values = mix(spectral, swapped, real_rows, imag_rows)
                if top:
                    values = jnp.concatenate([jnp.zeros((top, LANES), values.dtype), values], axis=0)
                mixed.append(values)
            values = dot_two(synth_low[two], *mixed)
            for which in range(2):
                begin = pl.multiple_of((2 * two + which) * layout.pitch, 8)
                grid_low[pl.ds(begin, layout.rows), :] = values[:, which * LANES : (which + 1) * LANES]
            return carry

        lax.fori_loop(start, stop, low_block, 0, unroll=4)
        lax.fori_loop(start, stop, mix_block, 0, unroll=4)


def spectral_kernel(layout, apart, side, *refs):
    held, lows, refs = refs[: layout.parts], refs[layout.parts : layout.parts + 2 + apart], refs[layout.parts + 2 + apart :]
    north, south, basis, back_low, pair_synth, pair_back, place, real_ref, imag_ref = refs[:9]
    keep, send, scratch, returned, spec_low, swap_low, spec_pair, swap_pair, sems = refs[9:]
    offset = 0 if apart else layout.low
    group = pl.program_id(0)
    rows, degrees, low = layout.rows, layout.degrees, layout.low
    if apart:
        sources = (lows[0].at[pl.ds(0, low * layout.pitch)], lows[1], lows[2])
        targets = (scratch.at[pl.ds(0, low * layout.pitch)], spec_low, swap_low)
        copies = [pltpu.make_async_copy(*ends, sems.at[at]) for at, ends in enumerate(zip(sources, targets))]

    @pl.when(group == 0)
    def _():
        if apart:
            for copy in copies:
                copy.start()
        else:
            low_orders(layout, held, *lows, real_ref, imag_ref, scratch, spec_low, swap_low)
        line = lax.broadcasted_iota(jnp.int32, (rows, LANES), 0)

        def pair_block(two, carry):
            mixed = []
            for pair in (2 * two, 2 * two + 1):
                total = sum(ref[offset + pair].astype(jnp.float32) for ref in held)
                spectral = total.astype(jnp.bfloat16)
                spec_pair[pair] = spectral
                natural = line >= layout.first_natural + pair
                real_rows = jnp.where(natural, real_ref[degrees : degrees + rows, :], real_ref[degrees + rows :, :])
                imag_rows = jnp.where(natural, imag_ref[degrees : degrees + rows, :], imag_ref[degrees + rows :, :])
                spectral = spectral.astype(jnp.float32)
                swapped = swap_halves(spectral)
                swap_pair[pair] = swapped.astype(jnp.bfloat16)
                mixed.append(mix(spectral, swapped, real_rows, imag_rows))
            values = dot_two(pair_synth[two], *mixed)
            for which in range(4):
                begin = pl.multiple_of((low + 4 * two + which) * layout.pitch, 8)
                columns = slice(which // 2 * LANES, (which // 2 + 1) * LANES)
                scratch[pl.ds(begin, rows), :] = values[which % 2 * rows : (which % 2 + 1) * rows, columns]
            return carry

        lax.fori_loop(0, layout.pairs // 2, pair_block, 0, unroll=4)
        used = (low + 2 * layout.pairs) * layout.pitch
        if used < layout.slots * layout.pitch:
            scratch[used : layout.slots * layout.pitch, :] = jnp.zeros(
                (layout.slots * layout.pitch - used, LANES), jnp.float32
            )
        if apart:
            copies[0].wait()

    for quad in range(PAIRS // 2):
        modes = gather_rows(layout, scratch, quad, group)
        signal = dot(modes, basis[...], (0, 0))
        incoming = grid_rows(layout, north, south, quad, group).astype(jnp.float32)
        upstream = (incoming * gelu_slope(signal)).astype(jnp.bfloat16)
        scatter_rows(layout, dot(basis[...], upstream, (1, 1)), returned, quad, group)

    @pl.when(group == pl.num_programs(0) - 1)
    def _():
        if apart:
            copies[1].wait()
            copies[2].wait()

        def products(spectral, swapped, back):
            return spectral.astype(jnp.float32) * back, swapped.astype(jnp.float32) * back

        zeros = jnp.zeros((degrees, LANES), jnp.float32)
        same, cross = zeros, zeros
        for start, stop, top in order_groups(layout):

            def low_block(two, carry):
                values = [order_rows(layout, returned, 2 * two + which, 1) for which in range(2)]
                back = dot_two(back_low[two, top:degrees, :], *values)
                for which in range(2):
                    order = 2 * two + which
                    first, second = products(
                        spec_low[order, top:degrees, :],
                        swap_low[order, top:degrees, :],
                        back[:, which * LANES : (which + 1) * LANES],
                    )
                    carry = carry[0] + first, carry[1] + second
                return carry

            part = jnp.zeros((degrees - top, LANES), jnp.float32)
            first, second = lax.fori_loop(start, stop, low_block, (part, part), unroll=4)
            if top:
                empty = jnp.zeros((top, LANES), jnp.float32)
                first = jnp.concatenate([empty, first], axis=0)
                second = jnp.concatenate([empty, second], axis=0)
            same, cross = same + first, cross + second

        line = lax.broadcasted_iota(jnp.int32, (rows, LANES), 0)

        def pair_block(two, carry):
            values = [order_rows(layout, returned, low + 4 * two + 2 * which, 2) for which in range(2)]
            back = dot_two(pair_back[two], *values)
            for which in range(2):
                pair = 2 * two + which
                first, second = products(
                    spec_pair[pair], swap_pair[pair], back[:, which * LANES : (which + 1) * LANES]
                )
                natural = line >= layout.first_natural + pair
                carry = (
                    carry[0] + jnp.where(natural, first, 0.0),
                    carry[1] + jnp.where(natural, second, 0.0),
                    carry[2] + jnp.where(natural, 0.0, first),
                    carry[3] + jnp.where(natural, 0.0, second),
                )
            return carry

        part = jnp.zeros((rows, LANES), jnp.float32)
        sums = lax.fori_loop(0, layout.pairs // 2, pair_block, (part,) * 4, unroll=4)
        placed = jnp.dot(
            place[...],
            jnp.concatenate(
                [jnp.concatenate(sums[:2], axis=1), jnp.concatenate(sums[2:], axis=1)], axis=0
            ),
            preferred_element_type=jnp.float32,
            precision=lax.Precision.HIGHEST,
        )
        same = same + placed[:, :LANES]
        cross = cross + placed[:, LANES:]
        real = same + swap_halves(same)
        imag = cross - swap_halves(cross)
        lane = lax.broadcasted_iota(jnp.int32, real.shape, 1)
        grads = jnp.where(lane < LANES // 2, real, imag).T
        upper, lower = grads[: LANES // 2], grads[LANES // 2 :]
        keep[...] = jnp.where(side[0] == 0, upper, lower)
        send[...] = jnp.where(side[0] == 0, lower, upper)


def grid_specs(layout, chunk):
    last = -(-layout.local // PAIRS) - 1
    shift = layout.half // PAIRS
    block = (1, PAIRS, LANES // 2, NLON)
    return [
        pl.BlockSpec(block, lambda g: (0, jnp.minimum(g, last), chunk, 0)),
        pl.BlockSpec(block, lambda g: (0, jnp.minimum(shift + g, last), chunk, 0)),
    ]


def whole():
    return pl.BlockSpec(memory_space=pltpu.VMEM)


def forward_call(layout, chunk, bounds, index, fields, pair_fwd):
    basis = jnp.asarray(fourier_constants(layout)[0])
    slots = basis.shape[0] // 2
    groups = layout.half // PAIRS
    anywhere = pl.BlockSpec(memory_space=pl.ANY)
    counts = [last - first for first, last in zip(bounds, bounds[1:])]
    return pl.pallas_call(
        functools.partial(forward_kernel, layout, chunk, bounds),
        in_specs=[pl.BlockSpec(memory_space=pltpu.SMEM)] + [anywhere] * 3,
        out_specs=[anywhere] * len(counts),
        out_shape=[jax.ShapeDtypeStruct((count, layout.rows, LANES), jnp.bfloat16) for count in counts],
        scratch_shapes=[
            pltpu.VMEM((slots * layout.pitch, LANES), jnp.float32),
            pltpu.VMEM((layout.rows, LANES // 2, NLON), jnp.bfloat16),
            pltpu.VMEM(basis.shape, jnp.bfloat16),
            pltpu.VMEM((layout.blocks, layout.rows, LANES), jnp.bfloat16),
            pltpu.VMEM(pair_fwd.shape[1:], jnp.bfloat16),
            pltpu.SemaphoreType.DMA((2 * groups,)),
            pltpu.SemaphoreType.DMA,
            pltpu.SemaphoreType.DMA,
            pltpu.SemaphoreType.DMA((3,)),
        ],
        compiler_params=pltpu.CompilerParams(vmem_limit_bytes=FORWARD_VMEM),
        cost_estimate=pl.CostEstimate(flops=1_000_000, bytes_accessed=100_000, transcendentals=0),
        name=f"forward_{chunk}",
    )(index, fields, basis, pair_fwd)


def low_call(layout, chunk, coeffs, tables, real_rows, imag_rows):
    operands = list(coeffs) + list(tables) + [real_rows, imag_rows]
    spectra = jax.ShapeDtypeStruct((2 * layout.twos, layout.degrees, LANES), jnp.bfloat16)
    return pl.pallas_call(
        functools.partial(low_kernel, layout),
        in_specs=[whole()] * len(operands),
        out_specs=[whole()] * 3,
        out_shape=[jax.ShapeDtypeStruct((2 * layout.twos * layout.pitch, LANES), jnp.float32), spectra, spectra],
        compiler_params=pltpu.CompilerParams(vmem_limit_bytes=VMEM),
        cost_estimate=pl.CostEstimate(flops=8_000_000_000, bytes_accessed=30_000_000, transcendentals=0),
        name=f"low_{chunk}",
    )(*operands)


def spectral_call(layout, chunk, apart, side, blocks, lows, cotangent, tables, real_rows, imag_rows):
    half = jax.ShapeDtypeStruct((LANES // 2, layout.degrees), jnp.float32)
    operands = [side] + list(blocks) + list(lows) + [cotangent, cotangent] + list(tables) + [real_rows, imag_rows]
    low_spec = pl.BlockSpec(memory_space=pl.ANY) if apart else whole()
    specs = [pl.BlockSpec(memory_space=pltpu.SMEM)] + [whole()] * len(blocks) + [low_spec] * len(lows)
    specs += grid_specs(layout, chunk) + [whole()] * (len(tables) + 2)
    return pl.pallas_call(
        functools.partial(spectral_kernel, layout, apart),
        grid=(layout.half // PAIRS,),
        in_specs=specs,
        out_specs=[whole()] * 2,
        out_shape=[half, half],
        scratch_shapes=[
            pltpu.VMEM((layout.slots * layout.pitch, LANES), jnp.float32),
            pltpu.VMEM((layout.slots * layout.pitch, LANES), jnp.float32),
            pltpu.VMEM((2 * layout.twos, layout.degrees, LANES), jnp.bfloat16),
            pltpu.VMEM((2 * layout.twos, layout.degrees, LANES), jnp.bfloat16),
            pltpu.VMEM((layout.pairs, layout.rows, LANES), jnp.bfloat16),
            pltpu.VMEM((layout.pairs, layout.rows, LANES), jnp.bfloat16),
            pltpu.SemaphoreType.DMA((3,)),
        ],
        compiler_params=pltpu.CompilerParams(vmem_limit_bytes=VMEM),
        cost_estimate=pl.CostEstimate(flops=8_000_000_000, bytes_accessed=30_000_000, transcendentals=0),
        name=f"spectral_{chunk}",
    )(*operands)


def radices(size):
    found, factor = [], 2
    while size > 1:
        while size % factor == 0:
            found.append(factor)
            size //= factor
        factor += 1
    return found


def sum_steps(axis):
    size = lax.axis_size(axis)
    steps, stride = [], 1
    for radix in radices(size):
        steps.append((axis, stride, radix))
        stride *= radix
    return steps


def hop_parcels(value, step):
    axis, stride, radix = step
    parcels = []
    for turn in range(1, radix):
        pairs = []
        for index in range(lax.axis_size(axis)):
            digit = index // stride % radix
            pairs.append((index, index + ((digit + turn) % radix - digit) * stride))
        parcels.append(lax.ppermute(value, axis, pairs))
    return parcels


def filter_rows(layout, spec):
    padded = jnp.pad(spec, ((0, layout.degrees - MODES), (0, 0)))
    front = jnp.pad(spec, ((layout.rows, layout.rows), (0, 0)))
    natural = front[MODES : MODES + layout.rows]
    backward = front[layout.rows + MODES - layout.rows : layout.rows + MODES][::-1]
    return jnp.concatenate([padded, natural, backward], axis=0).astype(jnp.float32)


def on_device(fields, cotangent, spec_real, spec_imag):
    parts = lax.axis_size("space")
    index = lax.axis_index("space")
    layout = Layout(parts, fields.shape[1])
    width = LANES // 2
    chunks = fields.shape[-1] // width
    inverse = jnp.asarray(fourier_constants(layout)[1])
    constants = legendre_constants(parts, layout.local)

    def local_table(name):
        return lax.dynamic_index_in_dim(jnp.asarray(constants[name]), index, keepdims=False)

    pair_fwd = jnp.asarray(constants["pair_fwd"])
    place = jnp.reshape(index, (1,)).astype(jnp.int32)
    def bands(name, first, count):
        table = jnp.asarray(constants[name])
        return lax.optimization_barrier(
            lax.dynamic_slice_in_dim(table, first * layout.rows, count * layout.rows, 1)
        )

    def side_by_side(table):
        return jnp.concatenate([table[::2], table[1::2]], axis=2)

    synth_own = bands("synth_low", index, 1)
    analysis = bands("analysis", parts - 1 - index, parts).reshape(layout.twos, -1, layout.degrees)
    analysis = jnp.swapaxes(analysis, 1, 2)
    back_low = jnp.swapaxes(synth_own.reshape(layout.twos, -1, layout.degrees), 1, 2)
    synth_low = side_by_side(synth_own)
    pair_tables = [local_table(name) for name in ("pair_synth", "pair_back")]
    low_tables = [analysis, synth_low]
    tables = [inverse, back_low] + pair_tables + [jnp.asarray(constants["place"])]
    fields, cotangent = jnp.swapaxes(fields, 2, 3), jnp.swapaxes(cotangent, 2, 3)
    real_all = filter_rows(layout, spec_real)
    imag_all = filter_rows(layout, spec_imag)

    def others(sent):
        routes = [[(source, (source + shift) % parts) for source in range(parts)] for shift in range(1, parts)]
        return [lax.ppermute(sent, "space", route) for route in routes]

    held = []
    for chunk in range(chunks):
        if chunk == 1:
            place, low_tables, tables = lax.optimization_barrier((place, low_tables, tables))
        bounds = (0, layout.blocks) if chunk < chunks - 1 else (0, layout.low, layout.blocks)
        made = forward_call(layout, chunk, bounds, place, fields, pair_fwd)
        place, made = lax.optimization_barrier((place, list(made)))
        if len(made) > 1 and held:
            made[1], held[0][1] = lax.optimization_barrier((made[1], held[0][1]))
        held += [[own] + others(own) for own in made]

    hops = sum_steps("dp") + sum_steps("space")
    count_dp = len(sum_steps("dp"))
    swap = [(device, device ^ 1) for device in range(lax.axis_size("dp"))]
    side = lax.rem(lax.axis_index("dp"), 2).reshape((1,)).astype(jnp.int32)
    waiting = []

    def launch(value, done):
        if done:
            return value, hop_parcels(value, hops[done])
        keep, send = value
        return keep, [lax.ppermute(send, "dp", swap)]

    def hop_all(limit, tie):
        moved = []
        for value, done in waiting:
            if done < limit:
                value, parcels = launch(value, done)
                parcels, value, tie = lax.optimization_barrier((parcels, value, tie))
                value, done = sum(parcels, value), done + 1
            moved.append((value, done))
        waiting[:] = moved
        return tie

    def hop_last(times):
        for _ in range(times):
            value, done = waiting[-1]
            value, parcels = launch(value, done)
            waiting[-1] = (sum(parcels, value), done + 1)

    def before(values):
        if not waiting:
            return values
        values, sums = lax.optimization_barrier((values, [value for value, _ in waiting]))
        waiting[:] = [(value, done) for value, (_, done) in zip(sums, waiting)]
        return values

    for chunk in range(chunks):
        columns = slice(chunk * width, (chunk + 1) * width)
        real, imag = real_all[:, columns], imag_all[:, columns]
        real_rows = jnp.concatenate([real, real], axis=1)
        imag_rows = jnp.concatenate([-imag, imag], axis=1)
        blocks, lows, apart = held[chunk], low_tables, chunk == chunks - 1
        if apart:
            lows = low_call(layout, chunk, blocks, low_tables, real_rows, imag_rows)
            lows = before(hop_all(count_dp, lows))
            blocks = held[-1]
        grads = spectral_call(layout, chunk, apart, side, blocks, lows, cotangent, tables, real_rows, imag_rows)
        grads = hop_all(len(hops) if apart else count_dp, grads)
        waiting.append((grads, 0))
        if chunk < chunks - 2:
            hop_last(count_dp // 2)
            held[chunk + 1] = before(held[chunk + 1])

    hop_last(1)
    total, done = waiting.pop()
    while done < len(hops):
        joined = [value for value, at in waiting if at == done]
        waiting = [(value, at) for value, at in waiting if at != done]
        if joined:
            total = jnp.concatenate(joined + [total], axis=0)
        total, done = sum(hop_parcels(total, hops[done]), total), done + 1
    mine = jnp.concatenate([value for value, _ in waiting] + [total], axis=0)
    other = lax.ppermute(mine, "dp", swap)
    real = jnp.where(side[0] == 0, mine, other)[:, :MODES]
    imag = jnp.where(side[0] == 0, other, mine)[:, :MODES]
    batch_total = fields.shape[0] * lax.axis_size("dp")
    return (real.T / batch_total, imag.T / batch_total)


def solution(mesh):
    in_specs = (P("dp", "space", None, None), P("dp", "space", None, None), P(), P())
    out_specs = (P(), P())
    return jax.shard_map(
        on_device, mesh=mesh, in_specs=in_specs, out_specs=out_specs, check_vma=False
    )
```

```python
import functools
import math

import jax
import jax.numpy as jnp
import ml_dtypes
import numpy as np
from jax import lax
from jax.experimental import pallas as pl
from jax.experimental.pallas import tpu as pltpu
from jax.sharding import PartitionSpec as P

NLAT = 126
NLON = 252
MODES = 126
LANES = 128
GROUP = 16
PAIRS = 8
VMEM = 30 * 1024 * 1024
FORWARD_VMEM = 56 * 1024 * 1024


def round_up(value, step):
    return -(-value // step) * step


def legendre_table():
    colatitude = math.pi * (np.arange(NLAT) + 0.5) / NLAT
    cos_theta, sin_theta = np.cos(colatitude), np.sin(colatitude)
    counters = np.arange(1, MODES)
    log_steps = 0.5 * np.log((2.0 * counters + 1.0) / (2.0 * counters))
    log_table = np.concatenate([[0.0], np.cumsum(log_steps)])
    table = np.zeros((MODES, MODES, NLAT))
    for order in range(MODES):
        table[order, order] = np.exp(
            0.5 * math.log(1.0 / (4.0 * math.pi)) + log_table[order] + order * np.log(sin_theta)
        )
        for degree in range(order + 1, MODES):
            growth = math.sqrt((4.0 * degree**2 - 1.0) / (degree**2 - order**2))
            below = degree - 1
            current = cos_theta * table[order, below]
            if below > order:
                damping = math.sqrt((below**2 - order**2) / (4.0 * below**2 - 1.0))
                current = current - damping * table[order, degree - 2]
            table[order, degree] = growth * current
    weight = math.pi / NLAT * (2.0 * math.pi / NLON) * sin_theta
    return table, table * weight


def to_bf16(array):
    return np.where(np.abs(array) < 2.0**-126, 0.0, array).astype(ml_dtypes.bfloat16)


class Layout:
    def __init__(self, parts, local):
        self.parts, self.local = parts, local
        self.rows = round_up(local + 1, 16)
        self.half = self.rows // 2
        self.pitch = self.rows + 8
        self.low = max(MODES - local, 0)
        high = MODES - self.low
        self.pairs = round_up((high + 1) // 2, 2)
        self.twos = round_up(self.low, 2) // 2
        self.blocks = self.low + self.pairs
        self.slots = round_up(self.low + 2 * self.pairs, 8)
        self.degrees = round_up(MODES, 16)
        self.first_natural = self.rows - MODES + self.low
        self.partner = MODES - 1 + self.low
        orders = list(range(self.low))
        for pair in range(self.pairs):
            order, mate = self.low + pair, self.partner - self.low - pair
            orders += [order if order <= mate else -1, mate if order < mate else -1]
        self.orders = np.array(orders + [-1] * (self.slots - len(orders)))


def fourier_constants(layout):
    orders = np.maximum(layout.orders, 0)
    angles = 2.0 * math.pi / NLON * (orders[:, None] * np.arange(NLON)[None] % NLON)
    live = (layout.orders >= 0)[:, None]
    basis = np.concatenate([np.cos(angles) * live, -np.sin(angles) * live])
    factor = np.where(layout.orders == 0, 1.0, 2.0)[:, None]
    inverse = basis * np.concatenate([factor, factor])
    return to_bf16(basis), to_bf16(inverse)


@functools.lru_cache(maxsize=None)
def legendre_constants(parts, local):
    layout = Layout(parts, local)
    plain, weighted = legendre_table()
    rows, degrees, low, pairs = layout.rows, layout.degrees, layout.low, layout.pairs
    analysis = np.zeros((2 * layout.twos, 2 * parts * rows, degrees))
    synth_low = np.zeros((2 * layout.twos, parts * rows, degrees))
    pair_fwd = np.zeros((parts, pairs, rows, 2 * rows))
    pair_back = np.zeros((parts, pairs, rows, 2 * rows))
    for part in range(parts):
        own = slice(part * local, (part + 1) * local)
        start = part * rows
        synth_low[:low, start : start + local, :MODES] = np.swapaxes(plain[:low, :, own], 1, 2)
        for turn in (1, 2):
            start = (turn * parts - 1 - part) * rows
            analysis[:low, start : start + local, :MODES] = np.swapaxes(weighted[:low, :, own], 1, 2)
        for pair in range(pairs):
            order = low + pair
            mate = layout.partner - order
            for target, table in ((pair_fwd, weighted), (pair_back, plain)):
                if order <= mate:
                    count = MODES - order
                    target[part, pair, rows - count :, :local] = table[order, order:, own]
                if order < mate:
                    count = MODES - mate
                    target[part, pair, :count, rows : rows + local] = table[mate, mate:, own][::-1]
    pair_synth = np.swapaxes(pair_back, -1, -2)
    place = np.zeros((degrees, 2 * rows))
    for row in range(rows):
        if row >= rows - MODES + low:
            place[MODES - rows + row, row] = 1.0
        if MODES - 1 - row >= 0:
            place[MODES - 1 - row, rows + row] = 1.0
    return {
        "analysis": to_bf16(analysis),
        "synth_low": to_bf16(synth_low),
        "pair_fwd": to_bf16(pair_fwd),
        "pair_back": to_bf16(np.concatenate([pair_back[:, ::2], pair_back[:, 1::2]], axis=3)),
        "pair_synth": to_bf16(np.concatenate([pair_synth[:, ::2], pair_synth[:, 1::2]], axis=3)),
        "place": place.astype(np.float32),
    }


def dot(left, right, sides=(1, 0)):
    contract = (((sides[0],), (sides[1],)), ((), ()))
    return lax.dot_general(left, right, contract, preferred_element_type=jnp.float32)


def dot_two(left, first, second):
    upper = jnp.concatenate([first, jnp.zeros_like(first)], axis=1)
    lower = jnp.concatenate([jnp.zeros_like(second), second], axis=1)
    return dot(left, jnp.concatenate([upper, lower], axis=0))


def swap_halves(values):
    return pltpu.roll(values, LANES // 2, 1)


def interleave(first, second):
    lane = lax.broadcasted_iota(jnp.int32, first.shape, 1)
    below = lane < LANES // 2
    return (
        jnp.where(below, first, swap_halves(second)),
        jnp.where(below, swap_halves(first), second),
    )


def gelu_slope(values):
    cumulative = 0.5 * (1.0 + lax.erf(values / math.sqrt(2.0)))
    density = jnp.exp(-0.5 * values * values) / math.sqrt(2.0 * math.pi)
    return cumulative + values * density


def grid_rows(layout, north, south, quad, group):
    rows = []
    for pair in (2 * quad, 2 * quad + 1):
        rows.append(north[0, pair])
        values = south[0, pair]
        if layout.rows > layout.local:
            latitude = layout.half + group * PAIRS + pair
            values = jnp.where(latitude < layout.local, values, jnp.zeros_like(values))
        rows.append(values)
    return jnp.concatenate(rows, axis=0)


def scatter_rows(layout, values, scratch, quad, group):
    slots = values.shape[0] // 2
    for which in range(2):
        columns = slice(which * LANES, (which + 1) * LANES)
        upper, lower = interleave(values[:slots, columns], values[slots:, columns])
        latitude = group * PAIRS + 2 * quad + which
        scratch[pl.ds(latitude, slots, stride=layout.pitch), :] = upper
        scratch[pl.ds(latitude + layout.half, slots, stride=layout.pitch), :] = lower


def gather_rows(layout, scratch, quad, group):
    slots = layout.slots
    cosine, sine = [], []
    for which in range(2):
        latitude = group * PAIRS + 2 * quad + which
        upper = scratch[pl.ds(latitude, slots, stride=layout.pitch), :]
        lower = scratch[pl.ds(latitude + layout.half, slots, stride=layout.pitch), :]
        first, second = interleave(upper, lower)
        cosine.append(first.astype(jnp.bfloat16))
        sine.append(second.astype(jnp.bfloat16))
    return jnp.concatenate(
        [jnp.concatenate(cosine, axis=1), jnp.concatenate(sine, axis=1)], axis=0
    )


def order_rows(layout, scratch, first, count):
    parts = []
    for order in range(count):
        start = pl.multiple_of((first + order) * layout.pitch, 8)
        parts.append(scratch[pl.ds(start, layout.rows), :])
    return jnp.concatenate(parts, axis=0).astype(jnp.bfloat16)


def band_copies(layout, chunk, fields, buffer, sems):
    width = LANES // 2
    copies = []
    for group in range(layout.half // PAIRS):
        started = []
        for side in range(2):
            first = side * layout.half + group * PAIRS
            count = min(PAIRS, layout.local - first)
            if count > 0:
                started.append(
                    pltpu.make_async_copy(
                        fields.at[0, pl.ds(first, count), pl.ds(chunk * width, width), :],
                        buffer.at[pl.ds(first, count)],
                        sems.at[2 * group + side],
                    )
                )
        copies.append(started)
    return copies


def forward_kernel(layout, chunk, bounds, index, fields, basis_all, pair_all, *refs):
    outs, refs = refs[: len(bounds) - 1], refs[len(bounds) - 1 :]
    scratch, buffer, basis, stage, pair_fwd, sems, basis_sem, pair_sem, out_sems = refs
    basis_copy = pltpu.make_async_copy(basis_all, basis, basis_sem)
    basis_copy.start()
    copies = band_copies(layout, chunk, fields, buffer, sems)
    for started in copies[:2]:
        for copy in started:
            copy.start()
    tables = pltpu.make_async_copy(pair_all.at[index[0]], pair_fwd, pair_sem)
    tables.start()
    if layout.rows > layout.local:
        shape = (layout.rows - layout.local,) + buffer.shape[1:]
        buffer[layout.local :] = jnp.zeros(shape, buffer.dtype)
    basis_copy.wait()
    for group, started in enumerate(copies):
        for copy in started:
            copy.wait()
        for copy in sum(copies[group + 2 : group + 3], []):
            copy.start()
        for quad in range(PAIRS // 2):
            rows = []
            for which in range(2):
                latitude = group * PAIRS + 2 * quad + which
                rows += [buffer[latitude], buffer[latitude + layout.half]]
            grid = jnp.concatenate(rows, axis=0)
            scatter_rows(layout, dot(basis[...], grid, (1, 1)), scratch, quad, group)

    def low_block(order, carry):
        stage[order] = order_rows(layout, scratch, order, 1)
        return carry

    def pair_block(pair, carry):
        values = order_rows(layout, scratch, layout.low + 2 * pair, 2)
        stage[layout.low + pair] = dot(pair_fwd[pair], values).astype(jnp.bfloat16)
        return carry

    flushes = []

    def flush(first, last):
        at = max(at for at in range(len(outs)) if bounds[at] <= first)
        flushes.append(
            pltpu.make_async_copy(
                stage.at[pl.ds(first, last - first)],
                outs[at].at[pl.ds(first - bounds[at], last - first)],
                out_sems.at[len(flushes)],
            )
        )
        flushes[-1].start()

    middle = layout.low // 2
    for first, last in ((0, middle), (middle, layout.low)):
        lax.fori_loop(first, last, low_block, 0, unroll=8)
        flush(first, last)
    tables.wait()
    lax.fori_loop(0, layout.pairs, pair_block, 0, unroll=8)
    flush(layout.low, layout.blocks)
    for copy in flushes:
        copy.wait()


def mix(spectral, swapped, real_rows, imag_rows):
    return (spectral * real_rows + swapped * imag_rows).astype(jnp.bfloat16)


def order_groups(layout):
    for start in range(0, layout.low, GROUP):
        stop = min(start + GROUP, layout.low)
        yield start // 2, (stop + 1) // 2, start // 16 * 16


def low_kernel(layout, *refs):
    low_orders(layout, refs[: layout.parts], *refs[layout.parts :])


def low_orders(layout, held, analysis, synth_low, real_ref, imag_ref, grid_low, spec_low, swap_low):
    degrees = layout.degrees
    for start, stop, top in order_groups(layout):
        real_rows = real_ref[top:degrees, :]
        imag_rows = imag_ref[top:degrees, :]

        def low_block(two, carry):
            values = []
            for order in (2 * two, jnp.minimum(2 * two + 1, layout.low - 1)):
                values.append(jnp.concatenate([ref[order] for ref in held], axis=0))
            spectral = dot_two(analysis[two, top:degrees, :], *values).astype(jnp.bfloat16)
            for which in range(2):
                spec_low[2 * two + which, top:degrees, :] = spectral[:, which * LANES : (which + 1) * LANES]
            return carry

        def mix_block(two, carry):
            mixed = []
            for order in (2 * two, 2 * two + 1):
                spectral = spec_low[order, top:degrees, :].astype(jnp.float32)
                swapped = swap_halves(spectral)
                swap_low[order, top:degrees, :] = swapped.astype(jnp.bfloat16)
                values = mix(spectral, swapped, real_rows, imag_rows)
                if top:
                    values = jnp.concatenate([jnp.zeros((top, LANES), values.dtype), values], axis=0)
                mixed.append(values)
            values = dot_two(synth_low[two], *mixed)
            for which in range(2):
                begin = pl.multiple_of((2 * two + which) * layout.pitch, 8)
                grid_low[pl.ds(begin, layout.rows), :] = values[:, which * LANES : (which + 1) * LANES]
            return carry

        lax.fori_loop(start, stop, low_block, 0, unroll=8)
        lax.fori_loop(start, stop, mix_block, 0, unroll=8)


def spectral_kernel(layout, apart, side, *refs):
    held, lows, refs = refs[: layout.parts], refs[layout.parts : layout.parts + 2 + apart], refs[layout.parts + 2 + apart :]
    north, south, basis, back_low, pair_synth, pair_back, place, real_ref, imag_ref = refs[:9]
    keep, send, scratch, returned, spec_low, swap_low, spec_pair, swap_pair, sems = refs[9:]
    offset = 0 if apart else layout.low
    group = pl.program_id(0)
    rows, degrees, low = layout.rows, layout.degrees, layout.low
    if apart:
        sources = (lows[0].at[pl.ds(0, low * layout.pitch)], lows[1], lows[2])
        targets = (scratch.at[pl.ds(0, low * layout.pitch)], spec_low, swap_low)
        copies = [pltpu.make_async_copy(*ends, sems.at[at]) for at, ends in enumerate(zip(sources, targets))]

    @pl.when(group == 0)
    def _():
        if apart:
            for copy in copies:
                copy.start()
        else:
            low_orders(layout, held, *lows, real_ref, imag_ref, scratch, spec_low, swap_low)
        line = lax.broadcasted_iota(jnp.int32, (rows, LANES), 0)

        def pair_block(two, carry):
            mixed = []
            for pair in (2 * two, 2 * two + 1):
                total = sum(ref[offset + pair].astype(jnp.float32) for ref in held)
                spectral = total.astype(jnp.bfloat16)
                spec_pair[pair] = spectral
                natural = line >= layout.first_natural + pair
                real_rows = jnp.where(natural, real_ref[degrees : degrees + rows, :], real_ref[degrees + rows :, :])
                imag_rows = jnp.where(natural, imag_ref[degrees : degrees + rows, :], imag_ref[degrees + rows :, :])
                spectral = spectral.astype(jnp.float32)
                swapped = swap_halves(spectral)
                swap_pair[pair] = swapped.astype(jnp.bfloat16)
                mixed.append(mix(spectral, swapped, real_rows, imag_rows))
            values = dot_two(pair_synth[two], *mixed)
            for which in range(4):
                begin = pl.multiple_of((low + 4 * two + which) * layout.pitch, 8)
                columns = slice(which // 2 * LANES, (which // 2 + 1) * LANES)
                scratch[pl.ds(begin, rows), :] = values[which % 2 * rows : (which % 2 + 1) * rows, columns]
            return carry

        lax.fori_loop(0, layout.pairs // 2, pair_block, 0, unroll=8)
        used = (low + 2 * layout.pairs) * layout.pitch
        if used < layout.slots * layout.pitch:
            scratch[used : layout.slots * layout.pitch, :] = jnp.zeros(
                (layout.slots * layout.pitch - used, LANES), jnp.float32
            )
        if apart:
            copies[0].wait()

    for quad in range(PAIRS // 2):
        modes = gather_rows(layout, scratch, quad, group)
        signal = dot(modes, basis[...], (0, 0))
        incoming = grid_rows(layout, north, south, quad, group).astype(jnp.float32)
        upstream = (incoming * gelu_slope(signal)).astype(jnp.bfloat16)
        scatter_rows(layout, dot(basis[...], upstream, (1, 1)), returned, quad, group)

    @pl.when(group == pl.num_programs(0) - 1)
    def _():
        if apart:
            copies[1].wait()
            copies[2].wait()

        def products(spectral, swapped, back):
            return spectral.astype(jnp.float32) * back, swapped.astype(jnp.float32) * back

        zeros = jnp.zeros((degrees, LANES), jnp.float32)
        same, cross = zeros, zeros
        for start, stop, top in order_groups(layout):

            def low_block(two, carry):
                values = [order_rows(layout, returned, 2 * two + which, 1) for which in range(2)]
                back = dot_two(back_low[two, top:degrees, :], *values)
                for which in range(2):
                    order = 2 * two + which
                    first, second = products(
                        spec_low[order, top:degrees, :],
                        swap_low[order, top:degrees, :],
                        back[:, which * LANES : (which + 1) * LANES],
                    )
                    carry = carry[0] + first, carry[1] + second
                return carry

            part = jnp.zeros((degrees - top, LANES), jnp.float32)
            first, second = lax.fori_loop(start, stop, low_block, (part, part), unroll=8)
            if top:
                empty = jnp.zeros((top, LANES), jnp.float32)
                first = jnp.concatenate([empty, first], axis=0)
                second = jnp.concatenate([empty, second], axis=0)
            same, cross = same + first, cross + second

        line = lax.broadcasted_iota(jnp.int32, (rows, LANES), 0)

        def pair_block(two, carry):
            values = [order_rows(layout, returned, low + 4 * two + 2 * which, 2) for which in range(2)]
            back = dot_two(pair_back[two], *values)
            for which in range(2):
                pair = 2 * two + which
                first, second = products(
                    spec_pair[pair], swap_pair[pair], back[:, which * LANES : (which + 1) * LANES]
                )
                natural = line >= layout.first_natural + pair
                carry = (
                    carry[0] + jnp.where(natural, first, 0.0),
                    carry[1] + jnp.where(natural, second, 0.0),
                    carry[2] + jnp.where(natural, 0.0, first),
                    carry[3] + jnp.where(natural, 0.0, second),
                )
            return carry

        part = jnp.zeros((rows, LANES), jnp.float32)
        sums = lax.fori_loop(0, layout.pairs // 2, pair_block, (part,) * 4, unroll=16)
        placed = jnp.dot(
            place[...],
            jnp.concatenate(
                [jnp.concatenate(sums[:2], axis=1), jnp.concatenate(sums[2:], axis=1)], axis=0
            ),
            preferred_element_type=jnp.float32,
            precision=lax.Precision.HIGHEST,
        )
        same = same + placed[:, :LANES]
        cross = cross + placed[:, LANES:]
        real = same + swap_halves(same)
        imag = cross - swap_halves(cross)
        lane = lax.broadcasted_iota(jnp.int32, real.shape, 1)
        grads = jnp.where(lane < LANES // 2, real, imag).T
        upper, lower = grads[: LANES // 2], grads[LANES // 2 :]
        keep[...] = jnp.where(side[0] == 0, upper, lower)
        send[...] = jnp.where(side[0] == 0, lower, upper)


def grid_specs(layout, chunk):
    last = -(-layout.local // PAIRS) - 1
    shift = layout.half // PAIRS
    block = (1, PAIRS, LANES // 2, NLON)
    return [
        pl.BlockSpec(block, lambda g: (0, jnp.minimum(g, last), chunk, 0)),
        pl.BlockSpec(block, lambda g: (0, jnp.minimum(shift + g, last), chunk, 0)),
    ]


def whole():
    return pl.BlockSpec(memory_space=pltpu.VMEM)


def forward_call(layout, chunk, bounds, index, fields, pair_fwd):
    basis = jnp.asarray(fourier_constants(layout)[0])
    slots = basis.shape[0] // 2
    groups = layout.half // PAIRS
    anywhere = pl.BlockSpec(memory_space=pl.ANY)
    counts = [last - first for first, last in zip(bounds, bounds[1:])]
    return pl.pallas_call(
        functools.partial(forward_kernel, layout, chunk, bounds),
        in_specs=[pl.BlockSpec(memory_space=pltpu.SMEM)] + [anywhere] * 3,
        out_specs=[anywhere] * len(counts),
        out_shape=[jax.ShapeDtypeStruct((count, layout.rows, LANES), jnp.bfloat16) for count in counts],
        scratch_shapes=[
            pltpu.VMEM((slots * layout.pitch, LANES), jnp.float32),
            pltpu.VMEM((layout.rows, LANES // 2, NLON), jnp.bfloat16),
            pltpu.VMEM(basis.shape, jnp.bfloat16),
            pltpu.VMEM((layout.blocks, layout.rows, LANES), jnp.bfloat16),
            pltpu.VMEM(pair_fwd.shape[1:], jnp.bfloat16),
            pltpu.SemaphoreType.DMA((2 * groups,)),
            pltpu.SemaphoreType.DMA,
            pltpu.SemaphoreType.DMA,
            pltpu.SemaphoreType.DMA((3,)),
        ],
        compiler_params=pltpu.CompilerParams(vmem_limit_bytes=FORWARD_VMEM),
        cost_estimate=pl.CostEstimate(flops=1_000_000, bytes_accessed=100_000, transcendentals=0),
        name=f"forward_{chunk}",
    )(index, fields, basis, pair_fwd)


def low_call(layout, chunk, coeffs, tables, real_rows, imag_rows):
    operands = list(coeffs) + list(tables) + [real_rows, imag_rows]
    spectra = jax.ShapeDtypeStruct((2 * layout.twos, layout.degrees, LANES), jnp.bfloat16)
    return pl.pallas_call(
        functools.partial(low_kernel, layout),
        in_specs=[whole()] * len(operands),
        out_specs=[whole()] * 3,
        out_shape=[jax.ShapeDtypeStruct((2 * layout.twos * layout.pitch, LANES), jnp.float32), spectra, spectra],
        compiler_params=pltpu.CompilerParams(vmem_limit_bytes=VMEM),
        cost_estimate=pl.CostEstimate(flops=8_000_000_000, bytes_accessed=30_000_000, transcendentals=0),
        name=f"low_{chunk}",
    )(*operands)


def spectral_call(layout, chunk, apart, side, blocks, lows, cotangent, tables, real_rows, imag_rows):
    half = jax.ShapeDtypeStruct((LANES // 2, layout.degrees), jnp.float32)
    operands = [side] + list(blocks) + list(lows) + [cotangent, cotangent] + list(tables) + [real_rows, imag_rows]
    low_spec = pl.BlockSpec(memory_space=pl.ANY) if apart else whole()
    specs = [pl.BlockSpec(memory_space=pltpu.SMEM)] + [whole()] * len(blocks) + [low_spec] * len(lows)
    specs += grid_specs(layout, chunk) + [whole()] * (len(tables) + 2)
    return pl.pallas_call(
        functools.partial(spectral_kernel, layout, apart),
        grid=(layout.half // PAIRS,),
        in_specs=specs,
        out_specs=[whole()] * 2,
        out_shape=[half, half],
        scratch_shapes=[
            pltpu.VMEM((layout.slots * layout.pitch, LANES), jnp.float32),
            pltpu.VMEM((layout.slots * layout.pitch, LANES), jnp.float32),
            pltpu.VMEM((2 * layout.twos, layout.degrees, LANES), jnp.bfloat16),
            pltpu.VMEM((2 * layout.twos, layout.degrees, LANES), jnp.bfloat16),
            pltpu.VMEM((layout.pairs, layout.rows, LANES), jnp.bfloat16),
            pltpu.VMEM((layout.pairs, layout.rows, LANES), jnp.bfloat16),
            pltpu.SemaphoreType.DMA((3,)),
        ],
        compiler_params=pltpu.CompilerParams(vmem_limit_bytes=VMEM),
        cost_estimate=pl.CostEstimate(flops=8_000_000_000, bytes_accessed=30_000_000, transcendentals=0),
        name=f"spectral_{chunk}",
    )(*operands)


def radices(size):
    found, factor = [], 2
    while size > 1:
        while size % factor == 0:
            found.append(factor)
            size //= factor
        factor += 1
    return found


def sum_steps(axis):
    size = lax.axis_size(axis)
    steps, stride = [], 1
    for radix in radices(size):
        steps.append((axis, stride, radix))
        stride *= radix
    return steps


def hop_parcels(value, step):
    axis, stride, radix = step
    parcels = []
    for turn in range(1, radix):
        pairs = []
        for index in range(lax.axis_size(axis)):
            digit = index // stride % radix
            pairs.append((index, index + ((digit + turn) % radix - digit) * stride))
        parcels.append(lax.ppermute(value, axis, pairs))
    return parcels


def filter_rows(layout, spec):
    padded = jnp.pad(spec, ((0, layout.degrees - MODES), (0, 0)))
    front = jnp.pad(spec, ((layout.rows, layout.rows), (0, 0)))
    natural = front[MODES : MODES + layout.rows]
    backward = front[layout.rows + MODES - layout.rows : layout.rows + MODES][::-1]
    return jnp.concatenate([padded, natural, backward], axis=0).astype(jnp.float32)


def on_device(fields, cotangent, spec_real, spec_imag):
    parts = lax.axis_size("space")
    index = lax.axis_index("space")
    layout = Layout(parts, fields.shape[1])
    width = LANES // 2
    chunks = fields.shape[-1] // width
    inverse = jnp.asarray(fourier_constants(layout)[1])
    constants = legendre_constants(parts, layout.local)

    def local_table(name):
        return lax.dynamic_index_in_dim(jnp.asarray(constants[name]), index, keepdims=False)

    pair_fwd = jnp.asarray(constants["pair_fwd"])
    place = jnp.reshape(index, (1,)).astype(jnp.int32)
    def bands(name, first, count):
        table = jnp.asarray(constants[name])
        return lax.optimization_barrier(
            lax.dynamic_slice_in_dim(table, first * layout.rows, count * layout.rows, 1)
        )

    def side_by_side(table):
        return jnp.concatenate([table[::2], table[1::2]], axis=2)

    synth_own = bands("synth_low", index, 1)
    analysis = bands("analysis", parts - 1 - index, parts).reshape(layout.twos, -1, layout.degrees)
    analysis = jnp.swapaxes(analysis, 1, 2)
    back_low = jnp.swapaxes(synth_own.reshape(layout.twos, -1, layout.degrees), 1, 2)
    synth_low = side_by_side(synth_own)
    pair_tables = [local_table(name) for name in ("pair_synth", "pair_back")]
    low_tables = [analysis, synth_low]
    tables = [inverse, back_low] + pair_tables + [jnp.asarray(constants["place"])]
    fields, cotangent = jnp.swapaxes(fields, 2, 3), jnp.swapaxes(cotangent, 2, 3)
    real_all = filter_rows(layout, spec_real)
    imag_all = filter_rows(layout, spec_imag)

    def others(sent):
        routes = [[(source, (source + shift) % parts) for source in range(parts)] for shift in range(1, parts)]
        return [lax.ppermute(sent, "space", route) for route in routes]

    held = []
    for chunk in range(chunks):
        if chunk == 1:
            place, low_tables, tables = lax.optimization_barrier((place, low_tables, tables))
        bounds = (0, layout.blocks) if chunk < chunks - 1 else (0, layout.low, layout.blocks)
        made = forward_call(layout, chunk, bounds, place, fields, pair_fwd)
        place, made = lax.optimization_barrier((place, list(made)))
        if len(made) > 1 and held:
            made[1], held[0][1] = lax.optimization_barrier((made[1], held[0][1]))
        held += [[own] + others(own) for own in made]

    hops = sum_steps("dp") + sum_steps("space")
    count_dp = len(sum_steps("dp"))
    swap = [(device, device ^ 1) for device in range(lax.axis_size("dp"))]
    side = lax.rem(lax.axis_index("dp"), 2).reshape((1,)).astype(jnp.int32)
    waiting = []

    def launch(value, done):
        if done:
            return value, hop_parcels(value, hops[done])
        keep, send = value
        return keep, [lax.ppermute(send, "dp", swap)]

    def hop_all(limit, tie):
        moved = []
        for value, done in waiting:
            if done < limit:
                value, parcels = launch(value, done)
                parcels, value, tie = lax.optimization_barrier((parcels, value, tie))
                value, done = sum(parcels, value), done + 1
            moved.append((value, done))
        waiting[:] = moved
        return tie

    def hop_last(times):
        for _ in range(times):
            value, done = waiting[-1]
            value, parcels = launch(value, done)
            waiting[-1] = (sum(parcels, value), done + 1)

    def before(values):
        if not waiting:
            return values
        values, sums = lax.optimization_barrier((values, [value for value, _ in waiting]))
        waiting[:] = [(value, done) for value, (_, done) in zip(sums, waiting)]
        return values

    for chunk in range(chunks):
        columns = slice(chunk * width, (chunk + 1) * width)
        real, imag = real_all[:, columns], imag_all[:, columns]
        real_rows = jnp.concatenate([real, real], axis=1)
        imag_rows = jnp.concatenate([-imag, imag], axis=1)
        blocks, lows, apart = held[chunk], low_tables, chunk == chunks - 1
        if apart:
            lows = low_call(layout, chunk, blocks, low_tables, real_rows, imag_rows)
            lows = before(hop_all(count_dp, lows))
            blocks = held[-1]
        grads = spectral_call(layout, chunk, apart, side, blocks, lows, cotangent, tables, real_rows, imag_rows)
        grads = hop_all(len(hops) if apart else count_dp, grads)
        waiting.append((grads, 0))
        if chunk < chunks - 2:
            hop_last(count_dp // 2)
            held[chunk + 1] = before(held[chunk + 1])

    hop_last(1)
    total, done = waiting.pop()
    while done < len(hops):
        joined = [value for value, at in waiting if at == done]
        waiting = [(value, at) for value, at in waiting if at != done]
        if joined:
            total = jnp.concatenate(joined + [total], axis=0)
        total, done = sum(hop_parcels(total, hops[done]), total), done + 1
    mine = jnp.concatenate([value for value, _ in waiting] + [total], axis=0)
    other = lax.ppermute(mine, "dp", swap)
    real = jnp.where(side[0] == 0, mine, other)[:, :MODES]
    imag = jnp.where(side[0] == 0, other, mine)[:, :MODES]
    batch_total = fields.shape[0] * lax.axis_size("dp")
    return (real.T / batch_total, imag.T / batch_total)


def solution(mesh):
    in_specs = (P("dp", "space", None, None), P("dp", "space", None, None), P(), P())
    out_specs = (P(), P())
    return jax.shard_map(
        on_device, mesh=mesh, in_specs=in_specs, out_specs=out_specs, check_vma=False
    )
```

```python
import functools
import math

import jax
import jax.numpy as jnp
import ml_dtypes
import numpy as np
from jax import lax
from jax.experimental import pallas as pl
from jax.experimental.pallas import tpu as pltpu
from jax.sharding import PartitionSpec as P

NLAT = 126
NLON = 252
MODES = 126
LANES = 128
GROUP = 16
PAIRS = 8
MOVED = 3
TAIL = 8
VMEM = 30 * 1024 * 1024
FORWARD_VMEM = 56 * 1024 * 1024


def round_up(value, step):
    return -(-value // step) * step


@functools.lru_cache(maxsize=None)
def legendre_table():
    single = np.float32
    colatitude = single(math.pi) * (np.arange(NLAT, dtype=single) + single(0.5)) / single(NLAT)
    cos_theta, sin_theta = np.cos(colatitude), np.sin(colatitude)
    counters = np.arange(1, MODES, dtype=single)
    log_steps = single(0.5) * np.log((2 * counters + 1) / (2 * counters))
    log_table = np.concatenate([np.zeros(1, single), np.cumsum(log_steps, dtype=single)])
    order = np.arange(MODES, dtype=single)[:, None]
    start = single(0.5 * math.log(1.0 / (4.0 * math.pi)))
    diagonal = np.exp(start + log_table[:, None] + order * np.log(sin_theta)[None])
    previous = earlier = np.zeros_like(diagonal)
    table = np.zeros((MODES, MODES, NLAT), single)
    for at in range(MODES):
        degree, below = single(at), single(at - 1)
        growth = np.sqrt(
            np.maximum(4 * degree * degree - 1, single(0)) / np.maximum(degree * degree - order * order, single(1))
        )
        damping = np.sqrt(
            np.maximum(below * below - order * order, single(0)) / np.maximum(4 * below * below - 1, single(1))
        )
        current = growth * (cos_theta[None] * previous - damping * earlier)
        current = np.where(order == degree, diagonal, np.where(order < degree, current, single(0)))
        table[:, at] = current
        previous, earlier = current, previous
    weight = single(math.pi / NLAT * (2.0 * math.pi / NLON)) * sin_theta
    return table, table * weight


def to_bf16(array):
    return np.where(np.abs(array) < 2.0**-126, 0.0, array).astype(ml_dtypes.bfloat16)


class Layout:
    def __init__(self, parts, local):
        self.parts, self.local = parts, local
        self.rows = round_up(local + 1, 16)
        self.half = self.rows // 2
        self.base = round_up(max(self.rows - local, 1), 8)
        self.pitch = self.rows + self.base
        self.low = max(MODES - local, 0)
        high = MODES - self.low
        self.pairs = round_up((high + 1) // 2, 2)
        self.twos = round_up(self.low, 2) // 2
        self.sent, self.runs = self.low, []
        self.carry()
        self.blocks = self.sent + self.pairs
        self.slots = round_up(self.low + 2 * self.pairs, 8)
        self.degrees = round_up(MODES, 16)
        self.first_natural = self.rows - MODES + self.low
        self.partner = MODES - 1 + self.low
        orders = list(range(self.low))
        for pair in range(self.pairs):
            order, mate = self.low + pair, self.partner - self.low - pair
            orders += [order if order <= mate else -1, mate if order < mate else -1]
        self.orders = np.array(orders + [-1] * (self.slots - len(orders)))

    def band(self, part):
        latitudes = np.arange(part * self.local, (part + 1) * self.local)
        return latitudes[::-1] if 2 * part < self.parts else latitudes

    def carry(self):
        plain = to_bf16(legendre_table()[0]).astype(np.float32)
        live = np.zeros(self.low, int)
        for part in range(self.parts):
            used = np.abs(plain[: self.low][:, :, self.band(part)]).max(axis=1) > 0
            for order in range(self.low):
                live[order] = max(live[order], *(1 + np.flatnonzero(used[order])), 1)
        sent = self.low - MOVED
        places = []
        for row in range(self.rows - 1, self.rows - TAIL - 1, -1):
            free = live[: max(sent, 0)] <= row
            first = int(np.flatnonzero(~free)[-1]) + 1 if (~free).any() else 0
            if first < sent:
                places.append((row, first, sent - first))
        runs = []
        for which in range(MOVED):
            done = 0
            while sent > 0 and done < live[sent + which] and places:
                row, first, count = places.pop(0)
                taken = min(count, live[sent + which] - done)
                runs.append((which, int(done), row, first, int(taken)))
                done += taken
                if taken < count:
                    places.insert(0, (row, int(first + taken), int(count - taken)))
            if sent <= 0 or done < live[sent + which]:
                return
        self.sent, self.runs = sent, runs


def fourier_constants(layout):
    orders = np.maximum(layout.orders, 0)
    angles = 2.0 * math.pi / NLON * (orders[:, None] * np.arange(NLON)[None] % NLON)
    live = (layout.orders >= 0)[:, None]
    basis = np.concatenate([np.cos(angles) * live, -np.sin(angles) * live])
    factor = np.where(layout.orders == 0, 1.0, 2.0)[:, None]
    inverse = basis * np.concatenate([factor, factor])
    return to_bf16(basis), to_bf16(inverse)


@functools.lru_cache(maxsize=None)
def legendre_constants(parts, local):
    layout = Layout(parts, local)
    plain, weighted = legendre_table()
    rows, degrees, low, pairs = layout.rows, layout.degrees, layout.low, layout.pairs
    analysis = np.zeros((2 * layout.twos, 2 * parts * rows, degrees))
    synth_low = np.zeros((2 * layout.twos, parts * rows, degrees))
    pair_fwd = np.zeros((parts, pairs, rows, 2 * rows))
    pair_back = np.zeros((parts, pairs, rows, 2 * rows))
    for part in range(parts):
        own = layout.band(part)
        start = part * rows
        synth_low[:low, start : start + local, :MODES] = np.swapaxes(plain[:low, :, own], 1, 2)
        for turn in (1, 2):
            start = (turn * parts - 1 - part) * rows
            analysis[:low, start : start + local, :MODES] = np.swapaxes(weighted[:low, :, own], 1, 2)
        for pair in range(pairs):
            order = low + pair
            mate = layout.partner - order
            for target, table in ((pair_fwd, weighted), (pair_back, plain)):
                if order <= mate:
                    count = MODES - order
                    target[part, pair, rows - count :, :local] = table[order][order:, own]
                if order < mate:
                    count = MODES - mate
                    target[part, pair, :count, rows : rows + local] = table[mate][mate:, own][::-1]
    pair_synth = np.swapaxes(pair_back, -1, -2)
    place = np.zeros((degrees, 2 * rows))
    for row in range(rows):
        if row >= rows - MODES + low:
            place[MODES - rows + row, row] = 1.0
        if MODES - 1 - row >= 0:
            place[MODES - 1 - row, rows + row] = 1.0
    return {
        "analysis": to_bf16(analysis),
        "synth_low": to_bf16(synth_low),
        "pair_fwd": to_bf16(pair_fwd),
        "pair_back": to_bf16(np.concatenate([pair_back[:, ::2], pair_back[:, 1::2]], axis=3)),
        "pair_synth": to_bf16(np.concatenate([pair_synth[:, ::2], pair_synth[:, 1::2]], axis=3)),
        "place": place.astype(np.float32),
    }


def dot(left, right, sides=(1, 0)):
    contract = (((sides[0],), (sides[1],)), ((), ()))
    return lax.dot_general(left, right, contract, preferred_element_type=jnp.float32)


def dot_two(left, first, second):
    upper = jnp.concatenate([first, jnp.zeros_like(first)], axis=1)
    lower = jnp.concatenate([jnp.zeros_like(second), second], axis=1)
    return dot(left, jnp.concatenate([upper, lower], axis=0))


def swap_halves(values):
    return pltpu.roll(values, LANES // 2, 1)


def interleave(first, second):
    lane = lax.broadcasted_iota(jnp.int32, first.shape, 1)
    below = lane < LANES // 2
    return (
        jnp.where(below, first, swap_halves(second)),
        jnp.where(below, swap_halves(first), second),
    )


def gelu_slope(values):
    cumulative = 0.5 * (1.0 + lax.erf(values / math.sqrt(2.0)))
    density = jnp.exp(-0.5 * values * values) / math.sqrt(2.0 * math.pi)
    return cumulative + values * density


def grid_rows(layout, north, south, quad, group):
    rows = []
    for pair in (2 * quad, 2 * quad + 1):
        rows.append(north[0, pair])
        values = south[0, pair]
        if layout.rows > layout.local:
            latitude = layout.half + group * PAIRS + pair
            values = jnp.where(latitude < layout.local, values, jnp.zeros_like(values))
        rows.append(values)
    return jnp.concatenate(rows, axis=0)


def row_of(layout, turned, group, place):
    latitude = group * PAIRS + place
    row = layout.local - 1 - latitude
    if not isinstance(turned, bool):
        row = jnp.where(turned, row, latitude) if latitude < layout.local else latitude
    elif not turned:
        row = latitude
    return layout.base + row


def scatter_rows(layout, turned, values, scratch, quad, group):
    slots = values.shape[0] // 2
    for which in range(2):
        columns = slice(which * LANES, (which + 1) * LANES)
        upper, lower = interleave(values[:slots, columns], values[slots:, columns])
        place = 2 * quad + which
        scratch[pl.ds(row_of(layout, turned, group, place), slots, stride=layout.pitch), :] = upper
        scratch[pl.ds(row_of(layout, turned, group, place + layout.half), slots, stride=layout.pitch), :] = lower


def gather_rows(layout, turned, scratch, quad, group):
    slots = layout.slots
    cosine, sine = [], []
    for which in range(2):
        place = 2 * quad + which
        upper = scratch[pl.ds(row_of(layout, turned, group, place), slots, stride=layout.pitch), :]
        lower = scratch[pl.ds(row_of(layout, turned, group, place + layout.half), slots, stride=layout.pitch), :]
        first, second = interleave(upper, lower)
        cosine.append(first.astype(jnp.bfloat16))
        sine.append(second.astype(jnp.bfloat16))
    return jnp.concatenate(
        [jnp.concatenate(cosine, axis=1), jnp.concatenate(sine, axis=1)], axis=0
    )


def order_rows(layout, scratch, first, count):
    parts = []
    for order in range(count):
        start = pl.multiple_of((first + order) * layout.pitch + layout.base, 8)
        parts.append(scratch[pl.ds(start, layout.rows), :])
    return jnp.concatenate(parts, axis=0).astype(jnp.bfloat16)


def band_copies(layout, chunk, fields, buffer, sems):
    width = LANES // 2
    copies = []
    for group in range(layout.half // PAIRS):
        started = []
        for side in range(2):
            first = side * layout.half + group * PAIRS
            count = min(PAIRS, layout.local - first)
            if count > 0:
                started.append(
                    pltpu.make_async_copy(
                        fields.at[0, pl.ds(first, count), pl.ds(chunk * width, width), :],
                        buffer.at[pl.ds(first, count)],
                        sems.at[2 * group + side],
                    )
                )
        copies.append(started)
    return copies


def forward_kernel(layout, chunk, bounds, index, fields, basis_all, pair_all, *refs):
    outs, refs = refs[: len(bounds) - 1], refs[len(bounds) - 1 :]
    scratch, buffer, basis, stage, pair_fwd, sems, basis_sem, pair_sem, out_sems = refs
    basis_copy = pltpu.make_async_copy(basis_all, basis, basis_sem)
    basis_copy.start()
    copies = band_copies(layout, chunk, fields, buffer, sems)
    for started in copies[:2]:
        for copy in started:
            copy.start()
    tables = pltpu.make_async_copy(pair_all.at[index[0]], pair_fwd, pair_sem)
    tables.start()
    if layout.rows > layout.local:
        shape = (layout.rows - layout.local,) + buffer.shape[1:]
        buffer[layout.local :] = jnp.zeros(shape, buffer.dtype)
    basis_copy.wait()
    turned = 2 * index[0] < layout.parts
    for group, started in enumerate(copies):
        for copy in started:
            copy.wait()
        for copy in sum(copies[group + 2 : group + 3], []):
            copy.start()
        for quad in range(PAIRS // 2):
            rows = []
            for which in range(2):
                latitude = group * PAIRS + 2 * quad + which
                rows += [buffer[latitude], buffer[latitude + layout.half]]
            grid = jnp.concatenate(rows, axis=0)
            scatter_rows(layout, turned, dot(basis[...], grid, (1, 1)), scratch, quad, group)

    def low_block(order, carry):
        stage[order] = order_rows(layout, scratch, order, 1)
        return carry

    def pair_block(pair, carry):
        values = order_rows(layout, scratch, layout.low + 2 * pair, 2)
        stage[layout.sent + pair] = dot(pair_fwd[pair], values).astype(jnp.bfloat16)
        return carry

    flushes = []

    def flush(first, last):
        at = max(at for at in range(len(outs)) if bounds[at] <= first)
        flushes.append(
            pltpu.make_async_copy(
                stage.at[pl.ds(first, last - first)],
                outs[at].at[pl.ds(first - bounds[at], last - first)],
                out_sems.at[len(flushes)],
            )
        )
        flushes[-1].start()

    for which, start, row, first, count in layout.runs:
        moved = scratch[pl.ds((layout.sent + which) * layout.pitch + layout.base + start, count), :]
        scratch[pl.ds(first * layout.pitch + layout.base + row, count, stride=layout.pitch), :] = moved
    middle = layout.sent // 2
    for first, last in ((0, middle), (middle, layout.sent)):
        lax.fori_loop(first, last, low_block, 0, unroll=8)
        flush(first, last)
    tables.wait()
    lax.fori_loop(0, layout.pairs, pair_block, 0, unroll=8)
    flush(layout.sent, layout.blocks)
    for copy in flushes:
        copy.wait()


def mix(spectral, swapped, real_rows, imag_rows):
    return (spectral * real_rows + swapped * imag_rows).astype(jnp.bfloat16)


def order_groups(layout):
    for start in range(0, layout.low, GROUP):
        stop = min(start + GROUP, layout.low)
        yield start // 2, (stop + 1) // 2, start // 16 * 16


def low_kernel(layout, *refs):
    low_orders(layout, refs[: layout.parts], *refs[layout.parts :])


def low_orders(
    layout, held, analysis, synth_low, real_ref, imag_ref, grid_low, spec_low, swap_low, tails, moved
):
    degrees, rows = layout.degrees, layout.rows
    if layout.runs:
        moved[...] = jnp.zeros_like(moved)
    for at, ref in enumerate(held):
        if layout.runs:

            def tail_block(order, carry):
                values = ref[order, rows - 16 :, :].astype(jnp.float32)
                tails[pl.ds(pl.multiple_of(order * TAIL, TAIL), TAIL), :] = values[16 - TAIL :]
                return carry

            lax.fori_loop(0, layout.sent, tail_block, 0, unroll=10)
        for which, start, row, first, count in layout.runs:
            begin = (at * MOVED + which) * rows + start
            source = pl.ds(first * TAIL + row - (rows - TAIL), count, stride=TAIL)
            moved[pl.ds(begin, count), :] = tails[source, :]

    def coefficients(order):
        if isinstance(order, int) and order >= layout.sent:
            which = min(order, layout.low - 1) - layout.sent
            starts = [(at * MOVED + which) * rows for at in range(layout.parts)]
            return jnp.concatenate([moved[start : start + rows, :] for start in starts], axis=0).astype(jnp.bfloat16)
        return jnp.concatenate([ref[order] for ref in held], axis=0)

    for start, stop, top in order_groups(layout):
        real_rows = real_ref[top:degrees, :]
        imag_rows = imag_ref[top:degrees, :]

        def low_block(two, carry):
            last = layout.low - 1
            second = min(2 * two + 1, last) if isinstance(two, int) else jnp.minimum(2 * two + 1, last)
            values = [coefficients(2 * two), coefficients(second)]
            spectral = dot_two(analysis[two, top:degrees, :], *values).astype(jnp.bfloat16)
            for which in range(2):
                spec_low[2 * two + which, top:degrees, :] = spectral[:, which * LANES : (which + 1) * LANES]
            return carry

        def mix_block(two, carry):
            mixed = []
            for order in (2 * two, 2 * two + 1):
                spectral = spec_low[order, top:degrees, :].astype(jnp.float32)
                swapped = swap_halves(spectral)
                swap_low[order, top:degrees, :] = swapped.astype(jnp.bfloat16)
                values = mix(spectral, swapped, real_rows, imag_rows)
                if top:
                    values = jnp.concatenate([jnp.zeros((top, LANES), values.dtype), values], axis=0)
                mixed.append(values)
            values = dot_two(synth_low[two], *mixed)
            for which in range(2):
                begin = pl.multiple_of((2 * two + which) * layout.pitch + layout.base, 8)
                grid_low[pl.ds(begin, layout.rows), :] = values[:, which * LANES : (which + 1) * LANES]
            return carry

        whole_twos = max(min(stop, layout.sent // 2 if layout.runs else stop), start)
        lax.fori_loop(start, whole_twos, low_block, 0, unroll=8)
        for two in range(whole_twos, stop):
            low_block(two, 0)
        lax.fori_loop(start, stop, mix_block, 0, unroll=8)


def spectral_kernel(layout, apart, side, *refs):
    held, lows, refs = refs[: layout.parts], refs[layout.parts : layout.parts + 2 + apart], refs[layout.parts + 2 + apart :]
    north, south, basis, back_low, pair_synth, pair_back, place, real_ref, imag_ref = refs[:9]
    keep, send, scratch, returned, spec_low, swap_low, spec_pair, swap_pair, tails, moved, sems = refs[9:]
    offset = 0 if apart else layout.sent
    group = pl.program_id(0)
    rows, degrees, low = layout.rows, layout.degrees, layout.low
    if apart:
        sources = (lows[0].at[pl.ds(0, low * layout.pitch)], lows[1], lows[2])
        targets = (scratch.at[pl.ds(0, low * layout.pitch)], spec_low, swap_low)
        copies = [pltpu.make_async_copy(*ends, sems.at[at]) for at, ends in enumerate(zip(sources, targets))]

    @pl.when(group == 0)
    def _():
        if apart:
            for copy in copies:
                copy.start()
        else:
            low_orders(layout, held, *lows, real_ref, imag_ref, scratch, spec_low, swap_low, tails, moved)
        line = lax.broadcasted_iota(jnp.int32, (rows, LANES), 0)

        def pair_block(two, carry):
            mixed = []
            for pair in (2 * two, 2 * two + 1):
                total = sum(ref[offset + pair].astype(jnp.float32) for ref in held)
                spectral = total.astype(jnp.bfloat16)
                spec_pair[pair] = spectral
                natural = line >= layout.first_natural + pair
                real_rows = jnp.where(natural, real_ref[degrees : degrees + rows, :], real_ref[degrees + rows :, :])
                imag_rows = jnp.where(natural, imag_ref[degrees : degrees + rows, :], imag_ref[degrees + rows :, :])
                spectral = spectral.astype(jnp.float32)
                swapped = swap_halves(spectral)
                swap_pair[pair] = swapped.astype(jnp.bfloat16)
                mixed.append(mix(spectral, swapped, real_rows, imag_rows))
            values = dot_two(pair_synth[two], *mixed)
            for which in range(4):
                begin = pl.multiple_of((low + 4 * two + which) * layout.pitch + layout.base, 8)
                columns = slice(which // 2 * LANES, (which // 2 + 1) * LANES)
                scratch[pl.ds(begin, rows), :] = values[which % 2 * rows : (which % 2 + 1) * rows, columns]
            return carry

        lax.fori_loop(0, layout.pairs // 2, pair_block, 0, unroll=8)
        used = (low + 2 * layout.pairs) * layout.pitch
        if used < layout.slots * layout.pitch:
            scratch[used : layout.slots * layout.pitch, :] = jnp.zeros(
                (layout.slots * layout.pitch - used, LANES), jnp.float32
            )
        for row in range(layout.base + layout.local, layout.pitch):
            returned[pl.ds(row, layout.slots, stride=layout.pitch), :] = jnp.zeros((layout.slots, LANES), jnp.float32)
        if apart:
            copies[0].wait()

    def grid_step(turned):
        for quad in range(PAIRS // 2):
            modes = gather_rows(layout, turned, scratch, quad, group)
            signal = dot(modes, basis[...], (0, 0))
            incoming = grid_rows(layout, north, south, quad, group).astype(jnp.float32)
            upstream = (incoming * gelu_slope(signal)).astype(jnp.bfloat16)
            scatter_rows(layout, turned, dot(basis[...], upstream, (1, 1)), returned, quad, group)

    pl.when(2 * side[1] < layout.parts)(functools.partial(grid_step, True))
    pl.when(2 * side[1] >= layout.parts)(functools.partial(grid_step, False))

    @pl.when(group == pl.num_programs(0) - 1)
    def _():
        if apart:
            copies[1].wait()
            copies[2].wait()

        def products(spectral, swapped, back):
            return spectral.astype(jnp.float32) * back, swapped.astype(jnp.float32) * back

        zeros = jnp.zeros((degrees, LANES), jnp.float32)
        same, cross = zeros, zeros
        for start, stop, top in order_groups(layout):

            def low_block(two, carry):
                values = [order_rows(layout, returned, 2 * two + which, 1) for which in range(2)]
                back = dot_two(back_low[two, top:degrees, :], *values)
                for which in range(2):
                    order = 2 * two + which
                    first, second = products(
                        spec_low[order, top:degrees, :],
                        swap_low[order, top:degrees, :],
                        back[:, which * LANES : (which + 1) * LANES],
                    )
                    carry = carry[0] + first, carry[1] + second
                return carry

            part = jnp.zeros((degrees - top, LANES), jnp.float32)
            first, second = lax.fori_loop(start, stop, low_block, (part, part), unroll=8)
            if top:
                empty = jnp.zeros((top, LANES), jnp.float32)
                first = jnp.concatenate([empty, first], axis=0)
                second = jnp.concatenate([empty, second], axis=0)
            same, cross = same + first, cross + second

        line = lax.broadcasted_iota(jnp.int32, (rows, LANES), 0)

        def pair_block(two, carry):
            values = [order_rows(layout, returned, low + 4 * two + 2 * which, 2) for which in range(2)]
            back = dot_two(pair_back[two], *values)
            for which in range(2):
                pair = 2 * two + which
                first, second = products(
                    spec_pair[pair], swap_pair[pair], back[:, which * LANES : (which + 1) * LANES]
                )
                natural = line >= layout.first_natural + pair
                carry = (
                    carry[0] + jnp.where(natural, first, 0.0),
                    carry[1] + jnp.where(natural, second, 0.0),
                    carry[2] + jnp.where(natural, 0.0, first),
                    carry[3] + jnp.where(natural, 0.0, second),
                )
            return carry

        part = jnp.zeros((rows, LANES), jnp.float32)
        sums = lax.fori_loop(0, layout.pairs // 2, pair_block, (part,) * 4, unroll=16)
        placed = jnp.dot(
            place[...],
            jnp.concatenate(
                [jnp.concatenate(sums[:2], axis=1), jnp.concatenate(sums[2:], axis=1)], axis=0
            ),
            preferred_element_type=jnp.float32,
            precision=lax.Precision.HIGHEST,
        )
        same = same + placed[:, :LANES]
        cross = cross + placed[:, LANES:]
        real = same + swap_halves(same)
        imag = cross - swap_halves(cross)
        lane = lax.broadcasted_iota(jnp.int32, real.shape, 1)
        grads = jnp.where(lane < LANES // 2, real, imag).T
        upper, lower = grads[: LANES // 2], grads[LANES // 2 :]
        keep[...] = jnp.where(side[0] == 0, upper, lower)
        send[...] = jnp.where(side[0] == 0, lower, upper)


def grid_specs(layout, chunk):
    last = -(-layout.local // PAIRS) - 1
    shift = layout.half // PAIRS
    block = (1, PAIRS, LANES // 2, NLON)
    return [
        pl.BlockSpec(block, lambda g: (0, jnp.minimum(g, last), chunk, 0)),
        pl.BlockSpec(block, lambda g: (0, jnp.minimum(shift + g, last), chunk, 0)),
    ]


def whole():
    return pl.BlockSpec(memory_space=pltpu.VMEM)


def forward_call(layout, chunk, bounds, index, fields, pair_fwd):
    basis = jnp.asarray(fourier_constants(layout)[0])
    slots = basis.shape[0] // 2
    groups = layout.half // PAIRS
    anywhere = pl.BlockSpec(memory_space=pl.ANY)
    counts = [last - first for first, last in zip(bounds, bounds[1:])]
    return pl.pallas_call(
        functools.partial(forward_kernel, layout, chunk, bounds),
        in_specs=[pl.BlockSpec(memory_space=pltpu.SMEM)] + [anywhere] * 3,
        out_specs=[anywhere] * len(counts),
        out_shape=[jax.ShapeDtypeStruct((count, layout.rows, LANES), jnp.bfloat16) for count in counts],
        scratch_shapes=[
            pltpu.VMEM((slots * layout.pitch, LANES), jnp.float32),
            pltpu.VMEM((layout.rows, LANES // 2, NLON), jnp.bfloat16),
            pltpu.VMEM(basis.shape, jnp.bfloat16),
            pltpu.VMEM((layout.blocks, layout.rows, LANES), jnp.bfloat16),
            pltpu.VMEM(pair_fwd.shape[1:], jnp.bfloat16),
            pltpu.SemaphoreType.DMA((2 * groups,)),
            pltpu.SemaphoreType.DMA,
            pltpu.SemaphoreType.DMA,
            pltpu.SemaphoreType.DMA((3,)),
        ],
        compiler_params=pltpu.CompilerParams(vmem_limit_bytes=FORWARD_VMEM),
        cost_estimate=pl.CostEstimate(flops=1_000_000, bytes_accessed=100_000, transcendentals=0),
        name=f"forward_{chunk}",
    )(index, fields, basis, pair_fwd)


def low_call(layout, chunk, coeffs, tables, real_rows, imag_rows):
    operands = list(coeffs) + list(tables) + [real_rows, imag_rows]
    spectra = jax.ShapeDtypeStruct((2 * layout.twos, layout.degrees, LANES), jnp.bfloat16)
    return pl.pallas_call(
        functools.partial(low_kernel, layout),
        in_specs=[whole()] * len(operands),
        out_specs=[whole()] * 3,
        out_shape=[jax.ShapeDtypeStruct((2 * layout.twos * layout.pitch, LANES), jnp.float32), spectra, spectra],
        scratch_shapes=[
            pltpu.VMEM((layout.sent * TAIL, LANES), jnp.float32),
            pltpu.VMEM((layout.parts * MOVED * layout.rows, LANES), jnp.float32),
        ],
        compiler_params=pltpu.CompilerParams(vmem_limit_bytes=VMEM),
        cost_estimate=pl.CostEstimate(flops=8_000_000_000, bytes_accessed=30_000_000, transcendentals=0),
        name=f"low_{chunk}",
    )(*operands)


def spectral_call(layout, chunk, apart, side, blocks, lows, cotangent, tables, real_rows, imag_rows):
    half = jax.ShapeDtypeStruct((LANES // 2, layout.degrees), jnp.float32)
    operands = [side] + list(blocks) + list(lows) + [cotangent, cotangent] + list(tables) + [real_rows, imag_rows]
    low_spec = pl.BlockSpec(memory_space=pl.ANY) if apart else whole()
    specs = [pl.BlockSpec(memory_space=pltpu.SMEM)] + [whole()] * len(blocks) + [low_spec] * len(lows)
    specs += grid_specs(layout, chunk) + [whole()] * (len(tables) + 2)
    return pl.pallas_call(
        functools.partial(spectral_kernel, layout, apart),
        grid=(layout.half // PAIRS,),
        in_specs=specs,
        out_specs=[whole()] * 2,
        out_shape=[half, half],
        scratch_shapes=[
            pltpu.VMEM((layout.slots * layout.pitch, LANES), jnp.float32),
            pltpu.VMEM((layout.slots * layout.pitch, LANES), jnp.float32),
            pltpu.VMEM((2 * layout.twos, layout.degrees, LANES), jnp.bfloat16),
            pltpu.VMEM((2 * layout.twos, layout.degrees, LANES), jnp.bfloat16),
            pltpu.VMEM((layout.pairs, layout.rows, LANES), jnp.bfloat16),
            pltpu.VMEM((layout.pairs, layout.rows, LANES), jnp.bfloat16),
            pltpu.VMEM((layout.sent * TAIL, LANES), jnp.float32),
            pltpu.VMEM((layout.parts * MOVED * layout.rows, LANES), jnp.float32),
            pltpu.SemaphoreType.DMA((3,)),
        ],
        compiler_params=pltpu.CompilerParams(vmem_limit_bytes=VMEM),
        cost_estimate=pl.CostEstimate(flops=8_000_000_000, bytes_accessed=30_000_000, transcendentals=0),
        name=f"spectral_{chunk}",
    )(*operands)


def radices(size):
    found, factor = [], 2
    while size > 1:
        while size % factor == 0:
            found.append(factor)
            size //= factor
        factor += 1
    return found


def sum_steps(axis):
    size = lax.axis_size(axis)
    steps, stride = [], 1
    for radix in radices(size):
        steps.append((axis, stride, radix))
        stride *= radix
    return steps


def hop_parcels(value, step):
    axis, stride, radix = step
    parcels = []
    for turn in range(1, radix):
        pairs = []
        for index in range(lax.axis_size(axis)):
            digit = index // stride % radix
            pairs.append((index, index + ((digit + turn) % radix - digit) * stride))
        parcels.append(lax.ppermute(value, axis, pairs))
    return parcels


def filter_rows(layout, spec):
    padded = jnp.pad(spec, ((0, layout.degrees - MODES), (0, 0)))
    front = jnp.pad(spec, ((layout.rows, layout.rows), (0, 0)))
    natural = front[MODES : MODES + layout.rows]
    backward = front[layout.rows + MODES - layout.rows : layout.rows + MODES][::-1]
    return jnp.concatenate([padded, natural, backward], axis=0).astype(jnp.float32)


def on_device(fields, cotangent, spec_real, spec_imag):
    parts = lax.axis_size("space")
    index = lax.axis_index("space")
    layout = Layout(parts, fields.shape[1])
    width = LANES // 2
    chunks = fields.shape[-1] // width
    inverse = jnp.asarray(fourier_constants(layout)[1])
    constants = legendre_constants(parts, layout.local)

    def local_table(name):
        return lax.dynamic_index_in_dim(jnp.asarray(constants[name]), index, keepdims=False)

    pair_fwd = jnp.asarray(constants["pair_fwd"])
    place = jnp.reshape(index, (1,)).astype(jnp.int32)
    def bands(name, first, count):
        table = jnp.asarray(constants[name])
        return lax.optimization_barrier(
            lax.dynamic_slice_in_dim(table, first * layout.rows, count * layout.rows, 1)
        )

    def side_by_side(table):
        return jnp.concatenate([table[::2], table[1::2]], axis=2)

    synth_own = bands("synth_low", index, 1)
    analysis = bands("analysis", parts - 1 - index, parts).reshape(layout.twos, -1, layout.degrees)
    analysis = jnp.swapaxes(analysis, 1, 2)
    back_low = jnp.swapaxes(synth_own.reshape(layout.twos, -1, layout.degrees), 1, 2)
    synth_low = side_by_side(synth_own)
    pair_tables = [local_table(name) for name in ("pair_synth", "pair_back")]
    low_tables = [analysis, synth_low]
    tables = [inverse, back_low] + pair_tables + [jnp.asarray(constants["place"])]
    fields, cotangent = jnp.swapaxes(fields, 2, 3), jnp.swapaxes(cotangent, 2, 3)
    real_all = filter_rows(layout, spec_real)
    imag_all = filter_rows(layout, spec_imag)

    def others(sent):
        routes = [[(source, (source + shift) % parts) for source in range(parts)] for shift in range(1, parts)]
        return [lax.ppermute(sent, "space", route) for route in routes]

    held = []
    for chunk in range(chunks):
        if chunk == 1:
            place, low_tables, tables = lax.optimization_barrier((place, low_tables, tables))
        bounds = (0, layout.blocks) if chunk < chunks - 1 else (0, layout.sent, layout.blocks)
        made = forward_call(layout, chunk, bounds, place, fields, pair_fwd)
        place, made = lax.optimization_barrier((place, list(made)))
        if len(made) > 1 and held:
            made[1], held[0][1] = lax.optimization_barrier((made[1], held[0][1]))
        held += [[own] + others(own) for own in made]

    hops = sum_steps("dp") + sum_steps("space")
    count_dp = len(sum_steps("dp"))
    swap = [(device, device ^ 1) for device in range(lax.axis_size("dp"))]
    side = jnp.stack([lax.rem(lax.axis_index("dp"), 2), index]).astype(jnp.int32)
    waiting = []

    def launch(value, done):
        if done:
            return value, hop_parcels(value, hops[done])
        keep, send = value
        return keep, [lax.ppermute(send, "dp", swap)]

    def hop_all(limit, tie):
        moved = []
        for value, done in waiting:
            if done < limit:
                value, parcels = launch(value, done)
                parcels, value, tie = lax.optimization_barrier((parcels, value, tie))
                value, done = sum(parcels, value), done + 1
            moved.append((value, done))
        waiting[:] = moved
        return tie

    def hop_last(times):
        for _ in range(times):
            value, done = waiting[-1]
            value, parcels = launch(value, done)
            waiting[-1] = (sum(parcels, value), done + 1)

    def before(values):
        if not waiting:
            return values
        values, sums = lax.optimization_barrier((values, [value for value, _ in waiting]))
        waiting[:] = [(value, done) for value, (_, done) in zip(sums, waiting)]
        return values

    for chunk in range(chunks):
        columns = slice(chunk * width, (chunk + 1) * width)
        real, imag = real_all[:, columns], imag_all[:, columns]
        real_rows = jnp.concatenate([real, real], axis=1)
        imag_rows = jnp.concatenate([-imag, imag], axis=1)
        blocks, lows, apart = held[chunk], low_tables, chunk == chunks - 1
        if apart:
            lows = low_call(layout, chunk, blocks, low_tables, real_rows, imag_rows)
            lows = before(hop_all(count_dp, lows))
            blocks = held[-1]
        grads = spectral_call(layout, chunk, apart, side, blocks, lows, cotangent, tables, real_rows, imag_rows)
        grads = hop_all(len(hops) if apart else count_dp, grads)
        waiting.append((grads, 0))
        if chunk < chunks - 2:
            hop_last(count_dp // 2)
            held[chunk + 1] = before(held[chunk + 1])

    hop_last(1)
    total, done = waiting.pop()
    while done < len(hops):
        joined = [value for value, at in waiting if at == done]
        waiting = [(value, at) for value, at in waiting if at != done]
        if joined:
            total = jnp.concatenate(joined + [total], axis=0)
        total, done = sum(hop_parcels(total, hops[done]), total), done + 1
    mine = jnp.concatenate([value for value, _ in waiting] + [total], axis=0)
    other = lax.ppermute(mine, "dp", swap)
    real = jnp.where(side[0] == 0, mine, other)[:, :MODES]
    imag = jnp.where(side[0] == 0, other, mine)[:, :MODES]
    batch_total = fields.shape[0] * lax.axis_size("dp")
    return (real.T / batch_total, imag.T / batch_total)


def solution(mesh):
    in_specs = (P("dp", "space", None, None), P("dp", "space", None, None), P(), P())
    out_specs = (P(), P())
    return jax.shard_map(
        on_device, mesh=mesh, in_specs=in_specs, out_specs=out_specs, check_vma=False
    )
```

```python
import functools
import math

import jax
import jax.numpy as jnp
import ml_dtypes
import numpy as np
from jax import lax
from jax.experimental import pallas as pl
from jax.experimental.pallas import tpu as pltpu
from jax.sharding import PartitionSpec as P

NLAT = 126
NLON = 252
MODES = 126
LANES = 128
GROUP = 16
PAIRS = 8
MOVED = 3
TAIL = 8
VMEM = 30 * 1024 * 1024
FORWARD_VMEM = 56 * 1024 * 1024


def round_up(value, step):
    return -(-value // step) * step


@functools.lru_cache(maxsize=None)
def legendre_table():
    single = np.float32
    colatitude = single(math.pi) * (np.arange(NLAT, dtype=single) + single(0.5)) / single(NLAT)
    cos_theta, sin_theta = np.cos(colatitude), np.sin(colatitude)
    counters = np.arange(1, MODES, dtype=single)
    log_steps = single(0.5) * np.log((2 * counters + 1) / (2 * counters))
    log_table = np.concatenate([np.zeros(1, single), np.cumsum(log_steps, dtype=single)])
    order = np.arange(MODES, dtype=single)[:, None]
    start = single(0.5 * math.log(1.0 / (4.0 * math.pi)))
    diagonal = np.exp(start + log_table[:, None] + order * np.log(sin_theta)[None])
    previous = earlier = np.zeros_like(diagonal)
    table = np.zeros((MODES, MODES, NLAT), single)
    for at in range(MODES):
        degree, below = single(at), single(at - 1)
        growth = np.sqrt(
            np.maximum(4 * degree * degree - 1, single(0)) / np.maximum(degree * degree - order * order, single(1))
        )
        damping = np.sqrt(
            np.maximum(below * below - order * order, single(0)) / np.maximum(4 * below * below - 1, single(1))
        )
        current = growth * (cos_theta[None] * previous - damping * earlier)
        current = np.where(order == degree, diagonal, np.where(order < degree, current, single(0)))
        table[:, at] = current
        previous, earlier = current, previous
    weight = single(math.pi / NLAT * (2.0 * math.pi / NLON)) * sin_theta
    return table, table * weight


def to_bf16(array):
    return np.where(np.abs(array) < 2.0**-126, 0.0, array).astype(ml_dtypes.bfloat16)


class Layout:
    def __init__(self, parts, local):
        self.parts, self.local = parts, local
        self.rows = round_up(local + 1, 16)
        self.half = self.rows // 2
        self.base = round_up(max(self.rows - local, 1), 8)
        self.pitch = self.rows + self.base
        self.low = max(MODES - local, 0)
        high = MODES - self.low
        self.pairs = round_up((high + 1) // 2, 2)
        self.twos = round_up(self.low, 2) // 2
        self.sent, self.runs = self.low, []
        self.carry()
        self.blocks = self.sent + self.pairs
        self.slots = round_up(self.low + 2 * self.pairs, 8)
        self.degrees = round_up(MODES, 16)
        self.first_natural = self.rows - MODES + self.low
        self.partner = MODES - 1 + self.low
        orders = list(range(self.low))
        for pair in range(self.pairs):
            order, mate = self.low + pair, self.partner - self.low - pair
            orders += [order if order <= mate else -1, mate if order < mate else -1]
        self.orders = np.array(orders + [-1] * (self.slots - len(orders)))

    def band(self, part):
        latitudes = np.arange(part * self.local, (part + 1) * self.local)
        return latitudes[::-1] if 2 * part < self.parts else latitudes

    def carry(self):
        plain = to_bf16(legendre_table()[0]).astype(np.float32)
        live = np.zeros(self.low, int)
        for part in range(self.parts):
            used = np.abs(plain[: self.low][:, :, self.band(part)]).max(axis=1) > 0
            for order in range(self.low):
                live[order] = max(live[order], *(1 + np.flatnonzero(used[order])), 1)
        sent = self.low - MOVED
        places = []
        for row in range(self.rows - 1, self.rows - TAIL - 1, -1):
            free = live[: max(sent, 0)] <= row
            first = int(np.flatnonzero(~free)[-1]) + 1 if (~free).any() else 0
            if first < sent:
                places.append((row, first, sent - first))
        runs = []
        for which in range(MOVED):
            done = 0
            while sent > 0 and done < live[sent + which] and places:
                row, first, count = places.pop(0)
                taken = min(count, live[sent + which] - done)
                runs.append((which, int(done), row, first, int(taken)))
                done += taken
                if taken < count:
                    places.insert(0, (row, int(first + taken), int(count - taken)))
            if sent <= 0 or done < live[sent + which]:
                return
        self.sent, self.runs = sent, runs


def fourier_constants(layout):
    orders = np.maximum(layout.orders, 0)
    angles = 2.0 * math.pi / NLON * (orders[:, None] * np.arange(NLON)[None] % NLON)
    live = (layout.orders >= 0)[:, None]
    basis = np.concatenate([np.cos(angles) * live, -np.sin(angles) * live])
    factor = np.where(layout.orders == 0, 1.0, 2.0)[:, None]
    inverse = basis * np.concatenate([factor, factor])
    return to_bf16(basis), to_bf16(inverse)


@functools.lru_cache(maxsize=None)
def legendre_constants(parts, local):
    layout = Layout(parts, local)
    plain, weighted = legendre_table()
    rows, degrees, low, pairs = layout.rows, layout.degrees, layout.low, layout.pairs
    analysis = np.zeros((2 * layout.twos, 2 * parts * rows, degrees))
    synth_low = np.zeros((2 * layout.twos, parts * rows, degrees))
    pair_fwd = np.zeros((parts, pairs, rows, 2 * rows))
    pair_back = np.zeros((parts, pairs, rows, 2 * rows))
    for part in range(parts):
        own = layout.band(part)
        start = part * rows
        synth_low[:low, start : start + local, :MODES] = np.swapaxes(plain[:low, :, own], 1, 2)
        for turn in (1, 2):
            start = (turn * parts - 1 - part) * rows
            analysis[:low, start : start + local, :MODES] = np.swapaxes(weighted[:low, :, own], 1, 2)
        for pair in range(pairs):
            order = low + pair
            mate = layout.partner - order
            for target, table in ((pair_fwd, weighted), (pair_back, plain)):
                if order <= mate:
                    count = MODES - order
                    target[part, pair, rows - count :, :local] = table[order][order:, own]
                if order < mate:
                    count = MODES - mate
                    target[part, pair, :count, rows : rows + local] = table[mate][mate:, own][::-1]
    pair_synth = np.swapaxes(pair_back, -1, -2)
    place = np.zeros((degrees, 2 * rows))
    for row in range(rows):
        if row >= rows - MODES + low:
            place[MODES - rows + row, row] = 1.0
        if MODES - 1 - row >= 0:
            place[MODES - 1 - row, rows + row] = 1.0
    return {
        "analysis": to_bf16(analysis),
        "synth_low": to_bf16(synth_low),
        "pair_fwd": to_bf16(pair_fwd),
        "pair_back": to_bf16(np.concatenate([pair_back[:, ::2], pair_back[:, 1::2]], axis=3)),
        "pair_synth": to_bf16(np.concatenate([pair_synth[:, ::2], pair_synth[:, 1::2]], axis=3)),
        "place": place.astype(np.float32),
    }


def dot(left, right, sides=(1, 0)):
    contract = (((sides[0],), (sides[1],)), ((), ()))
    return lax.dot_general(left, right, contract, preferred_element_type=jnp.float32)


def dot_two(left, first, second):
    upper = jnp.concatenate([first, jnp.zeros_like(first)], axis=1)
    lower = jnp.concatenate([jnp.zeros_like(second), second], axis=1)
    return dot(left, jnp.concatenate([upper, lower], axis=0))


def swap_halves(values):
    return pltpu.roll(values, LANES // 2, 1)


def interleave(first, second):
    lane = lax.broadcasted_iota(jnp.int32, first.shape, 1)
    below = lane < LANES // 2
    return (
        jnp.where(below, first, swap_halves(second)),
        jnp.where(below, swap_halves(first), second),
    )


def gelu_slope(values):
    cumulative = 0.5 * (1.0 + lax.erf(values / math.sqrt(2.0)))
    density = jnp.exp(-0.5 * values * values) / math.sqrt(2.0 * math.pi)
    return cumulative + values * density


def grid_rows(layout, north, south, quad, group):
    rows = []
    for pair in (2 * quad, 2 * quad + 1):
        rows.append(north[0, pair])
        values = south[0, pair]
        if layout.rows > layout.local:
            latitude = layout.half + group * PAIRS + pair
            values = jnp.where(latitude < layout.local, values, jnp.zeros_like(values))
        rows.append(values)
    return jnp.concatenate(rows, axis=0)


def row_of(layout, turned, group, place):
    if turned is True:
        steps = layout.half // PAIRS - 1
        return (steps - group) * PAIRS + (layout.base + layout.local - 1 - place - steps * PAIRS)
    row = latitude = group * PAIRS + place
    if turned is not False and latitude < layout.local:
        row = jnp.where(turned, layout.local - 1 - latitude, latitude)
    return layout.base + row


def scatter_rows(layout, turned, values, scratch, quad, group):
    slots = values.shape[0] // 2
    for which in range(2):
        columns = slice(which * LANES, (which + 1) * LANES)
        upper, lower = interleave(values[:slots, columns], values[slots:, columns])
        place = 2 * quad + which
        scratch[pl.ds(row_of(layout, turned, group, place), slots, stride=layout.pitch), :] = upper
        scratch[pl.ds(row_of(layout, turned, group, place + layout.half), slots, stride=layout.pitch), :] = lower


def gather_rows(layout, turned, scratch, quad, group):
    slots = layout.slots
    cosine, sine = [], []
    for which in range(2):
        place = 2 * quad + which
        upper = scratch[pl.ds(row_of(layout, turned, group, place), slots, stride=layout.pitch), :]
        lower = scratch[pl.ds(row_of(layout, turned, group, place + layout.half), slots, stride=layout.pitch), :]
        first, second = interleave(upper, lower)
        cosine.append(first.astype(jnp.bfloat16))
        sine.append(second.astype(jnp.bfloat16))
    return jnp.concatenate(
        [jnp.concatenate(cosine, axis=1), jnp.concatenate(sine, axis=1)], axis=0
    )


def order_rows(layout, scratch, first, count):
    parts = []
    for order in range(count):
        start = pl.multiple_of((first + order) * layout.pitch + layout.base, 8)
        parts.append(scratch[pl.ds(start, layout.rows), :])
    return jnp.concatenate(parts, axis=0).astype(jnp.bfloat16)


def band_copies(layout, chunk, fields, buffer, sems):
    width = LANES // 2
    copies = []
    for group in range(layout.half // PAIRS):
        started = []
        for side in range(2):
            first = side * layout.half + group * PAIRS
            count = min(PAIRS, layout.local - first)
            if count > 0:
                started.append(
                    pltpu.make_async_copy(
                        fields.at[0, pl.ds(first, count), pl.ds(chunk * width, width), :],
                        buffer.at[pl.ds(first, count)],
                        sems.at[2 * group + side],
                    )
                )
        copies.append(started)
    return copies


def forward_kernel(layout, chunk, bounds, index, fields, basis_all, pair_all, *refs):
    outs, refs = refs[: len(bounds) - 1], refs[len(bounds) - 1 :]
    scratch, buffer, basis, stage, pair_fwd, sems, basis_sem, pair_sem, out_sems = refs
    basis_copy = pltpu.make_async_copy(basis_all, basis, basis_sem)
    basis_copy.start()
    copies = band_copies(layout, chunk, fields, buffer, sems)
    for started in copies[:2]:
        for copy in started:
            copy.start()
    tables = pltpu.make_async_copy(pair_all.at[index[0]], pair_fwd, pair_sem)
    tables.start()
    if layout.rows > layout.local:
        shape = (layout.rows - layout.local,) + buffer.shape[1:]
        buffer[layout.local :] = jnp.zeros(shape, buffer.dtype)
    basis_copy.wait()
    turned = 2 * index[0] < layout.parts
    for group, started in enumerate(copies):
        for copy in started:
            copy.wait()
        for copy in sum(copies[group + 2 : group + 3], []):
            copy.start()
        for quad in range(PAIRS // 2):
            rows = []
            for which in range(2):
                latitude = group * PAIRS + 2 * quad + which
                rows += [buffer[latitude], buffer[latitude + layout.half]]
            grid = jnp.concatenate(rows, axis=0)
            scatter_rows(layout, turned, dot(basis[...], grid, (1, 1)), scratch, quad, group)

    def low_block(order, carry):
        stage[order] = order_rows(layout, scratch, order, 1)
        return carry

    def pair_block(pair, carry):
        values = order_rows(layout, scratch, layout.low + 2 * pair, 2)
        stage[layout.sent + pair] = dot(pair_fwd[pair], values).astype(jnp.bfloat16)
        return carry

    flushes = []

    def flush(first, last):
        at = max(at for at in range(len(outs)) if bounds[at] <= first)
        flushes.append(
            pltpu.make_async_copy(
                stage.at[pl.ds(first, last - first)],
                outs[at].at[pl.ds(first - bounds[at], last - first)],
                out_sems.at[len(flushes)],
            )
        )
        flushes[-1].start()

    for which, start, row, first, count in layout.runs:
        moved = scratch[pl.ds((layout.sent + which) * layout.pitch + layout.base + start, count), :]
        scratch[pl.ds(first * layout.pitch + layout.base + row, count, stride=layout.pitch), :] = moved
    middle = layout.sent // 2
    for first, last in ((0, middle), (middle, layout.sent)):
        lax.fori_loop(first, last, low_block, 0, unroll=8)
        flush(first, last)
    tables.wait()
    lax.fori_loop(0, layout.pairs, pair_block, 0, unroll=8)
    flush(layout.sent, layout.blocks)
    for copy in flushes:
        copy.wait()


def mix(spectral, swapped, real_rows, imag_rows):
    return (spectral * real_rows + swapped * imag_rows).astype(jnp.bfloat16)


def order_groups(layout):
    for start in range(0, layout.low, GROUP):
        stop = min(start + GROUP, layout.low)
        yield start // 2, (stop + 1) // 2, start // 16 * 16


def low_kernel(layout, *refs):
    low_orders(layout, refs[: layout.parts], *refs[layout.parts :])


def low_orders(
    layout, held, analysis, synth_low, real_ref, imag_ref, grid_low, spec_low, swap_low, tails, moved
):
    degrees, rows = layout.degrees, layout.rows
    if layout.runs:
        moved[...] = jnp.zeros_like(moved)
    for at, ref in enumerate(held):
        if layout.runs:

            def tail_block(order, carry):
                values = ref[order, rows - 16 :, :].astype(jnp.float32)
                tails[pl.ds(pl.multiple_of(order * TAIL, TAIL), TAIL), :] = values[16 - TAIL :]
                return carry

            lax.fori_loop(0, layout.sent, tail_block, 0, unroll=10)
        for which, start, row, first, count in layout.runs:
            begin = (at * MOVED + which) * rows + start
            source = pl.ds(first * TAIL + row - (rows - TAIL), count, stride=TAIL)
            moved[pl.ds(begin, count), :] = tails[source, :]

    def coefficients(order):
        if isinstance(order, int) and order >= layout.sent:
            which = min(order, layout.low - 1) - layout.sent
            starts = [(at * MOVED + which) * rows for at in range(layout.parts)]
            return jnp.concatenate([moved[start : start + rows, :] for start in starts], axis=0).astype(jnp.bfloat16)
        return jnp.concatenate([ref[order] for ref in held], axis=0)

    for start, stop, top in order_groups(layout):
        real_rows = real_ref[top:degrees, :]
        imag_rows = imag_ref[top:degrees, :]

        def low_block(two, carry):
            last = layout.low - 1
            second = min(2 * two + 1, last) if isinstance(two, int) else jnp.minimum(2 * two + 1, last)
            values = [coefficients(2 * two), coefficients(second)]
            spectral = dot_two(analysis[two, top:degrees, :], *values).astype(jnp.bfloat16)
            for which in range(2):
                spec_low[2 * two + which, top:degrees, :] = spectral[:, which * LANES : (which + 1) * LANES]
            return carry

        def mix_block(two, carry):
            mixed = []
            for order in (2 * two, 2 * two + 1):
                spectral = spec_low[order, top:degrees, :].astype(jnp.float32)
                swapped = swap_halves(spectral)
                swap_low[order, top:degrees, :] = swapped.astype(jnp.bfloat16)
                values = mix(spectral, swapped, real_rows, imag_rows)
                if top:
                    values = jnp.concatenate([jnp.zeros((top, LANES), values.dtype), values], axis=0)
                mixed.append(values)
            values = dot_two(synth_low[two], *mixed)
            for which in range(2):
                begin = pl.multiple_of((2 * two + which) * layout.pitch + layout.base, 8)
                grid_low[pl.ds(begin, layout.rows), :] = values[:, which * LANES : (which + 1) * LANES]
            return carry

        whole_twos = max(min(stop, layout.sent // 2 if layout.runs else stop), start)
        lax.fori_loop(start, whole_twos, low_block, 0, unroll=8)
        for two in range(whole_twos, stop):
            low_block(two, 0)
        lax.fori_loop(start, stop, mix_block, 0, unroll=8)


def spectral_kernel(layout, apart, side, *refs):
    held, lows, refs = refs[: layout.parts], refs[layout.parts : layout.parts + 2 + apart], refs[layout.parts + 2 + apart :]
    north, south, basis, back_low, pair_synth, pair_back, place, real_ref, imag_ref = refs[:9]
    keep, send, scratch, returned, spec_low, swap_low, spec_pair, swap_pair, tails, moved, sems = refs[9:]
    offset = 0 if apart else layout.sent
    group = pl.program_id(0)
    rows, degrees, low = layout.rows, layout.degrees, layout.low
    if apart:
        sources = (lows[0].at[pl.ds(0, low * layout.pitch)], lows[1], lows[2])
        targets = (scratch.at[pl.ds(0, low * layout.pitch)], spec_low, swap_low)
        copies = [pltpu.make_async_copy(*ends, sems.at[at]) for at, ends in enumerate(zip(sources, targets))]

    @pl.when(group == 0)
    def _():
        if apart:
            copies[0].start()
        else:
            low_orders(layout, held, *lows, real_ref, imag_ref, scratch, spec_low, swap_low, tails, moved)
        line = lax.broadcasted_iota(jnp.int32, (rows, LANES), 0)

        def pair_block(two, carry):
            mixed = []
            for pair in (2 * two, 2 * two + 1):
                total = sum(ref[offset + pair].astype(jnp.float32) for ref in held)
                spectral = total.astype(jnp.bfloat16)
                spec_pair[pair] = spectral
                natural = line >= layout.first_natural + pair
                real_rows = jnp.where(natural, real_ref[degrees : degrees + rows, :], real_ref[degrees + rows :, :])
                imag_rows = jnp.where(natural, imag_ref[degrees : degrees + rows, :], imag_ref[degrees + rows :, :])
                spectral = spectral.astype(jnp.float32)
                swapped = swap_halves(spectral)
                swap_pair[pair] = swapped.astype(jnp.bfloat16)
                mixed.append(mix(spectral, swapped, real_rows, imag_rows))
            values = dot_two(pair_synth[two], *mixed)
            for which in range(4):
                begin = pl.multiple_of((low + 4 * two + which) * layout.pitch + layout.base, 8)
                columns = slice(which // 2 * LANES, (which // 2 + 1) * LANES)
                scratch[pl.ds(begin, rows), :] = values[which % 2 * rows : (which % 2 + 1) * rows, columns]
            return carry

        lax.fori_loop(0, layout.pairs // 2, pair_block, 0, unroll=8)
        used = (low + 2 * layout.pairs) * layout.pitch
        if used < layout.slots * layout.pitch:
            scratch[used : layout.slots * layout.pitch, :] = jnp.zeros(
                (layout.slots * layout.pitch - used, LANES), jnp.float32
            )
        for row in range(layout.base + layout.local, layout.pitch):
            returned[pl.ds(row, layout.slots, stride=layout.pitch), :] = jnp.zeros((layout.slots, LANES), jnp.float32)
        if apart:
            copies[0].wait()
            copies[1].start()
            copies[2].start()

    def grid_step(turned):
        for quad in range(PAIRS // 2):
            modes = gather_rows(layout, turned, scratch, quad, group)
            signal = dot(modes, basis[...], (0, 0))
            incoming = grid_rows(layout, north, south, quad, group).astype(jnp.float32)
            upstream = (incoming * gelu_slope(signal)).astype(jnp.bfloat16)
            scatter_rows(layout, turned, dot(basis[...], upstream, (1, 1)), returned, quad, group)

    pl.when(2 * side[1] < layout.parts)(functools.partial(grid_step, True))
    pl.when(2 * side[1] >= layout.parts)(functools.partial(grid_step, False))

    @pl.when(group == pl.num_programs(0) - 1)
    def _():
        if apart:
            copies[1].wait()
            copies[2].wait()

        def products(spectral, swapped, back):
            return spectral.astype(jnp.float32) * back, swapped.astype(jnp.float32) * back

        zeros = jnp.zeros((degrees, LANES), jnp.float32)
        same, cross = zeros, zeros
        for start, stop, top in order_groups(layout):

            def low_block(two, carry):
                values = [order_rows(layout, returned, 2 * two + which, 1) for which in range(2)]
                back = dot_two(back_low[two, top:degrees, :], *values)
                for which in range(2):
                    order = 2 * two + which
                    first, second = products(
                        spec_low[order, top:degrees, :],
                        swap_low[order, top:degrees, :],
                        back[:, which * LANES : (which + 1) * LANES],
                    )
                    carry = carry[0] + first, carry[1] + second
                return carry

            part = jnp.zeros((degrees - top, LANES), jnp.float32)
            first, second = lax.fori_loop(start, stop, low_block, (part, part), unroll=8)
            if top:
                empty = jnp.zeros((top, LANES), jnp.float32)
                first = jnp.concatenate([empty, first], axis=0)
                second = jnp.concatenate([empty, second], axis=0)
            same, cross = same + first, cross + second

        line = lax.broadcasted_iota(jnp.int32, (rows, LANES), 0)

        def pair_block(two, carry):
            values = [order_rows(layout, returned, low + 4 * two + 2 * which, 2) for which in range(2)]
            back = dot_two(pair_back[two], *values)
            for which in range(2):
                pair = 2 * two + which
                first, second = products(
                    spec_pair[pair], swap_pair[pair], back[:, which * LANES : (which + 1) * LANES]
                )
                natural = line >= layout.first_natural + pair
                carry = (
                    carry[0] + jnp.where(natural, first, 0.0),
                    carry[1] + jnp.where(natural, second, 0.0),
                    carry[2] + jnp.where(natural, 0.0, first),
                    carry[3] + jnp.where(natural, 0.0, second),
                )
            return carry

        part = jnp.zeros((rows, LANES), jnp.float32)
        sums = lax.fori_loop(0, layout.pairs // 2, pair_block, (part,) * 4, unroll=16)
        placed = jnp.dot(
            place[...],
            jnp.concatenate(
                [jnp.concatenate(sums[:2], axis=1), jnp.concatenate(sums[2:], axis=1)], axis=0
            ),
            preferred_element_type=jnp.float32,
            precision=lax.Precision.HIGHEST,
        )
        same = same + placed[:, :LANES]
        cross = cross + placed[:, LANES:]
        real = same + swap_halves(same)
        imag = cross - swap_halves(cross)
        lane = lax.broadcasted_iota(jnp.int32, real.shape, 1)
        grads = jnp.where(lane < LANES // 2, real, imag).T
        upper, lower = grads[: LANES // 2], grads[LANES // 2 :]
        keep[...] = jnp.where(side[0] == 0, upper, lower)
        send[...] = jnp.where(side[0] == 0, lower, upper)


def grid_specs(layout, chunk):
    last = -(-layout.local // PAIRS) - 1
    shift = layout.half // PAIRS
    block = (1, PAIRS, LANES // 2, NLON)
    return [
        pl.BlockSpec(block, lambda g: (0, jnp.minimum(g, last), chunk, 0)),
        pl.BlockSpec(block, lambda g: (0, jnp.minimum(shift + g, last), chunk, 0)),
    ]


def whole():
    return pl.BlockSpec(memory_space=pltpu.VMEM)


def forward_call(layout, chunk, bounds, index, fields, pair_fwd):
    basis = jnp.asarray(fourier_constants(layout)[0])
    slots = basis.shape[0] // 2
    groups = layout.half // PAIRS
    anywhere = pl.BlockSpec(memory_space=pl.ANY)
    counts = [last - first for first, last in zip(bounds, bounds[1:])]
    return pl.pallas_call(
        functools.partial(forward_kernel, layout, chunk, bounds),
        in_specs=[pl.BlockSpec(memory_space=pltpu.SMEM)] + [anywhere] * 3,
        out_specs=[anywhere] * len(counts),
        out_shape=[jax.ShapeDtypeStruct((count, layout.rows, LANES), jnp.bfloat16) for count in counts],
        scratch_shapes=[
            pltpu.VMEM((slots * layout.pitch, LANES), jnp.float32),
            pltpu.VMEM((layout.rows, LANES // 2, NLON), jnp.bfloat16),
            pltpu.VMEM(basis.shape, jnp.bfloat16),
            pltpu.VMEM((layout.blocks, layout.rows, LANES), jnp.bfloat16),
            pltpu.VMEM(pair_fwd.shape[1:], jnp.bfloat16),
            pltpu.SemaphoreType.DMA((2 * groups,)),
            pltpu.SemaphoreType.DMA,
            pltpu.SemaphoreType.DMA,
            pltpu.SemaphoreType.DMA((3,)),
        ],
        compiler_params=pltpu.CompilerParams(vmem_limit_bytes=FORWARD_VMEM),
        cost_estimate=pl.CostEstimate(flops=1_000_000, bytes_accessed=100_000, transcendentals=0),
        name=f"forward_{chunk}",
    )(index, fields, basis, pair_fwd)


def low_call(layout, chunk, coeffs, tables, real_rows, imag_rows):
    operands = list(coeffs) + list(tables) + [real_rows, imag_rows]
    spectra = jax.ShapeDtypeStruct((2 * layout.twos, layout.degrees, LANES), jnp.bfloat16)
    return pl.pallas_call(
        functools.partial(low_kernel, layout),
        in_specs=[whole()] * len(operands),
        out_specs=[whole()] * 3,
        out_shape=[jax.ShapeDtypeStruct((2 * layout.twos * layout.pitch, LANES), jnp.float32), spectra, spectra],
        scratch_shapes=[
            pltpu.VMEM((layout.sent * TAIL, LANES), jnp.float32),
            pltpu.VMEM((layout.parts * MOVED * layout.rows, LANES), jnp.float32),
        ],
        compiler_params=pltpu.CompilerParams(vmem_limit_bytes=VMEM),
        cost_estimate=pl.CostEstimate(flops=8_000_000_000, bytes_accessed=30_000_000, transcendentals=0),
        name=f"low_{chunk}",
    )(*operands)


def spectral_call(layout, chunk, apart, side, blocks, lows, cotangent, tables, real_rows, imag_rows):
    half = jax.ShapeDtypeStruct((LANES // 2, layout.degrees), jnp.float32)
    operands = [side] + list(blocks) + list(lows) + [cotangent, cotangent] + list(tables) + [real_rows, imag_rows]
    low_spec = pl.BlockSpec(memory_space=pl.ANY) if apart else whole()
    specs = [pl.BlockSpec(memory_space=pltpu.SMEM)] + [whole()] * len(blocks) + [low_spec] * len(lows)
    specs += grid_specs(layout, chunk) + [whole()] * (len(tables) + 2)
    return pl.pallas_call(
        functools.partial(spectral_kernel, layout, apart),
        grid=(layout.half // PAIRS,),
        in_specs=specs,
        out_specs=[whole()] * 2,
        out_shape=[half, half],
        scratch_shapes=[
            pltpu.VMEM((layout.slots * layout.pitch, LANES), jnp.float32),
            pltpu.VMEM((layout.slots * layout.pitch, LANES), jnp.float32),
            pltpu.VMEM((2 * layout.twos, layout.degrees, LANES), jnp.bfloat16),
            pltpu.VMEM((2 * layout.twos, layout.degrees, LANES), jnp.bfloat16),
            pltpu.VMEM((layout.pairs, layout.rows, LANES), jnp.bfloat16),
            pltpu.VMEM((layout.pairs, layout.rows, LANES), jnp.bfloat16),
            pltpu.VMEM((layout.sent * TAIL, LANES), jnp.float32),
            pltpu.VMEM((layout.parts * MOVED * layout.rows, LANES), jnp.float32),
            pltpu.SemaphoreType.DMA((3,)),
        ],
        compiler_params=pltpu.CompilerParams(vmem_limit_bytes=VMEM),
        cost_estimate=pl.CostEstimate(flops=8_000_000_000, bytes_accessed=30_000_000, transcendentals=0),
        name=f"spectral_{chunk}",
    )(*operands)


def radices(size):
    found, factor = [], 2
    while size > 1:
        while size % factor == 0:
            found.append(factor)
            size //= factor
        factor += 1
    return found


def sum_steps(axis):
    size = lax.axis_size(axis)
    steps, stride = [], 1
    for radix in radices(size):
        steps.append((axis, stride, radix))
        stride *= radix
    return steps


def hop_parcels(value, step):
    axis, stride, radix = step
    parcels = []
    for turn in range(1, radix):
        pairs = []
        for index in range(lax.axis_size(axis)):
            digit = index // stride % radix
            pairs.append((index, index + ((digit + turn) % radix - digit) * stride))
        parcels.append(lax.ppermute(value, axis, pairs))
    return parcels


def filter_rows(layout, spec):
    padded = jnp.pad(spec, ((0, layout.degrees - MODES), (0, 0)))
    front = jnp.pad(spec, ((layout.rows, layout.rows), (0, 0)))
    natural = front[MODES : MODES + layout.rows]
    backward = front[layout.rows + MODES - layout.rows : layout.rows + MODES][::-1]
    return jnp.concatenate([padded, natural, backward], axis=0).astype(jnp.float32)


def on_device(fields, cotangent, spec_real, spec_imag):
    parts = lax.axis_size("space")
    index = lax.axis_index("space")
    layout = Layout(parts, fields.shape[1])
    width = LANES // 2
    chunks = fields.shape[-1] // width
    inverse = jnp.asarray(fourier_constants(layout)[1])
    constants = legendre_constants(parts, layout.local)

    def local_table(name):
        return lax.dynamic_index_in_dim(jnp.asarray(constants[name]), index, keepdims=False)

    pair_fwd = jnp.asarray(constants["pair_fwd"])
    place = jnp.reshape(index, (1,)).astype(jnp.int32)
    def bands(name, first, count):
        table = jnp.asarray(constants[name])
        return lax.optimization_barrier(
            lax.dynamic_slice_in_dim(table, first * layout.rows, count * layout.rows, 1)
        )

    def side_by_side(table):
        return jnp.concatenate([table[::2], table[1::2]], axis=2)

    synth_own = bands("synth_low", index, 1)
    analysis = bands("analysis", parts - 1 - index, parts).reshape(layout.twos, -1, layout.degrees)
    analysis = jnp.swapaxes(analysis, 1, 2)
    back_low = jnp.swapaxes(synth_own.reshape(layout.twos, -1, layout.degrees), 1, 2)
    synth_low = side_by_side(synth_own)
    pair_tables = [local_table(name) for name in ("pair_synth", "pair_back")]
    low_tables = [analysis, synth_low]
    tables = [inverse, back_low] + pair_tables + [jnp.asarray(constants["place"])]
    fields, cotangent = jnp.swapaxes(fields, 2, 3), jnp.swapaxes(cotangent, 2, 3)
    real_all = filter_rows(layout, spec_real)
    imag_all = filter_rows(layout, spec_imag)

    def others(sent):
        routes = [[(source, (source + shift) % parts) for source in range(parts)] for shift in range(1, parts)]
        return [lax.ppermute(sent, "space", route) for route in routes]

    held = []
    for chunk in range(chunks):
        if chunk == 1:
            place, low_tables, tables = lax.optimization_barrier((place, low_tables, tables))
        bounds = (0, layout.blocks) if chunk < chunks - 1 else (0, layout.sent, layout.blocks)
        made = forward_call(layout, chunk, bounds, place, fields, pair_fwd)
        place, made = lax.optimization_barrier((place, list(made)))
        if len(made) > 1 and held:
            made[1], held[0][1] = lax.optimization_barrier((made[1], held[0][1]))
        held += [[own] + others(own) for own in made]

    hops = sum_steps("dp") + sum_steps("space")
    count_dp = len(sum_steps("dp"))
    swap = [(device, device ^ 1) for device in range(lax.axis_size("dp"))]
    side = jnp.stack([lax.rem(lax.axis_index("dp"), 2), index]).astype(jnp.int32)
    waiting = []

    def launch(value, done):
        if done:
            return value, hop_parcels(value, hops[done])
        keep, send = value
        return keep, [lax.ppermute(send, "dp", swap)]

    def hop_all(limit, tie):
        moved = []
        for value, done in waiting:
            if done < limit:
                value, parcels = launch(value, done)
                parcels, value, tie = lax.optimization_barrier((parcels, value, tie))
                value, done = sum(parcels, value), done + 1
            moved.append((value, done))
        waiting[:] = moved
        return tie

    def hop_last(times):
        for _ in range(times):
            value, done = waiting[-1]
            value, parcels = launch(value, done)
            waiting[-1] = (sum(parcels, value), done + 1)

    def before(values):
        if not waiting:
            return values
        values, sums = lax.optimization_barrier((values, [value for value, _ in waiting]))
        waiting[:] = [(value, done) for value, (_, done) in zip(sums, waiting)]
        return values

    for chunk in range(chunks):
        columns = slice(chunk * width, (chunk + 1) * width)
        real, imag = real_all[:, columns], imag_all[:, columns]
        real_rows = jnp.concatenate([real, real], axis=1)
        imag_rows = jnp.concatenate([-imag, imag], axis=1)
        blocks, lows, apart = held[chunk], low_tables, chunk == chunks - 1
        if apart:
            lows = low_call(layout, chunk, blocks, low_tables, real_rows, imag_rows)
            lows = before(hop_all(count_dp, lows))
            blocks = held[-1]
        grads = spectral_call(layout, chunk, apart, side, blocks, lows, cotangent, tables, real_rows, imag_rows)
        grads = hop_all(len(hops) if apart else count_dp, grads)
        waiting.append((grads, 0))
        if chunk < chunks - 2:
            hop_last(count_dp // 2)
            held[chunk + 1] = before(held[chunk + 1])

    hop_last(1)
    total, done = waiting.pop()
    while done < len(hops):
        joined = [value for value, at in waiting if at == done]
        waiting = [(value, at) for value, at in waiting if at != done]
        if joined:
            total = jnp.concatenate(joined + [total], axis=0)
        total, done = sum(hop_parcels(total, hops[done]), total), done + 1
    mine = jnp.concatenate([value for value, _ in waiting] + [total], axis=0)
    other = lax.ppermute(mine, "dp", swap)
    real = jnp.where(side[0] == 0, mine, other)[:, :MODES]
    imag = jnp.where(side[0] == 0, other, mine)[:, :MODES]
    batch_total = fields.shape[0] * lax.axis_size("dp")
    return (real.T / batch_total, imag.T / batch_total)


def solution(mesh):
    in_specs = (P("dp", "space", None, None), P("dp", "space", None, None), P(), P())
    out_specs = (P(), P())
    return jax.shard_map(
        on_device, mesh=mesh, in_specs=in_specs, out_specs=out_specs, check_vma=False
    )
```

```python
import functools
import math

import jax
import jax.numpy as jnp
import ml_dtypes
import numpy as np
from jax import lax
from jax.experimental import pallas as pl
from jax.experimental.pallas import tpu as pltpu
from jax.sharding import PartitionSpec as P

NLAT = 126
NLON = 252
MODES = 126
LANES = 128
GROUP = 16
PAIRS = 16
MOVED = 3
TAIL = 8
VMEM = 30 * 1024 * 1024
FORWARD_VMEM = 56 * 1024 * 1024


def round_up(value, step):
    return -(-value // step) * step


@functools.lru_cache(maxsize=None)
def legendre_table():
    single = np.float32
    colatitude = single(math.pi) * (np.arange(NLAT, dtype=single) + single(0.5)) / single(NLAT)
    cos_theta, sin_theta = np.cos(colatitude), np.sin(colatitude)
    counters = np.arange(1, MODES, dtype=single)
    log_steps = single(0.5) * np.log((2 * counters + 1) / (2 * counters))
    log_table = np.concatenate([np.zeros(1, single), np.cumsum(log_steps, dtype=single)])
    order = np.arange(MODES, dtype=single)[:, None]
    start = single(0.5 * math.log(1.0 / (4.0 * math.pi)))
    diagonal = np.exp(start + log_table[:, None] + order * np.log(sin_theta)[None])
    previous = earlier = np.zeros_like(diagonal)
    table = np.zeros((MODES, MODES, NLAT), single)
    for at in range(MODES):
        degree, below = single(at), single(at - 1)
        growth = np.sqrt(
            np.maximum(4 * degree * degree - 1, single(0)) / np.maximum(degree * degree - order * order, single(1))
        )
        damping = np.sqrt(
            np.maximum(below * below - order * order, single(0)) / np.maximum(4 * below * below - 1, single(1))
        )
        current = growth * (cos_theta[None] * previous - damping * earlier)
        current = np.where(order == degree, diagonal, np.where(order < degree, current, single(0)))
        table[:, at] = current
        previous, earlier = current, previous
    weight = single(math.pi / NLAT * (2.0 * math.pi / NLON)) * sin_theta
    return table, table * weight


def to_bf16(array):
    return np.where(np.abs(array) < 2.0**-126, 0.0, array).astype(ml_dtypes.bfloat16)


class Layout:
    def __init__(self, parts, local):
        self.parts, self.local = parts, local
        self.rows = round_up(local + 1, 16)
        self.half = self.rows // 2
        self.base = round_up(max(self.rows - local, 1), 8)
        self.pitch = self.rows + self.base
        self.low = max(MODES - local, 0)
        high = MODES - self.low
        self.pairs = round_up((high + 1) // 2, 2)
        self.twos = round_up(self.low, 2) // 2
        self.sent, self.runs = self.low, []
        self.carry()
        self.blocks = self.sent + self.pairs
        self.slots = round_up(self.low + 2 * self.pairs, 8)
        self.degrees = round_up(MODES, 16)
        self.first_natural = self.rows - MODES + self.low
        self.partner = MODES - 1 + self.low
        orders = list(range(self.low))
        for pair in range(self.pairs):
            order, mate = self.low + pair, self.partner - self.low - pair
            orders += [order if order <= mate else -1, mate if order < mate else -1]
        self.orders = np.array(orders + [-1] * (self.slots - len(orders)))

    def band(self, part):
        latitudes = np.arange(part * self.local, (part + 1) * self.local)
        return latitudes[::-1] if 2 * part < self.parts else latitudes

    def carry(self):
        plain = to_bf16(legendre_table()[0]).astype(np.float32)
        live = np.zeros(self.low, int)
        for part in range(self.parts):
            used = np.abs(plain[: self.low][:, :, self.band(part)]).max(axis=1) > 0
            for order in range(self.low):
                live[order] = max(live[order], *(1 + np.flatnonzero(used[order])), 1)
        sent = self.low - MOVED
        places = []
        for row in range(self.rows - 1, self.rows - TAIL - 1, -1):
            free = live[: max(sent, 0)] <= row
            first = int(np.flatnonzero(~free)[-1]) + 1 if (~free).any() else 0
            if first < sent:
                places.append((row, first, sent - first))
        runs = []
        for which in range(MOVED):
            done = 0
            while sent > 0 and done < live[sent + which] and places:
                row, first, count = places.pop(0)
                taken = min(count, live[sent + which] - done)
                runs.append((which, int(done), row, first, int(taken)))
                done += taken
                if taken < count:
                    places.insert(0, (row, int(first + taken), int(count - taken)))
            if sent <= 0 or done < live[sent + which]:
                return
        self.sent, self.runs = sent, runs


def fourier_constants(layout):
    orders = np.maximum(layout.orders, 0)
    angles = 2.0 * math.pi / NLON * (orders[:, None] * np.arange(NLON)[None] % NLON)
    live = (layout.orders >= 0)[:, None]
    basis = np.concatenate([np.cos(angles) * live, -np.sin(angles) * live])
    factor = np.where(layout.orders == 0, 1.0, 2.0)[:, None]
    inverse = basis * np.concatenate([factor, factor])
    return to_bf16(basis), to_bf16(inverse)


@functools.lru_cache(maxsize=None)
def legendre_constants(parts, local):
    layout = Layout(parts, local)
    plain, weighted = legendre_table()
    rows, degrees, low, pairs = layout.rows, layout.degrees, layout.low, layout.pairs
    analysis = np.zeros((2 * layout.twos, 2 * parts * rows, degrees))
    synth_low = np.zeros((2 * layout.twos, parts * rows, degrees))
    pair_fwd = np.zeros((parts, pairs, rows, 2 * rows))
    pair_back = np.zeros((parts, pairs, rows, 2 * rows))
    for part in range(parts):
        own = layout.band(part)
        start = part * rows
        synth_low[:low, start : start + local, :MODES] = np.swapaxes(plain[:low, :, own], 1, 2)
        for turn in (1, 2):
            start = (turn * parts - 1 - part) * rows
            analysis[:low, start : start + local, :MODES] = np.swapaxes(weighted[:low, :, own], 1, 2)
        for pair in range(pairs):
            order = low + pair
            mate = layout.partner - order
            for target, table in ((pair_fwd, weighted), (pair_back, plain)):
                if order <= mate:
                    count = MODES - order
                    target[part, pair, rows - count :, :local] = table[order][order:, own]
                if order < mate:
                    count = MODES - mate
                    target[part, pair, :count, rows : rows + local] = table[mate][mate:, own][::-1]
    pair_synth = np.swapaxes(pair_back, -1, -2)
    place = np.zeros((degrees, 2 * rows))
    for row in range(rows):
        if row >= rows - MODES + low:
            place[MODES - rows + row, row] = 1.0
        if MODES - 1 - row >= 0:
            place[MODES - 1 - row, rows + row] = 1.0
    return {
        "analysis": to_bf16(analysis),
        "synth_low": to_bf16(synth_low),
        "pair_fwd": to_bf16(pair_fwd),
        "pair_back": to_bf16(np.concatenate([pair_back[:, ::2], pair_back[:, 1::2]], axis=3)),
        "pair_synth": to_bf16(np.concatenate([pair_synth[:, ::2], pair_synth[:, 1::2]], axis=3)),
        "place": place.astype(np.float32),
    }


def dot(left, right, sides=(1, 0)):
    contract = (((sides[0],), (sides[1],)), ((), ()))
    return lax.dot_general(left, right, contract, preferred_element_type=jnp.float32)


def dot_two(left, first, second):
    upper = jnp.concatenate([first, jnp.zeros_like(first)], axis=1)
    lower = jnp.concatenate([jnp.zeros_like(second), second], axis=1)
    return dot(left, jnp.concatenate([upper, lower], axis=0))


def swap_halves(values):
    return pltpu.roll(values, LANES // 2, 1)


def interleave(first, second):
    lane = lax.broadcasted_iota(jnp.int32, first.shape, 1)
    below = lane < LANES // 2
    return (
        jnp.where(below, first, swap_halves(second)),
        jnp.where(below, swap_halves(first), second),
    )


def gelu_slope(values):
    cumulative = 0.5 * (1.0 + lax.erf(values / math.sqrt(2.0)))
    density = jnp.exp(-0.5 * values * values) / math.sqrt(2.0 * math.pi)
    return cumulative + values * density


def grid_rows(layout, north, south, quad, group):
    rows = []
    for pair in (2 * quad, 2 * quad + 1):
        rows.append(north[0, pair])
        values = south[0, pair]
        if layout.rows > layout.local:
            latitude = layout.half + group * PAIRS + pair
            values = jnp.where(latitude < layout.local, values, jnp.zeros_like(values))
        rows.append(values)
    return jnp.concatenate(rows, axis=0)


def row_of(layout, turned, group, place):
    if turned is True:
        steps = layout.half // PAIRS - 1
        return (steps - group) * PAIRS + (layout.base + layout.local - 1 - place - steps * PAIRS)
    row = latitude = group * PAIRS + place
    if turned is not False and latitude < layout.local:
        row = jnp.where(turned, layout.local - 1 - latitude, latitude)
    return layout.base + row


def scatter_rows(layout, turned, values, scratch, quad, group):
    slots = values.shape[0] // 2
    for which in range(2):
        columns = slice(which * LANES, (which + 1) * LANES)
        upper, lower = interleave(values[:slots, columns], values[slots:, columns])
        place = 2 * quad + which
        scratch[pl.ds(row_of(layout, turned, group, place), slots, stride=layout.pitch), :] = upper
        scratch[pl.ds(row_of(layout, turned, group, place + layout.half), slots, stride=layout.pitch), :] = lower


def gather_rows(layout, turned, scratch, quad, group):
    slots = layout.slots
    cosine, sine = [], []
    for which in range(2):
        place = 2 * quad + which
        upper = scratch[pl.ds(row_of(layout, turned, group, place), slots, stride=layout.pitch), :]
        lower = scratch[pl.ds(row_of(layout, turned, group, place + layout.half), slots, stride=layout.pitch), :]
        first, second = interleave(upper, lower)
        cosine.append(first.astype(jnp.bfloat16))
        sine.append(second.astype(jnp.bfloat16))
    return jnp.concatenate(
        [jnp.concatenate(cosine, axis=1), jnp.concatenate(sine, axis=1)], axis=0
    )


def order_rows(layout, scratch, first, count):
    parts = []
    for order in range(count):
        start = pl.multiple_of((first + order) * layout.pitch + layout.base, 8)
        parts.append(scratch[pl.ds(start, layout.rows), :])
    return jnp.concatenate(parts, axis=0).astype(jnp.bfloat16)


def band_copies(layout, chunk, fields, buffer, sems):
    width = LANES // 2
    copies = []
    for group in range(layout.half // PAIRS):
        started = []
        for side in range(2):
            first = side * layout.half + group * PAIRS
            count = min(PAIRS, layout.local - first)
            if count > 0:
                started.append(
                    pltpu.make_async_copy(
                        fields.at[0, pl.ds(first, count), pl.ds(chunk * width, width), :],
                        buffer.at[pl.ds(first, count)],
                        sems.at[2 * group + side],
                    )
                )
        copies.append(started)
    return copies


def forward_kernel(layout, chunk, bounds, index, fields, basis_all, pair_all, *refs):
    outs, refs = refs[: len(bounds) - 1], refs[len(bounds) - 1 :]
    scratch, buffer, basis, stage, pair_fwd, sems, basis_sem, pair_sem, out_sems = refs
    basis_copy = pltpu.make_async_copy(basis_all, basis, basis_sem)
    basis_copy.start()
    copies = band_copies(layout, chunk, fields, buffer, sems)
    for started in copies[:2]:
        for copy in started:
            copy.start()
    tables = pltpu.make_async_copy(pair_all.at[index[0]], pair_fwd, pair_sem)
    tables.start()
    if layout.rows > layout.local:
        shape = (layout.rows - layout.local,) + buffer.shape[1:]
        buffer[layout.local :] = jnp.zeros(shape, buffer.dtype)
    basis_copy.wait()
    turned = 2 * index[0] < layout.parts
    for group, started in enumerate(copies):
        for copy in started:
            copy.wait()
        for copy in sum(copies[group + 2 : group + 3], []):
            copy.start()
        for quad in range(PAIRS // 2):
            rows = []
            for which in range(2):
                latitude = group * PAIRS + 2 * quad + which
                rows += [buffer[latitude], buffer[latitude + layout.half]]
            grid = jnp.concatenate(rows, axis=0)
            scatter_rows(layout, turned, dot(basis[...], grid, (1, 1)), scratch, quad, group)

    def low_block(order, carry):
        stage[order] = order_rows(layout, scratch, order, 1)
        return carry

    def pair_block(pair, carry):
        values = order_rows(layout, scratch, layout.low + 2 * pair, 2)
        stage[layout.sent + pair] = dot(pair_fwd[pair], values).astype(jnp.bfloat16)
        return carry

    flushes = []

    def flush(first, last):
        at = max(at for at in range(len(outs)) if bounds[at] <= first)
        flushes.append(
            pltpu.make_async_copy(
                stage.at[pl.ds(first, last - first)],
                outs[at].at[pl.ds(first - bounds[at], last - first)],
                out_sems.at[len(flushes)],
            )
        )
        flushes[-1].start()

    for which, start, row, first, count in layout.runs:
        moved = scratch[pl.ds((layout.sent + which) * layout.pitch + layout.base + start, count), :]
        scratch[pl.ds(first * layout.pitch + layout.base + row, count, stride=layout.pitch), :] = moved
    middle = layout.sent // 2
    for first, last in ((0, middle), (middle, layout.sent)):
        lax.fori_loop(first, last, low_block, 0, unroll=8)
        flush(first, last)
    tables.wait()
    lax.fori_loop(0, layout.pairs, pair_block, 0, unroll=8)
    flush(layout.sent, layout.blocks)
    for copy in flushes:
        copy.wait()


def mix(spectral, swapped, real_rows, imag_rows):
    return (spectral * real_rows + swapped * imag_rows).astype(jnp.bfloat16)


def order_groups(layout):
    for start in range(0, layout.low, GROUP):
        stop = min(start + GROUP, layout.low)
        yield start // 2, (stop + 1) // 2, start // 16 * 16


def low_kernel(layout, *refs):
    low_orders(layout, refs[: layout.parts], *refs[layout.parts :])


def low_orders(
    layout, held, analysis, synth_low, real_ref, imag_ref, grid_low, spec_low, swap_low, tails, moved
):
    degrees, rows = layout.degrees, layout.rows
    if layout.runs:
        moved[...] = jnp.zeros_like(moved)
    for at, ref in enumerate(held):
        if layout.runs:

            def tail_block(order, carry):
                values = ref[order, rows - 16 :, :].astype(jnp.float32)
                tails[pl.ds(pl.multiple_of(order * TAIL, TAIL), TAIL), :] = values[16 - TAIL :]
                return carry

            lax.fori_loop(0, layout.sent, tail_block, 0, unroll=10)
        for which, start, row, first, count in layout.runs:
            begin = (at * MOVED + which) * rows + start
            source = pl.ds(first * TAIL + row - (rows - TAIL), count, stride=TAIL)
            moved[pl.ds(begin, count), :] = tails[source, :]

    def coefficients(order):
        if isinstance(order, int) and order >= layout.sent:
            which = min(order, layout.low - 1) - layout.sent
            starts = [(at * MOVED + which) * rows for at in range(layout.parts)]
            return jnp.concatenate([moved[start : start + rows, :] for start in starts], axis=0).astype(jnp.bfloat16)
        return jnp.concatenate([ref[order] for ref in held], axis=0)

    for start, stop, top in order_groups(layout):
        real_rows = real_ref[top:degrees, :]
        imag_rows = imag_ref[top:degrees, :]

        def low_block(two, carry):
            last = layout.low - 1
            second = min(2 * two + 1, last) if isinstance(two, int) else jnp.minimum(2 * two + 1, last)
            values = [coefficients(2 * two), coefficients(second)]
            spectral = dot_two(analysis[two, top:degrees, :], *values).astype(jnp.bfloat16)
            for which in range(2):
                spec_low[2 * two + which, top:degrees, :] = spectral[:, which * LANES : (which + 1) * LANES]
            return carry

        def mix_block(two, carry):
            mixed = []
            for order in (2 * two, 2 * two + 1):
                spectral = spec_low[order, top:degrees, :].astype(jnp.float32)
                swapped = swap_halves(spectral)
                swap_low[order, top:degrees, :] = swapped.astype(jnp.bfloat16)
                values = mix(spectral, swapped, real_rows, imag_rows)
                if top:
                    values = jnp.concatenate([jnp.zeros((top, LANES), values.dtype), values], axis=0)
                mixed.append(values)
            values = dot_two(synth_low[two], *mixed)
            for which in range(2):
                begin = pl.multiple_of((2 * two + which) * layout.pitch + layout.base, 8)
                grid_low[pl.ds(begin, layout.rows), :] = values[:, which * LANES : (which + 1) * LANES]
            return carry

        whole_twos = max(min(stop, layout.sent // 2 if layout.runs else stop), start)
        lax.fori_loop(start, whole_twos, low_block, 0, unroll=8)
        for two in range(whole_twos, stop):
            low_block(two, 0)
        lax.fori_loop(start, stop, mix_block, 0, unroll=8)


def spectral_kernel(layout, apart, side, *refs):
    held, lows, refs = refs[: layout.parts], refs[layout.parts : layout.parts + 2 + apart], refs[layout.parts + 2 + apart :]
    north, south, basis, back_low, pair_synth, pair_back, place, real_ref, imag_ref = refs[:9]
    keep, send, scratch, returned, spec_low, swap_low, spec_pair, swap_pair, tails, moved, sems = refs[9:]
    offset = 0 if apart else layout.sent
    group = pl.program_id(0)
    rows, degrees, low = layout.rows, layout.degrees, layout.low
    if apart:
        sources = (lows[0].at[pl.ds(0, low * layout.pitch)], lows[1], lows[2])
        targets = (scratch.at[pl.ds(0, low * layout.pitch)], spec_low, swap_low)
        copies = [pltpu.make_async_copy(*ends, sems.at[at]) for at, ends in enumerate(zip(sources, targets))]

    @pl.when(group == 0)
    def _():
        if apart:
            copies[0].start()
        else:
            low_orders(layout, held, *lows, real_ref, imag_ref, scratch, spec_low, swap_low, tails, moved)
        line = lax.broadcasted_iota(jnp.int32, (rows, LANES), 0)

        def pair_block(two, carry):
            mixed = []
            for pair in (2 * two, 2 * two + 1):
                total = sum(ref[offset + pair].astype(jnp.float32) for ref in held)
                spectral = total.astype(jnp.bfloat16)
                spec_pair[pair] = spectral
                natural = line >= layout.first_natural + pair
                real_rows = jnp.where(natural, real_ref[degrees : degrees + rows, :], real_ref[degrees + rows :, :])
                imag_rows = jnp.where(natural, imag_ref[degrees : degrees + rows, :], imag_ref[degrees + rows :, :])
                spectral = spectral.astype(jnp.float32)
                swapped = swap_halves(spectral)
                swap_pair[pair] = swapped.astype(jnp.bfloat16)
                mixed.append(mix(spectral, swapped, real_rows, imag_rows))
            values = dot_two(pair_synth[two], *mixed)
            for which in range(4):
                begin = pl.multiple_of((low + 4 * two + which) * layout.pitch + layout.base, 8)
                columns = slice(which // 2 * LANES, (which // 2 + 1) * LANES)
                scratch[pl.ds(begin, rows), :] = values[which % 2 * rows : (which % 2 + 1) * rows, columns]
            return carry

        lax.fori_loop(0, layout.pairs // 2, pair_block, 0, unroll=8)
        used = (low + 2 * layout.pairs) * layout.pitch
        if used < layout.slots * layout.pitch:
            scratch[used : layout.slots * layout.pitch, :] = jnp.zeros(
                (layout.slots * layout.pitch - used, LANES), jnp.float32
            )
        for row in range(layout.base + layout.local, layout.pitch):
            returned[pl.ds(row, layout.slots, stride=layout.pitch), :] = jnp.zeros((layout.slots, LANES), jnp.float32)
        if apart:
            copies[0].wait()
            copies[1].start()
            copies[2].start()

    def grid_step(turned):
        for quad in range(PAIRS // 2):
            modes = gather_rows(layout, turned, scratch, quad, group)
            signal = dot(modes, basis[...], (0, 0))
            incoming = grid_rows(layout, north, south, quad, group).astype(jnp.float32)
            upstream = (incoming * gelu_slope(signal)).astype(jnp.bfloat16)
            scatter_rows(layout, turned, dot(basis[...], upstream, (1, 1)), returned, quad, group)

    pl.when(2 * side[1] < layout.parts)(functools.partial(grid_step, True))
    pl.when(2 * side[1] >= layout.parts)(functools.partial(grid_step, False))

    @pl.when(group == pl.num_programs(0) - 1)
    def _():
        if apart:
            copies[1].wait()
            copies[2].wait()

        def products(spectral, swapped, back):
            return spectral.astype(jnp.float32) * back, swapped.astype(jnp.float32) * back

        zeros = jnp.zeros((degrees, LANES), jnp.float32)
        same, cross = zeros, zeros
        for start, stop, top in order_groups(layout):

            def low_block(two, carry):
                values = [order_rows(layout, returned, 2 * two + which, 1) for which in range(2)]
                back = dot_two(back_low[two, top:degrees, :], *values)
                for which in range(2):
                    order = 2 * two + which
                    first, second = products(
                        spec_low[order, top:degrees, :],
                        swap_low[order, top:degrees, :],
                        back[:, which * LANES : (which + 1) * LANES],
                    )
                    carry = carry[0] + first, carry[1] + second
                return carry

            part = jnp.zeros((degrees - top, LANES), jnp.float32)
            first, second = lax.fori_loop(start, stop, low_block, (part, part), unroll=8)
            if top:
                empty = jnp.zeros((top, LANES), jnp.float32)
                first = jnp.concatenate([empty, first], axis=0)
                second = jnp.concatenate([empty, second], axis=0)
            same, cross = same + first, cross + second

        line = lax.broadcasted_iota(jnp.int32, (rows, LANES), 0)

        def pair_block(two, carry):
            values = [order_rows(layout, returned, low + 4 * two + 2 * which, 2) for which in range(2)]
            back = dot_two(pair_back[two], *values)
            for which in range(2):
                pair = 2 * two + which
                first, second = products(
                    spec_pair[pair], swap_pair[pair], back[:, which * LANES : (which + 1) * LANES]
                )
                natural = line >= layout.first_natural + pair
                carry = (
                    carry[0] + jnp.where(natural, first, 0.0),
                    carry[1] + jnp.where(natural, second, 0.0),
                    carry[2] + jnp.where(natural, 0.0, first),
                    carry[3] + jnp.where(natural, 0.0, second),
                )
            return carry

        part = jnp.zeros((rows, LANES), jnp.float32)
        sums = lax.fori_loop(0, layout.pairs // 2, pair_block, (part,) * 4, unroll=16)
        placed = jnp.dot(
            place[...],
            jnp.concatenate(
                [jnp.concatenate(sums[:2], axis=1), jnp.concatenate(sums[2:], axis=1)], axis=0
            ),
            preferred_element_type=jnp.float32,
            precision=lax.Precision.HIGHEST,
        )
        same = same + placed[:, :LANES]
        cross = cross + placed[:, LANES:]
        real = same + swap_halves(same)
        imag = cross - swap_halves(cross)
        lane = lax.broadcasted_iota(jnp.int32, real.shape, 1)
        grads = jnp.where(lane < LANES // 2, real, imag).T
        upper, lower = grads[: LANES // 2], grads[LANES // 2 :]
        keep[...] = jnp.where(side[0] == 0, upper, lower)
        send[...] = jnp.where(side[0] == 0, lower, upper)


def grid_specs(layout, chunk):
    last = -(-layout.local // PAIRS) - 1
    shift = layout.half // PAIRS
    block = (1, PAIRS, LANES // 2, NLON)
    return [
        pl.BlockSpec(block, lambda g: (0, jnp.minimum(g, last), chunk, 0)),
        pl.BlockSpec(block, lambda g: (0, jnp.minimum(shift + g, last), chunk, 0)),
    ]


def whole():
    return pl.BlockSpec(memory_space=pltpu.VMEM)


def forward_call(layout, chunk, bounds, index, fields, pair_fwd):
    basis = jnp.asarray(fourier_constants(layout)[0])
    slots = basis.shape[0] // 2
    groups = layout.half // PAIRS
    anywhere = pl.BlockSpec(memory_space=pl.ANY)
    counts = [last - first for first, last in zip(bounds, bounds[1:])]
    return pl.pallas_call(
        functools.partial(forward_kernel, layout, chunk, bounds),
        in_specs=[pl.BlockSpec(memory_space=pltpu.SMEM)] + [anywhere] * 3,
        out_specs=[anywhere] * len(counts),
        out_shape=[jax.ShapeDtypeStruct((count, layout.rows, LANES), jnp.bfloat16) for count in counts],
        scratch_shapes=[
            pltpu.VMEM((slots * layout.pitch, LANES), jnp.float32),
            pltpu.VMEM((layout.rows, LANES // 2, NLON), jnp.bfloat16),
            pltpu.VMEM(basis.shape, jnp.bfloat16),
            pltpu.VMEM((layout.blocks, layout.rows, LANES), jnp.bfloat16),
            pltpu.VMEM(pair_fwd.shape[1:], jnp.bfloat16),
            pltpu.SemaphoreType.DMA((2 * groups,)),
            pltpu.SemaphoreType.DMA,
            pltpu.SemaphoreType.DMA,
            pltpu.SemaphoreType.DMA((3,)),
        ],
        compiler_params=pltpu.CompilerParams(vmem_limit_bytes=FORWARD_VMEM),
        cost_estimate=pl.CostEstimate(flops=1_000_000, bytes_accessed=100_000, transcendentals=0),
        name=f"forward_{chunk}",
    )(index, fields, basis, pair_fwd)


def low_call(layout, chunk, coeffs, tables, real_rows, imag_rows):
    operands = list(coeffs) + list(tables) + [real_rows, imag_rows]
    spectra = jax.ShapeDtypeStruct((2 * layout.twos, layout.degrees, LANES), jnp.bfloat16)
    return pl.pallas_call(
        functools.partial(low_kernel, layout),
        in_specs=[whole()] * len(operands),
        out_specs=[whole()] * 3,
        out_shape=[jax.ShapeDtypeStruct((2 * layout.twos * layout.pitch, LANES), jnp.float32), spectra, spectra],
        scratch_shapes=[
            pltpu.VMEM((layout.sent * TAIL, LANES), jnp.float32),
            pltpu.VMEM((layout.parts * MOVED * layout.rows, LANES), jnp.float32),
        ],
        compiler_params=pltpu.CompilerParams(vmem_limit_bytes=VMEM),
        cost_estimate=pl.CostEstimate(flops=8_000_000_000, bytes_accessed=30_000_000, transcendentals=0),
        name=f"low_{chunk}",
    )(*operands)


def spectral_call(layout, chunk, apart, side, blocks, lows, cotangent, tables, real_rows, imag_rows):
    half = jax.ShapeDtypeStruct((LANES // 2, layout.degrees), jnp.float32)
    operands = [side] + list(blocks) + list(lows) + [cotangent, cotangent] + list(tables) + [real_rows, imag_rows]
    low_spec = pl.BlockSpec(memory_space=pl.ANY) if apart else whole()
    specs = [pl.BlockSpec(memory_space=pltpu.SMEM)] + [whole()] * len(blocks) + [low_spec] * len(lows)
    specs += grid_specs(layout, chunk) + [whole()] * (len(tables) + 2)
    return pl.pallas_call(
        functools.partial(spectral_kernel, layout, apart),
        grid=(layout.half // PAIRS,),
        in_specs=specs,
        out_specs=[whole()] * 2,
        out_shape=[half, half],
        scratch_shapes=[
            pltpu.VMEM((layout.slots * layout.pitch, LANES), jnp.float32),
            pltpu.VMEM((layout.slots * layout.pitch, LANES), jnp.float32),
            pltpu.VMEM((2 * layout.twos, layout.degrees, LANES), jnp.bfloat16),
            pltpu.VMEM((2 * layout.twos, layout.degrees, LANES), jnp.bfloat16),
            pltpu.VMEM((layout.pairs, layout.rows, LANES), jnp.bfloat16),
            pltpu.VMEM((layout.pairs, layout.rows, LANES), jnp.bfloat16),
            pltpu.VMEM((layout.sent * TAIL, LANES), jnp.float32),
            pltpu.VMEM((layout.parts * MOVED * layout.rows, LANES), jnp.float32),
            pltpu.SemaphoreType.DMA((3,)),
        ],
        compiler_params=pltpu.CompilerParams(vmem_limit_bytes=VMEM),
        cost_estimate=pl.CostEstimate(flops=8_000_000_000, bytes_accessed=30_000_000, transcendentals=0),
        name=f"spectral_{chunk}",
    )(*operands)


def radices(size):
    found, factor = [], 2
    while size > 1:
        while size % factor == 0:
            found.append(factor)
            size //= factor
        factor += 1
    return found


def sum_steps(axis):
    size = lax.axis_size(axis)
    steps, stride = [], 1
    for radix in radices(size):
        steps.append((axis, stride, radix))
        stride *= radix
    return steps


def hop_parcels(value, step):
    axis, stride, radix = step
    parcels = []
    for turn in range(1, radix):
        pairs = []
        for index in range(lax.axis_size(axis)):
            digit = index // stride % radix
            pairs.append((index, index + ((digit + turn) % radix - digit) * stride))
        parcels.append(lax.ppermute(value, axis, pairs))
    return parcels


def filter_rows(layout, spec):
    padded = jnp.pad(spec, ((0, layout.degrees - MODES), (0, 0)))
    front = jnp.pad(spec, ((layout.rows, layout.rows), (0, 0)))
    natural = front[MODES : MODES + layout.rows]
    backward = front[layout.rows + MODES - layout.rows : layout.rows + MODES][::-1]
    return jnp.concatenate([padded, natural, backward], axis=0).astype(jnp.float32)


def on_device(fields, cotangent, spec_real, spec_imag):
    parts = lax.axis_size("space")
    index = lax.axis_index("space")
    layout = Layout(parts, fields.shape[1])
    width = LANES // 2
    chunks = fields.shape[-1] // width
    inverse = jnp.asarray(fourier_constants(layout)[1])
    constants = legendre_constants(parts, layout.local)

    def local_table(name):
        return lax.dynamic_index_in_dim(jnp.asarray(constants[name]), index, keepdims=False)

    pair_fwd = jnp.asarray(constants["pair_fwd"])
    place = jnp.reshape(index, (1,)).astype(jnp.int32)
    def bands(name, first, count):
        table = jnp.asarray(constants[name])
        return lax.optimization_barrier(
            lax.dynamic_slice_in_dim(table, first * layout.rows, count * layout.rows, 1)
        )

    def side_by_side(table):
        return jnp.concatenate([table[::2], table[1::2]], axis=2)

    synth_own = bands("synth_low", index, 1)
    analysis = bands("analysis", parts - 1 - index, parts).reshape(layout.twos, -1, layout.degrees)
    analysis = jnp.swapaxes(analysis, 1, 2)
    back_low = jnp.swapaxes(synth_own.reshape(layout.twos, -1, layout.degrees), 1, 2)
    synth_low = side_by_side(synth_own)
    pair_tables = [local_table(name) for name in ("pair_synth", "pair_back")]
    low_tables = [analysis, synth_low]
    tables = [inverse, back_low] + pair_tables + [jnp.asarray(constants["place"])]
    fields, cotangent = jnp.swapaxes(fields, 2, 3), jnp.swapaxes(cotangent, 2, 3)
    real_all = filter_rows(layout, spec_real)
    imag_all = filter_rows(layout, spec_imag)

    def others(sent):
        routes = [[(source, (source + shift) % parts) for source in range(parts)] for shift in range(1, parts)]
        return [lax.ppermute(sent, "space", route) for route in routes]

    held = []
    for chunk in range(chunks):
        if chunk == 1:
            place, low_tables, tables = lax.optimization_barrier((place, low_tables, tables))
        bounds = (0, layout.blocks) if chunk < chunks - 1 else (0, layout.sent, layout.blocks)
        made = forward_call(layout, chunk, bounds, place, fields, pair_fwd)
        place, made = lax.optimization_barrier((place, list(made)))
        if len(made) > 1 and held:
            made[1], held[0][1] = lax.optimization_barrier((made[1], held[0][1]))
        held += [[own] + others(own) for own in made]

    hops = sum_steps("dp") + sum_steps("space")
    count_dp = len(sum_steps("dp"))
    swap = [(device, device ^ 1) for device in range(lax.axis_size("dp"))]
    side = jnp.stack([lax.rem(lax.axis_index("dp"), 2), index]).astype(jnp.int32)
    waiting = []

    def launch(value, done):
        if done:
            return value, hop_parcels(value, hops[done])
        keep, send = value
        return keep, [lax.ppermute(send, "dp", swap)]

    def hop_all(limit, tie):
        moved = []
        for value, done in waiting:
            if done < limit:
                value, parcels = launch(value, done)
                parcels, value, tie = lax.optimization_barrier((parcels, value, tie))
                value, done = sum(parcels, value), done + 1
            moved.append((value, done))
        waiting[:] = moved
        return tie

    def hop_last(times):
        for _ in range(times):
            value, done = waiting[-1]
            value, parcels = launch(value, done)
            waiting[-1] = (sum(parcels, value), done + 1)

    def before(values):
        if not waiting:
            return values
        values, sums = lax.optimization_barrier((values, [value for value, _ in waiting]))
        waiting[:] = [(value, done) for value, (_, done) in zip(sums, waiting)]
        return values

    for chunk in range(chunks):
        columns = slice(chunk * width, (chunk + 1) * width)
        real, imag = real_all[:, columns], imag_all[:, columns]
        real_rows = jnp.concatenate([real, real], axis=1)
        imag_rows = jnp.concatenate([-imag, imag], axis=1)
        blocks, lows, apart = held[chunk], low_tables, chunk == chunks - 1
        if apart:
            lows = low_call(layout, chunk, blocks, low_tables, real_rows, imag_rows)
            lows = before(hop_all(count_dp, lows))
            blocks = held[-1]
        grads = spectral_call(layout, chunk, apart, side, blocks, lows, cotangent, tables, real_rows, imag_rows)
        grads = hop_all(len(hops) if apart else count_dp, grads)
        waiting.append((grads, 0))
        if chunk < chunks - 2:
            hop_last(count_dp // 2)
            held[chunk + 1] = before(held[chunk + 1])

    hop_last(1)
    total, done = waiting.pop()
    while done < len(hops):
        joined = [value for value, at in waiting if at == done]
        waiting = [(value, at) for value, at in waiting if at != done]
        if joined:
            total = jnp.concatenate(joined + [total], axis=0)
        total, done = sum(hop_parcels(total, hops[done]), total), done + 1
    mine = jnp.concatenate([value for value, _ in waiting] + [total], axis=0)
    other = lax.ppermute(mine, "dp", swap)
    real = jnp.where(side[0] == 0, mine, other)[:, :MODES]
    imag = jnp.where(side[0] == 0, other, mine)[:, :MODES]
    batch_total = fields.shape[0] * lax.axis_size("dp")
    return (real.T / batch_total, imag.T / batch_total)


def solution(mesh):
    in_specs = (P("dp", "space", None, None), P("dp", "space", None, None), P(), P())
    out_specs = (P(), P())
    return jax.shard_map(
        on_device, mesh=mesh, in_specs=in_specs, out_specs=out_specs, check_vma=False
    )
```

```python
import functools
import math

import jax
import jax.numpy as jnp
import ml_dtypes
import numpy as np
from jax import lax
from jax.experimental import pallas as pl
from jax.experimental.pallas import tpu as pltpu
from jax.sharding import PartitionSpec as P

NLAT = 126
NLON = 252
MODES = 126
LANES = 128
GROUP = 16
PAIRS = 16
MOVED = 3
TAIL = 8
VMEM = 30 * 1024 * 1024
FORWARD_VMEM = 56 * 1024 * 1024


def round_up(value, step):
    return -(-value // step) * step


@functools.lru_cache(maxsize=None)
def legendre_table():
    single = np.float32
    colatitude = single(math.pi) * (np.arange(NLAT, dtype=single) + single(0.5)) / single(NLAT)
    cos_theta, sin_theta = np.cos(colatitude), np.sin(colatitude)
    counters = np.arange(1, MODES, dtype=single)
    log_steps = single(0.5) * np.log((2 * counters + 1) / (2 * counters))
    log_table = np.concatenate([np.zeros(1, single), np.cumsum(log_steps, dtype=single)])
    order = np.arange(MODES, dtype=single)[:, None]
    start = single(0.5 * math.log(1.0 / (4.0 * math.pi)))
    diagonal = np.exp(start + log_table[:, None] + order * np.log(sin_theta)[None])
    previous = earlier = np.zeros_like(diagonal)
    table = np.zeros((MODES, MODES, NLAT), single)
    for at in range(MODES):
        degree, below = single(at), single(at - 1)
        growth = np.sqrt(
            np.maximum(4 * degree * degree - 1, single(0)) / np.maximum(degree * degree - order * order, single(1))
        )
        damping = np.sqrt(
            np.maximum(below * below - order * order, single(0)) / np.maximum(4 * below * below - 1, single(1))
        )
        current = growth * (cos_theta[None] * previous - damping * earlier)
        current = np.where(order == degree, diagonal, np.where(order < degree, current, single(0)))
        table[:, at] = current
        previous, earlier = current, previous
    weight = single(math.pi / NLAT * (2.0 * math.pi / NLON)) * sin_theta
    return table, table * weight


def to_bf16(array):
    return np.where(np.abs(array) < 2.0**-126, 0.0, array).astype(ml_dtypes.bfloat16)


class Layout:
    def __init__(self, parts, local):
        self.parts, self.local = parts, local
        self.rows = round_up(local + 1, 16)
        self.half = self.rows // 2
        self.base = round_up(max(self.rows - local, 1), 8)
        self.pitch = self.rows + self.base
        self.low = max(MODES - local, 0)
        high = MODES - self.low
        self.pairs = round_up((high + 1) // 2, 2)
        self.twos = round_up(self.low, 2) // 2
        self.sent, self.runs = self.low, []
        self.carry()
        self.blocks = self.sent + self.pairs
        self.slots = round_up(self.low + 2 * self.pairs, 8)
        self.degrees = round_up(MODES, 16)
        self.first_natural = self.rows - MODES + self.low
        self.partner = MODES - 1 + self.low
        orders = list(range(self.low))
        for pair in range(self.pairs):
            order, mate = self.low + pair, self.partner - self.low - pair
            orders += [order if order <= mate else -1, mate if order < mate else -1]
        self.orders = np.array(orders + [-1] * (self.slots - len(orders)))

    def band(self, part):
        latitudes = np.arange(part * self.local, (part + 1) * self.local)
        return latitudes[::-1] if 2 * part < self.parts else latitudes

    def carry(self):
        plain = to_bf16(legendre_table()[0]).astype(np.float32)
        live = np.zeros(self.low, int)
        for part in range(self.parts):
            used = np.abs(plain[: self.low][:, :, self.band(part)]).max(axis=1) > 0
            for order in range(self.low):
                live[order] = max(live[order], *(1 + np.flatnonzero(used[order])), 1)
        sent = self.low - MOVED
        places = []
        for row in range(self.rows - 1, self.rows - TAIL - 1, -1):
            free = live[: max(sent, 0)] <= row
            first = int(np.flatnonzero(~free)[-1]) + 1 if (~free).any() else 0
            if first < sent:
                places.append((row, first, sent - first))
        runs = []
        for which in range(MOVED):
            done = 0
            while sent > 0 and done < live[sent + which] and places:
                row, first, count = places.pop(0)
                taken = min(count, live[sent + which] - done)
                runs.append((which, int(done), row, first, int(taken)))
                done += taken
                if taken < count:
                    places.insert(0, (row, int(first + taken), int(count - taken)))
            if sent <= 0 or done < live[sent + which]:
                return
        self.sent, self.runs = sent, runs


def fourier_constants(layout):
    orders = np.maximum(layout.orders, 0)
    angles = 2.0 * math.pi / NLON * (orders[:, None] * np.arange(NLON)[None] % NLON)
    live = (layout.orders >= 0)[:, None]
    basis = np.concatenate([np.cos(angles) * live, -np.sin(angles) * live])
    factor = np.where(layout.orders == 0, 1.0, 2.0)[:, None]
    inverse = basis * np.concatenate([factor, factor])
    return to_bf16(basis), to_bf16(inverse)


@functools.lru_cache(maxsize=None)
def legendre_constants(parts, local):
    layout = Layout(parts, local)
    plain, weighted = legendre_table()
    rows, degrees, low, pairs = layout.rows, layout.degrees, layout.low, layout.pairs
    analysis = np.zeros((2 * layout.twos, 2 * parts * rows, degrees))
    synth_low = np.zeros((2 * layout.twos, parts * rows, degrees))
    pair_fwd = np.zeros((parts, pairs, rows, 2 * rows))
    pair_back = np.zeros((parts, pairs, rows, 2 * rows))
    for part in range(parts):
        own = layout.band(part)
        start = part * rows
        synth_low[:low, start : start + local, :MODES] = np.swapaxes(plain[:low, :, own], 1, 2)
        for turn in (1, 2):
            start = (turn * parts - 1 - part) * rows
            analysis[:low, start : start + local, :MODES] = np.swapaxes(weighted[:low, :, own], 1, 2)
        for pair in range(pairs):
            order = low + pair
            mate = layout.partner - order
            for target, table in ((pair_fwd, weighted), (pair_back, plain)):
                if order <= mate:
                    count = MODES - order
                    target[part, pair, rows - count :, :local] = table[order][order:, own]
                if order < mate:
                    count = MODES - mate
                    target[part, pair, :count, rows : rows + local] = table[mate][mate:, own][::-1]
    pair_synth = np.swapaxes(pair_back, -1, -2)
    place = np.zeros((degrees, 2 * rows))
    for row in range(rows):
        if row >= rows - MODES + low:
            place[MODES - rows + row, row] = 1.0
        if MODES - 1 - row >= 0:
            place[MODES - 1 - row, rows + row] = 1.0
    return {
        "analysis": to_bf16(analysis),
        "synth_low": to_bf16(synth_low),
        "pair_fwd": to_bf16(pair_fwd),
        "pair_back": to_bf16(np.concatenate([pair_back[:, ::2], pair_back[:, 1::2]], axis=3)),
        "pair_synth": to_bf16(np.concatenate([pair_synth[:, ::2], pair_synth[:, 1::2]], axis=3)),
        "place": place.astype(np.float32),
    }


def dot(left, right, sides=(1, 0)):
    contract = (((sides[0],), (sides[1],)), ((), ()))
    return lax.dot_general(left, right, contract, preferred_element_type=jnp.float32)


def dot_two(left, first, second):
    upper = jnp.concatenate([first, jnp.zeros_like(first)], axis=1)
    lower = jnp.concatenate([jnp.zeros_like(second), second], axis=1)
    return dot(left, jnp.concatenate([upper, lower], axis=0))


def swap_halves(values):
    return pltpu.roll(values, LANES // 2, 1)


def interleave(first, second):
    lane = lax.broadcasted_iota(jnp.int32, first.shape, 1)
    below = lane < LANES // 2
    return (
        jnp.where(below, first, swap_halves(second)),
        jnp.where(below, swap_halves(first), second),
    )


def gelu_slope(values):
    cumulative = 0.5 * (1.0 + lax.erf(values / math.sqrt(2.0)))
    density = jnp.exp(-0.5 * values * values) / math.sqrt(2.0 * math.pi)
    return cumulative + values * density


def grid_rows(layout, north, south, quad, group):
    rows = []
    for pair in (2 * quad, 2 * quad + 1):
        rows.append(north[0, pair])
        values = south[0, pair]
        if layout.rows > layout.local:
            latitude = layout.half + group * PAIRS + pair
            values = jnp.where(latitude < layout.local, values, jnp.zeros_like(values))
        rows.append(values)
    return jnp.concatenate(rows, axis=0)


def row_of(layout, turned, group, place):
    if turned is True:
        steps = layout.half // PAIRS - 1
        return (steps - group) * PAIRS + (layout.base + layout.local - 1 - place - steps * PAIRS)
    row = latitude = group * PAIRS + place
    if turned is not False and latitude < layout.local:
        row = jnp.where(turned, layout.local - 1 - latitude, latitude)
    return layout.base + row


def scatter_rows(layout, turned, values, scratch, quad, group):
    slots = values.shape[0] // 2
    for which in range(2):
        columns = slice(which * LANES, (which + 1) * LANES)
        upper, lower = interleave(values[:slots, columns], values[slots:, columns])
        place = 2 * quad + which
        scratch[pl.ds(row_of(layout, turned, group, place), slots, stride=layout.pitch), :] = upper
        scratch[pl.ds(row_of(layout, turned, group, place + layout.half), slots, stride=layout.pitch), :] = lower


def gather_rows(layout, turned, scratch, quad, group):
    slots = layout.slots
    cosine, sine = [], []
    for which in range(2):
        place = 2 * quad + which
        upper = scratch[pl.ds(row_of(layout, turned, group, place), slots, stride=layout.pitch), :]
        lower = scratch[pl.ds(row_of(layout, turned, group, place + layout.half), slots, stride=layout.pitch), :]
        first, second = interleave(upper, lower)
        cosine.append(first.astype(jnp.bfloat16))
        sine.append(second.astype(jnp.bfloat16))
    return jnp.concatenate(
        [jnp.concatenate(cosine, axis=1), jnp.concatenate(sine, axis=1)], axis=0
    )


def order_rows(layout, scratch, first, count):
    parts = []
    for order in range(count):
        start = pl.multiple_of((first + order) * layout.pitch + layout.base, 8)
        parts.append(scratch[pl.ds(start, layout.rows), :])
    return jnp.concatenate(parts, axis=0).astype(jnp.bfloat16)


def band_copies(layout, chunk, fields, buffer, sems):
    width = LANES // 2
    copies = []
    for group in range(layout.half // PAIRS):
        started = []
        for side in range(2):
            first = side * layout.half + group * PAIRS
            count = min(PAIRS, layout.local - first)
            if count > 0:
                started.append(
                    pltpu.make_async_copy(
                        fields.at[0, pl.ds(first, count), pl.ds(chunk * width, width), :],
                        buffer.at[pl.ds(first, count)],
                        sems.at[2 * group + side],
                    )
                )
        copies.append(started)
    return copies


def forward_kernel(layout, chunk, bounds, index, fields, basis_all, pair_all, *refs):
    outs, refs = refs[: len(bounds) - 1], refs[len(bounds) - 1 :]
    scratch, buffer, basis, stage, pair_fwd, sems, basis_sem, pair_sem, out_sems = refs
    basis_copy = pltpu.make_async_copy(basis_all, basis, basis_sem)
    basis_copy.start()
    copies = band_copies(layout, chunk, fields, buffer, sems)
    for started in copies[:2]:
        for copy in started:
            copy.start()
    tables = pltpu.make_async_copy(pair_all.at[index[0]], pair_fwd, pair_sem)
    tables.start()
    if layout.rows > layout.local:
        shape = (layout.rows - layout.local,) + buffer.shape[1:]
        buffer[layout.local :] = jnp.zeros(shape, buffer.dtype)
    basis_copy.wait()
    turned = 2 * index[0] < layout.parts
    for group, started in enumerate(copies):
        for copy in started:
            copy.wait()
        for copy in sum(copies[group + 2 : group + 3], []):
            copy.start()
        for quad in range(PAIRS // 2):
            rows = []
            for which in range(2):
                latitude = group * PAIRS + 2 * quad + which
                rows += [buffer[latitude], buffer[latitude + layout.half]]
            grid = jnp.concatenate(rows, axis=0)
            scatter_rows(layout, turned, dot(basis[...], grid, (1, 1)), scratch, quad, group)

    def low_block(order, carry):
        stage[order] = order_rows(layout, scratch, order, 1)
        return carry

    def pair_block(pair, carry):
        values = order_rows(layout, scratch, layout.low + 2 * pair, 2)
        stage[layout.sent + pair] = dot(pair_fwd[pair], values).astype(jnp.bfloat16)
        return carry

    flushes = []

    def flush(first, last):
        at = max(at for at in range(len(outs)) if bounds[at] <= first)
        flushes.append(
            pltpu.make_async_copy(
                stage.at[pl.ds(first, last - first)],
                outs[at].at[pl.ds(first - bounds[at], last - first)],
                out_sems.at[len(flushes)],
            )
        )
        flushes[-1].start()

    for which, start, row, first, count in layout.runs:
        moved = scratch[pl.ds((layout.sent + which) * layout.pitch + layout.base + start, count), :]
        scratch[pl.ds(first * layout.pitch + layout.base + row, count, stride=layout.pitch), :] = moved
    middle = layout.sent // 2
    for first, last in ((0, middle), (middle, layout.sent)):
        lax.fori_loop(first, last, low_block, 0, unroll=8)
        flush(first, last)
    tables.wait()
    lax.fori_loop(0, layout.pairs, pair_block, 0, unroll=8)
    flush(layout.sent, layout.blocks)
    for copy in flushes:
        copy.wait()


def mix(spectral, swapped, real_rows, imag_rows):
    return (spectral * real_rows + swapped * imag_rows).astype(jnp.bfloat16)


def order_groups(layout):
    for start in range(0, layout.low, GROUP):
        stop = min(start + GROUP, layout.low)
        yield start // 2, (stop + 1) // 2, start // 16 * 16


def low_kernel(layout, *refs):
    low_orders(layout, refs[: layout.parts], *refs[layout.parts :])


def low_orders(
    layout, held, analysis, synth_low, real_ref, imag_ref, grid_low, spec_low, swap_low, tails, moved
):
    degrees, rows = layout.degrees, layout.rows
    if layout.runs:
        moved[...] = jnp.zeros_like(moved)
    for at, ref in enumerate(held):
        if layout.runs:

            def tail_block(order, carry):
                values = ref[order, rows - 16 :, :].astype(jnp.float32)
                tails[pl.ds(pl.multiple_of(order * TAIL, TAIL), TAIL), :] = values[16 - TAIL :]
                return carry

            lax.fori_loop(0, layout.sent, tail_block, 0, unroll=10)
        for which, start, row, first, count in layout.runs:
            begin = (at * MOVED + which) * rows + start
            source = pl.ds(first * TAIL + row - (rows - TAIL), count, stride=TAIL)
            moved[pl.ds(begin, count), :] = tails[source, :]

    def coefficients(order):
        if isinstance(order, int) and order >= layout.sent:
            which = min(order, layout.low - 1) - layout.sent
            starts = [(at * MOVED + which) * rows for at in range(layout.parts)]
            return jnp.concatenate([moved[start : start + rows, :] for start in starts], axis=0).astype(jnp.bfloat16)
        return jnp.concatenate([ref[order] for ref in held], axis=0)

    for start, stop, top in order_groups(layout):
        real_rows = real_ref[top:degrees, :]
        imag_rows = imag_ref[top:degrees, :]

        def low_block(two, carry):
            last = layout.low - 1
            second = min(2 * two + 1, last) if isinstance(two, int) else jnp.minimum(2 * two + 1, last)
            values = [coefficients(2 * two), coefficients(second)]
            spectral = dot_two(analysis[two, top:degrees, :], *values).astype(jnp.bfloat16)
            for which in range(2):
                spec_low[2 * two + which, top:degrees, :] = spectral[:, which * LANES : (which + 1) * LANES]
            return carry

        def mix_block(two, carry):
            mixed = []
            for order in (2 * two, 2 * two + 1):
                spectral = spec_low[order, top:degrees, :].astype(jnp.float32)
                swapped = swap_halves(spectral)
                swap_low[order, top:degrees, :] = swapped.astype(jnp.bfloat16)
                values = mix(spectral, swapped, real_rows, imag_rows)
                if top:
                    values = jnp.concatenate([jnp.zeros((top, LANES), values.dtype), values], axis=0)
                mixed.append(values)
            values = dot_two(synth_low[two], *mixed)
            for which in range(2):
                begin = pl.multiple_of((2 * two + which) * layout.pitch + layout.base, 8)
                grid_low[pl.ds(begin, layout.rows), :] = values[:, which * LANES : (which + 1) * LANES]
            return carry

        whole_twos = max(min(stop, layout.sent // 2 if layout.runs else stop), start)
        lax.fori_loop(start, whole_twos, low_block, 0, unroll=8)
        for two in range(whole_twos, stop):
            low_block(two, 0)
        lax.fori_loop(start, stop, mix_block, 0, unroll=8)


def spectral_kernel(layout, apart, side, *refs):
    held, lows, refs = refs[: layout.parts], refs[layout.parts : layout.parts + 2 + apart], refs[layout.parts + 2 + apart :]
    north, south, basis, back_low, pair_synth, pair_back, place, real_ref, imag_ref = refs[:9]
    keep, send, scratch, returned, spec_low, swap_low, spec_pair, swap_pair, tails, moved, sems = refs[9:]
    offset = 0 if apart else layout.sent
    group = pl.program_id(0)
    rows, degrees, low = layout.rows, layout.degrees, layout.low
    if apart:
        sources = (lows[0].at[pl.ds(0, low * layout.pitch)], lows[1], lows[2])
        targets = (scratch.at[pl.ds(0, low * layout.pitch)], spec_low, swap_low)
        copies = [pltpu.make_async_copy(*ends, sems.at[at]) for at, ends in enumerate(zip(sources, targets))]

    @pl.when(group == 0)
    def _():
        if apart:
            copies[0].start()
        else:
            low_orders(layout, held, *lows, real_ref, imag_ref, scratch, spec_low, swap_low, tails, moved)
        line = lax.broadcasted_iota(jnp.int32, (rows, LANES), 0)

        def pair_block(two, carry):
            mixed = []
            for pair in (2 * two, 2 * two + 1):
                total = sum(ref[offset + pair].astype(jnp.float32) for ref in held)
                spectral = total.astype(jnp.bfloat16)
                spec_pair[pair] = spectral
                natural = line >= layout.first_natural + pair
                real_rows = jnp.where(natural, real_ref[degrees : degrees + rows, :], real_ref[degrees + rows :, :])
                imag_rows = jnp.where(natural, imag_ref[degrees : degrees + rows, :], imag_ref[degrees + rows :, :])
                spectral = spectral.astype(jnp.float32)
                swapped = swap_halves(spectral)
                swap_pair[pair] = swapped.astype(jnp.bfloat16)
                mixed.append(mix(spectral, swapped, real_rows, imag_rows))
            values = dot_two(pair_synth[two], *mixed)
            for which in range(4):
                begin = pl.multiple_of((low + 4 * two + which) * layout.pitch + layout.base, 8)
                columns = slice(which // 2 * LANES, (which // 2 + 1) * LANES)
                scratch[pl.ds(begin, rows), :] = values[which % 2 * rows : (which % 2 + 1) * rows, columns]
            return carry

        lax.fori_loop(0, layout.pairs // 2, pair_block, 0, unroll=8)
        used = (low + 2 * layout.pairs) * layout.pitch
        if used < layout.slots * layout.pitch:
            scratch[used : layout.slots * layout.pitch, :] = jnp.zeros(
                (layout.slots * layout.pitch - used, LANES), jnp.float32
            )
        for row in range(layout.base + layout.local, layout.pitch):
            returned[pl.ds(row, layout.slots, stride=layout.pitch), :] = jnp.zeros((layout.slots, LANES), jnp.float32)
        if apart:
            copies[0].wait()
            copies[1].start()
            copies[2].start()

    def grid_step(turned):
        for quad in range(PAIRS // 2):
            modes = gather_rows(layout, turned, scratch, quad, group)
            signal = dot(modes, basis[...], (0, 0))
            incoming = grid_rows(layout, north, south, quad, group).astype(jnp.float32)
            upstream = (incoming * gelu_slope(signal)).astype(jnp.bfloat16)
            scatter_rows(layout, turned, dot(basis[...], upstream, (1, 1)), returned, quad, group)

    pl.when(2 * side[1] < layout.parts)(functools.partial(grid_step, True))
    pl.when(2 * side[1] >= layout.parts)(functools.partial(grid_step, False))

    @pl.when(group == pl.num_programs(0) - 1)
    def _():
        if apart:
            copies[1].wait()
            copies[2].wait()

        def products(spectral, swapped, back):
            return spectral.astype(jnp.float32) * back, swapped.astype(jnp.float32) * back

        zeros = jnp.zeros((degrees, LANES), jnp.float32)
        same, cross = zeros, zeros
        for start, stop, top in order_groups(layout):

            def low_block(two, carry):
                values = [order_rows(layout, returned, 2 * two + which, 1) for which in range(2)]
                back = dot_two(back_low[two, top:degrees, :], *values)
                for which in range(2):
                    order = 2 * two + which
                    first, second = products(
                        spec_low[order, top:degrees, :],
                        swap_low[order, top:degrees, :],
                        back[:, which * LANES : (which + 1) * LANES],
                    )
                    carry = carry[0] + first, carry[1] + second
                return carry

            part = jnp.zeros((degrees - top, LANES), jnp.float32)
            first, second = lax.fori_loop(start, stop, low_block, (part, part), unroll=8)
            if top:
                empty = jnp.zeros((top, LANES), jnp.float32)
                first = jnp.concatenate([empty, first], axis=0)
                second = jnp.concatenate([empty, second], axis=0)
            same, cross = same + first, cross + second

        line = lax.broadcasted_iota(jnp.int32, (rows, LANES), 0)

        def pair_block(two, carry):
            values = [order_rows(layout, returned, low + 4 * two + 2 * which, 2) for which in range(2)]
            back = dot_two(pair_back[two], *values)
            for which in range(2):
                pair = 2 * two + which
                first, second = products(
                    spec_pair[pair], swap_pair[pair], back[:, which * LANES : (which + 1) * LANES]
                )
                natural = line >= layout.first_natural + pair
                carry = (
                    carry[0] + jnp.where(natural, first, 0.0),
                    carry[1] + jnp.where(natural, second, 0.0),
                    carry[2] + jnp.where(natural, 0.0, first),
                    carry[3] + jnp.where(natural, 0.0, second),
                )
            return carry

        part = jnp.zeros((rows, LANES), jnp.float32)
        sums = lax.fori_loop(0, layout.pairs // 2, pair_block, (part,) * 4, unroll=16)
        placed = jnp.dot(
            place[...],
            jnp.concatenate(
                [jnp.concatenate(sums[:2], axis=1), jnp.concatenate(sums[2:], axis=1)], axis=0
            ),
            preferred_element_type=jnp.float32,
            precision=lax.Precision.HIGHEST,
        )
        same = same + placed[:, :LANES]
        cross = cross + placed[:, LANES:]
        real = same + swap_halves(same)
        imag = cross - swap_halves(cross)
        lane = lax.broadcasted_iota(jnp.int32, real.shape, 1)
        grads = jnp.where(lane < LANES // 2, real, imag).T
        upper, lower = grads[: LANES // 2], grads[LANES // 2 :]
        keep[...] = jnp.where(side[0] == 0, upper, lower)
        send[...] = jnp.where(side[0] == 0, lower, upper)


def grid_specs(layout, chunk):
    last = -(-layout.local // PAIRS) - 1
    shift = layout.half // PAIRS
    block = (1, PAIRS, LANES // 2, NLON)
    return [
        pl.BlockSpec(block, lambda g: (0, jnp.minimum(g, last), chunk, 0)),
        pl.BlockSpec(block, lambda g: (0, jnp.minimum(shift + g, last), chunk, 0)),
    ]


def whole():
    return pl.BlockSpec(memory_space=pltpu.VMEM)


def forward_call(layout, chunk, bounds, index, fields, pair_fwd):
    basis = jnp.asarray(fourier_constants(layout)[0])
    slots = basis.shape[0] // 2
    groups = layout.half // PAIRS
    anywhere = pl.BlockSpec(memory_space=pl.ANY)
    counts = [last - first for first, last in zip(bounds, bounds[1:])]
    return pl.pallas_call(
        functools.partial(forward_kernel, layout, chunk, bounds),
        in_specs=[pl.BlockSpec(memory_space=pltpu.SMEM)] + [anywhere] * 3,
        out_specs=[anywhere] * len(counts),
        out_shape=[jax.ShapeDtypeStruct((count, layout.rows, LANES), jnp.bfloat16) for count in counts],
        scratch_shapes=[
            pltpu.VMEM(((slots + 1) * layout.pitch, LANES), jnp.float32),
            pltpu.VMEM((layout.rows, LANES // 2, NLON), jnp.bfloat16),
            pltpu.VMEM(basis.shape, jnp.bfloat16),
            pltpu.VMEM((layout.blocks, layout.rows, LANES), jnp.bfloat16),
            pltpu.VMEM(pair_fwd.shape[1:], jnp.bfloat16),
            pltpu.SemaphoreType.DMA((2 * groups,)),
            pltpu.SemaphoreType.DMA,
            pltpu.SemaphoreType.DMA,
            pltpu.SemaphoreType.DMA((3,)),
        ],
        compiler_params=pltpu.CompilerParams(vmem_limit_bytes=FORWARD_VMEM),
        cost_estimate=pl.CostEstimate(flops=1_000_000, bytes_accessed=100_000, transcendentals=0),
        name=f"forward_{chunk}",
    )(index, fields, basis, pair_fwd)


def low_call(layout, chunk, coeffs, tables, real_rows, imag_rows):
    operands = list(coeffs) + list(tables) + [real_rows, imag_rows]
    spectra = jax.ShapeDtypeStruct((2 * layout.twos, layout.degrees, LANES), jnp.bfloat16)
    return pl.pallas_call(
        functools.partial(low_kernel, layout),
        in_specs=[whole()] * len(operands),
        out_specs=[whole()] * 3,
        out_shape=[jax.ShapeDtypeStruct((2 * layout.twos * layout.pitch, LANES), jnp.float32), spectra, spectra],
        scratch_shapes=[
            pltpu.VMEM(((layout.sent + 8) * TAIL, LANES), jnp.float32),
            pltpu.VMEM((layout.parts * MOVED * layout.rows, LANES), jnp.float32),
        ],
        compiler_params=pltpu.CompilerParams(vmem_limit_bytes=VMEM),
        cost_estimate=pl.CostEstimate(flops=8_000_000_000, bytes_accessed=30_000_000, transcendentals=0),
        name=f"low_{chunk}",
    )(*operands)


def spectral_call(layout, chunk, apart, side, blocks, lows, cotangent, tables, real_rows, imag_rows):
    half = jax.ShapeDtypeStruct((LANES // 2, layout.degrees), jnp.float32)
    operands = [side] + list(blocks) + list(lows) + [cotangent, cotangent] + list(tables) + [real_rows, imag_rows]
    low_spec = pl.BlockSpec(memory_space=pl.ANY) if apart else whole()
    specs = [pl.BlockSpec(memory_space=pltpu.SMEM)] + [whole()] * len(blocks) + [low_spec] * len(lows)
    specs += grid_specs(layout, chunk) + [whole()] * (len(tables) + 2)
    return pl.pallas_call(
        functools.partial(spectral_kernel, layout, apart),
        grid=(layout.half // PAIRS,),
        in_specs=specs,
        out_specs=[whole()] * 2,
        out_shape=[half, half],
        scratch_shapes=[
            pltpu.VMEM(((layout.slots + 1) * layout.pitch, LANES), jnp.float32),
            pltpu.VMEM(((layout.slots + 1) * layout.pitch, LANES), jnp.float32),
            pltpu.VMEM((2 * layout.twos, layout.degrees, LANES), jnp.bfloat16),
            pltpu.VMEM((2 * layout.twos, layout.degrees, LANES), jnp.bfloat16),
            pltpu.VMEM((layout.pairs, layout.rows, LANES), jnp.bfloat16),
            pltpu.VMEM((layout.pairs, layout.rows, LANES), jnp.bfloat16),
            pltpu.VMEM(((layout.sent + 8) * TAIL, LANES), jnp.float32),
            pltpu.VMEM((layout.parts * MOVED * layout.rows, LANES), jnp.float32),
            pltpu.SemaphoreType.DMA((3,)),
        ],
        compiler_params=pltpu.CompilerParams(vmem_limit_bytes=VMEM),
        cost_estimate=pl.CostEstimate(flops=8_000_000_000, bytes_accessed=30_000_000, transcendentals=0),
        name=f"spectral_{chunk}",
    )(*operands)


def radices(size):
    found, factor = [], 2
    while size > 1:
        while size % factor == 0:
            found.append(factor)
            size //= factor
        factor += 1
    return found


def sum_steps(axis):
    size = lax.axis_size(axis)
    steps, stride = [], 1
    for radix in radices(size):
        steps.append((axis, stride, radix))
        stride *= radix
    return steps


def hop_parcels(value, step):
    axis, stride, radix = step
    parcels = []
    for turn in range(1, radix):
        pairs = []
        for index in range(lax.axis_size(axis)):
            digit = index // stride % radix
            pairs.append((index, index + ((digit + turn) % radix - digit) * stride))
        parcels.append(lax.ppermute(value, axis, pairs))
    return parcels


def filter_rows(layout, spec):
    padded = jnp.pad(spec, ((0, layout.degrees - MODES), (0, 0)))
    front = jnp.pad(spec, ((layout.rows, layout.rows), (0, 0)))
    natural = front[MODES : MODES + layout.rows]
    backward = front[layout.rows + MODES - layout.rows : layout.rows + MODES][::-1]
    return jnp.concatenate([padded, natural, backward], axis=0).astype(jnp.float32)


def on_device(fields, cotangent, spec_real, spec_imag):
    parts = lax.axis_size("space")
    index = lax.axis_index("space")
    layout = Layout(parts, fields.shape[1])
    width = LANES // 2
    chunks = fields.shape[-1] // width
    inverse = jnp.asarray(fourier_constants(layout)[1])
    constants = legendre_constants(parts, layout.local)

    def local_table(name):
        return lax.dynamic_index_in_dim(jnp.asarray(constants[name]), index, keepdims=False)

    pair_fwd = jnp.asarray(constants["pair_fwd"])
    place = jnp.reshape(index, (1,)).astype(jnp.int32)
    def bands(name, first, count):
        table = jnp.asarray(constants[name])
        return lax.optimization_barrier(
            lax.dynamic_slice_in_dim(table, first * layout.rows, count * layout.rows, 1)
        )

    def side_by_side(table):
        return jnp.concatenate([table[::2], table[1::2]], axis=2)

    synth_own = bands("synth_low", index, 1)
    analysis = bands("analysis", parts - 1 - index, parts).reshape(layout.twos, -1, layout.degrees)
    analysis = jnp.swapaxes(analysis, 1, 2)
    back_low = jnp.swapaxes(synth_own.reshape(layout.twos, -1, layout.degrees), 1, 2)
    synth_low = side_by_side(synth_own)
    pair_tables = [local_table(name) for name in ("pair_synth", "pair_back")]
    low_tables = [analysis, synth_low]
    tables = [inverse, back_low] + pair_tables + [jnp.asarray(constants["place"])]
    fields, cotangent = jnp.swapaxes(fields, 2, 3), jnp.swapaxes(cotangent, 2, 3)
    real_all = filter_rows(layout, spec_real)
    imag_all = filter_rows(layout, spec_imag)

    def others(sent):
        routes = [[(source, (source + shift) % parts) for source in range(parts)] for shift in range(1, parts)]
        return [lax.ppermute(sent, "space", route) for route in routes]

    held = []
    for chunk in range(chunks):
        if chunk == 1:
            place, low_tables, tables = lax.optimization_barrier((place, low_tables, tables))
        bounds = (0, layout.blocks) if chunk < chunks - 1 else (0, layout.sent, layout.blocks)
        made = forward_call(layout, chunk, bounds, place, fields, pair_fwd)
        place, made = lax.optimization_barrier((place, list(made)))
        if len(made) > 1 and held:
            made[1], held[0][1] = lax.optimization_barrier((made[1], held[0][1]))
        held += [[own] + others(own) for own in made]

    hops = sum_steps("dp") + sum_steps("space")
    count_dp = len(sum_steps("dp"))
    swap = [(device, device ^ 1) for device in range(lax.axis_size("dp"))]
    side = jnp.stack([lax.rem(lax.axis_index("dp"), 2), index]).astype(jnp.int32)
    waiting = []

    def launch(value, done):
        if done:
            return value, hop_parcels(value, hops[done])
        keep, send = value
        return keep, [lax.ppermute(send, "dp", swap)]

    def hop_all(limit, tie):
        moved = []
        for value, done in waiting:
            if done < limit:
                value, parcels = launch(value, done)
                parcels, value, tie = lax.optimization_barrier((parcels, value, tie))
                value, done = sum(parcels, value), done + 1
            moved.append((value, done))
        waiting[:] = moved
        return tie

    def hop_last(times):
        for _ in range(times):
            value, done = waiting[-1]
            value, parcels = launch(value, done)
            waiting[-1] = (sum(parcels, value), done + 1)

    def before(values):
        if not waiting:
            return values
        values, sums = lax.optimization_barrier((values, [value for value, _ in waiting]))
        waiting[:] = [(value, done) for value, (_, done) in zip(sums, waiting)]
        return values

    for chunk in range(chunks):
        columns = slice(chunk * width, (chunk + 1) * width)
        real, imag = real_all[:, columns], imag_all[:, columns]
        real_rows = jnp.concatenate([real, real], axis=1)
        imag_rows = jnp.concatenate([-imag, imag], axis=1)
        blocks, lows, apart = held[chunk], low_tables, chunk == chunks - 1
        if apart:
            lows = low_call(layout, chunk, blocks, low_tables, real_rows, imag_rows)
            lows = before(hop_all(count_dp, lows))
            blocks = held[-1]
        grads = spectral_call(layout, chunk, apart, side, blocks, lows, cotangent, tables, real_rows, imag_rows)
        grads = hop_all(len(hops) if apart else count_dp, grads)
        waiting.append((grads, 0))
        if chunk < chunks - 2:
            hop_last(count_dp // 2)
            held[chunk + 1] = before(held[chunk + 1])

    hop_last(1)
    total, done = waiting.pop()
    while done < len(hops):
        joined = [value for value, at in waiting if at == done]
        waiting = [(value, at) for value, at in waiting if at != done]
        if joined:
            total = jnp.concatenate(joined + [total], axis=0)
        total, done = sum(hop_parcels(total, hops[done]), total), done + 1
    mine = jnp.concatenate([value for value, _ in waiting] + [total], axis=0)
    other = lax.ppermute(mine, "dp", swap)
    real = jnp.where(side[0] == 0, mine, other)[:, :MODES]
    imag = jnp.where(side[0] == 0, other, mine)[:, :MODES]
    batch_total = fields.shape[0] * lax.axis_size("dp")
    return (real.T / batch_total, imag.T / batch_total)


def solution(mesh):
    in_specs = (P("dp", "space", None, None), P("dp", "space", None, None), P(), P())
    out_specs = (P(), P())
    return jax.shard_map(
        on_device, mesh=mesh, in_specs=in_specs, out_specs=out_specs, check_vma=False
    )
```
